32 devices in a mesh: pipe: 4 (over z), expert: 4 (over y, x), dp: 2 (over core).
Axes of the slice: x: 2, y: 2, z: 4, core: 2. Of those that a mesh axis runs over, the one named last changes fastest.
Arguments:
- enter_fwd: bfloat16 [4, 512, 7168], P('pipe', 'expert', 'dp'), may hold values from -6 to 6
- enter_rev: bfloat16 [4, 512, 7168], P('pipe', 'expert', 'dp'), may hold values from -6 to 6
- cot_rev: bfloat16 [4, 512, 7168], P('pipe', 'expert', 'dp'), may hold values from -0.1875 to 0.1875
- gain: bfloat16 [2, 4, 7168], P(None, 'pipe', 'dp'), may hold values from 0.5 to 1.5
- proj_down: bfloat16 [2, 4, 256, 7168], P(None, 'pipe', None, 'dp'), may hold values from -0.0625 to 0.0625
- proj_up: bfloat16 [2, 4, 256, 7168], P(None, 'pipe', None, 'dp'), may hold values from -0.375 to 0.375
- master: float32 [2, 4, 256, 7168], P(None, 'pipe', 'expert', 'dp'), may hold values from -0.125 to 0.125
- moment: bfloat16 [2, 4, 256, 7168], P(None, 'pipe', 'expert', 'dp'), may hold values from -6 to 6
- second: bfloat16 [2, 4, 256, 7168], P(None, 'pipe', 'expert', 'dp'), may hold values from 0.5 to 20
Outputs:
- leave_fwd: bfloat16 [4, 512, 7168], P('pipe', 'expert', 'dp')
- codes: bfloat16 [2, 4, 256, 7168], P(None, 'pipe', 'expert', 'dp')
- scales: float32 [2, 4, 2, 56], P(None, 'pipe', None, 'dp')
The draws below stay inside these ranges and needn't reach their ends.
All inputs are finite; a program needn't handle non-finite values.
Results may differ from the reference program's by a relative error of at most 0.0047.
The reference program's roundings to bfloat16 on the way count: a program that leaves them out, or rounds other values in their place, can miss the bound.
Values may be sent and summed in bfloat16 or wider, within the bound.
No kernel may reach another device: no remote copies, remote signals or barrier semaphores. Data moves between devices by JAX's collectives and lax.ppermute only.
A program may use at most 64 MiB of HBM per device.

```python
import math
import jax
import jax.numpy as jnp
from jax import lax

D = 7168
LATENT = 256
TOK_DEV = 128
SECTIONS = 4
TOKENS = 512
N_EXPERT = 4


def block_levels(own_key, extent, split, smallest, top_value):
    loudness, own = 1.0, jax.random.fold_in(own_key, 6)
    for position, shards_of in split:
        heights = jnp.exp(jax.random.uniform(jax.random.fold_in(own, position), (shards_of,), jnp.float32, smallest / len(split), top_value / len(split)))
        loudness = loudness * jnp.repeat(heights, extent[position] // shards_of).reshape([-1 if axis == position else 1 for axis in range(len(extent))])
    return loudness


def scatter_about(rng, extent, scale, limit, split=(), held_as=jnp.bfloat16):
    loudness = block_levels(rng, extent, split, -0.22, 0.18) if split else 1.0
    drawn = jax.random.normal(rng, extent, jnp.float32) * scale * loudness
    return jnp.minimum(jnp.maximum(drawn, -limit), limit).astype(held_as)


def setup_inputs(seed: int = 0) -> dict:
    key_list = jax.random.split(jax.random.key(seed), 10)
    return {
        "enter_fwd": scatter_about(key_list[0], (SECTIONS, TOKENS, D), 1.0, 6.0, ((0, 4), (1, 4), (2, 2))),
        "enter_rev": scatter_about(key_list[1], (SECTIONS, TOKENS, D), 1.0, 6.0, ((0, 4), (1, 4), (2, 2))),
        "cot_rev": scatter_about(key_list[2], (SECTIONS, TOKENS, D), 0.03, 0.1875, ((0, 4), (1, 4), (2, 2))),
        "gain": jnp.clip(1.0 + 0.1 * jax.random.normal(key_list[3], (2, SECTIONS, D), jnp.float32), 0.5, 1.5).astype(jnp.bfloat16),
        "proj_down": scatter_about(key_list[4], (2, SECTIONS, LATENT, D), D ** -0.5, 0.0625, ((1, 4), (3, 2))),
        "proj_up": scatter_about(key_list[5], (2, SECTIONS, LATENT, D), LATENT ** -0.5, 0.375, ((1, 4), (3, 2))),
        "master": scatter_about(key_list[6], (2, SECTIONS, LATENT, D), 0.02, 0.125, ((1, 4), (2, 4), (3, 2)), jnp.float32),
        "moment": scatter_about(key_list[7], (2, SECTIONS, LATENT, D), 1.0, 6.0, ((1, 4), (2, 4), (3, 2))),
        "second": jnp.clip(jnp.exp(math.log(20.0) - 3.6888795 * jax.random.uniform(key_list[8], (2, SECTIONS, LATENT, D), jnp.float32) ** block_levels(key_list[8], (2, SECTIONS, LATENT, D), ((1, 4), (2, 4), (3, 2)), -0.2, 0.2)), 0.5, 20.0).astype(jnp.bfloat16),
    }


def prepare(rows, gain_row, down):
    scaled = (rows.astype(jnp.float32) * gain_row).astype(jnp.bfloat16)
    squares = lax.optimization_barrier(jnp.sum(jnp.square(rows.astype(jnp.float32)), axis=-1))
    raw = jnp.dot(scaled, down.T, preferred_element_type=jnp.float32)
    rscale = lax.rsqrt(squares / D + 1e-06)
    return (scaled, raw, rscale)

def pick(array, first, index):
    return lax.dynamic_index_in_dim(array[first], index, 0, keepdims=False)

def reference(enter_fwd, enter_rev, cot_rev, gain, proj_down, proj_up, master, moment, second):

    def section(index):
        mirror_index = (SECTIONS - 1 - index).astype(jnp.int32)
        fwd_rows = lax.dynamic_index_in_dim(enter_fwd, index, 0, keepdims=False)
        back_rows = lax.dynamic_index_in_dim(enter_rev, mirror_index, 0, keepdims=False)
        back_cot = lax.dynamic_index_in_dim(cot_rev, mirror_index, 0, keepdims=False)
        own_gain = pick(gain, 0, index).astype(jnp.float32)
        own_down = pick(proj_down, 0, index)
        own_upper = pick(proj_up, 0, index)
        copy_gain = pick(gain, 1, mirror_index).astype(jnp.float32)
        copy_down = pick(proj_down, 1, mirror_index)
        copy_upper = pick(proj_up, 1, mirror_index)
        fwd_scaled, fwd_raw, fwd_r = prepare(fwd_rows, own_gain, own_down)
        hidden_one = (fwd_raw * fwd_r[:, None]).astype(jnp.bfloat16)
        result = (fwd_rows.astype(jnp.float32) + jnp.dot(hidden_one, own_upper, preferred_element_type=jnp.float32)).astype(jnp.bfloat16)
        back_scaled, back_raw, back_r = prepare(back_rows, copy_gain, copy_down)
        hidden_two = (back_raw * back_r[:, None]).astype(jnp.bfloat16)
        back_dlat = jnp.dot(back_cot, copy_upper.T, preferred_element_type=jnp.float32)
        error = (back_dlat * back_r[:, None]).astype(jnp.bfloat16)
        error_groups = error.astype(jnp.float32).reshape(N_EXPERT, TOK_DEV, LATENT)
        hidden_groups = hidden_two.astype(jnp.float32).reshape(N_EXPERT, TOK_DEV, LATENT)
        scaled_groups = back_scaled.astype(jnp.float32).reshape(N_EXPERT, TOK_DEV, D)
        cot_groups = back_cot.astype(jnp.float32).reshape(N_EXPERT, TOK_DEV, D)
        part_down = jnp.einsum('ktr,ktd->krd', error_groups, scaled_groups).astype(jnp.bfloat16)
        part_up = jnp.einsum('ktr,ktd->krd', hidden_groups, cot_groups).astype(jnp.bfloat16)
        part_down = lax.optimization_barrier(part_down)
        part_up = lax.optimization_barrier(part_up)
        partial_value = jnp.stack([lax.optimization_barrier(jnp.sum(part_down.astype(jnp.float32), axis=0)), lax.optimization_barrier(jnp.sum(part_up.astype(jnp.float32), axis=0))])
        share = lax.optimization_barrier(partial_value.astype(jnp.bfloat16))
        grad = share.astype(jnp.float32)
        weights = lax.dynamic_index_in_dim(master, index, 1, keepdims=False)
        first = lax.dynamic_index_in_dim(moment, index, 1, keepdims=False).astype(jnp.float32)
        secnd = lax.dynamic_index_in_dim(second, index, 1, keepdims=False).astype(jnp.float32)
        first = 0.9 * first + 0.1 * grad
        secnd = 0.95 * secnd + 0.05 * grad * grad
        update = first / (1.0 - 0.9 ** 10) / (jnp.sqrt(secnd / (1.0 - 0.95 ** 10)) + 1e-08)
        fresh = weights - 0.01 * (update + 0.1 * weights)
        blocks = jnp.abs(fresh).reshape(2, LATENT // 128, 128, D // 128, 128)
        block_scale = lax.optimization_barrier(jnp.max(blocks, axis=(2, 4))) + 1e-06
        expanded = jnp.repeat(jnp.repeat(block_scale, 128, axis=1), 128, axis=2)
        coded = (fresh / expanded).astype(jnp.bfloat16)
        return (result, coded, block_scale)
    results, coded, block_scale = lax.map(section, jnp.arange(SECTIONS, dtype=jnp.int32))
    leave_fwd = jnp.concatenate([jnp.zeros((1, TOKENS, D), jnp.bfloat16), results[:-1]], axis=0)
    return (leave_fwd, jnp.moveaxis(coded, 0, 1), jnp.moveaxis(block_scale, 0, 1))
```

```python
import jax
import jax.numpy as jnp
from jax import lax
from jax.experimental import pallas as pl
from jax.experimental.pallas import tpu as pltpu
from jax.sharding import PartitionSpec as P

D = 7168
LANES = 128
F32 = jnp.float32
BF16 = jnp.bfloat16
BOTH_LAST = (((1,), (1,)), ((), ()))


def exchange(block, axis, offset):
    count = lax.axis_size(axis)
    return lax.ppermute(block, axis, [(i, i ^ offset) for i in range(count)])


def mirrored(block, axis):
    count = lax.axis_size(axis)
    return lax.ppermute(block, axis, [(i, count - 1 - i) for i in range(count)])


def shifted(block, axis):
    count = lax.axis_size(axis)
    return lax.ppermute(block, axis, [(i, i + 1) for i in range(count - 1)])


def halves_of_sum(block, axis):
    count = lax.axis_size(axis)
    offset = 1
    while True:
        other = exchange(block, axis, offset)
        offset *= 2
        if offset >= count:
            return block, other
        block = block + other


def cost(flops, nbytes):
    return pl.CostEstimate(flops=flops, bytes_accessed=nbytes, transcendentals=0)


def folded_squares(rows):
    tokens, width = rows.shape
    total = jnp.zeros((tokens, LANES), F32)
    for at in range(0, width, LANES):
        part = rows[:, at : at + LANES]
        total = total + part * part
    return total


def fwd_latent_kernel(x_ref, g_ref, a_ref, out_ref):
    latent = a_ref.shape[0]

    @pl.when(pl.program_id(0) == 0)
    def _():
        out_ref[...] = jnp.zeros_like(out_ref)

    rows = x_ref[...].astype(F32)
    scaled = (rows * g_ref[...].astype(F32)).astype(BF16)
    out_ref[:, :latent] += lax.dot_general(scaled, a_ref[...], BOTH_LAST, preferred_element_type=F32)
    out_ref[:, latent:] += folded_squares(rows)


def back_latent_kernel(x_ref, c_ref, g_ref, a_ref, b_ref, out_ref):
    latent = a_ref.shape[0]

    @pl.when(pl.program_id(0) == 0)
    def _():
        out_ref[...] = jnp.zeros_like(out_ref)

    rows = x_ref[...].astype(F32)
    scaled = (rows * g_ref[...].astype(F32)).astype(BF16)
    out_ref[:latent] += lax.dot_general(a_ref[...], scaled, BOTH_LAST, preferred_element_type=F32)
    out_ref[latent : 2 * latent] += lax.dot_general(b_ref[...], c_ref[...], BOTH_LAST, preferred_element_type=F32)
    out_ref[2 * latent :] += folded_squares(rows)


def leaving_kernel(own_ref, other_ref, x_ref, b_ref, *rest):
    out_ref, hidden = rest[-2], rest[-1]
    latent = b_ref.shape[0]

    @pl.when(pl.program_id(0) == 0)
    def _():
        total = own_ref[...] + other_ref[...]
        squares = jnp.sum(total[:, latent:], axis=1, keepdims=True)
        hidden[...] = (total[:, :latent] * lax.rsqrt(squares / D + 1e-06)).astype(BF16)

    out_ref[...] = (
        x_ref[...].astype(F32) + jnp.dot(hidden[...], b_ref[...], preferred_element_type=F32)
    ).astype(BF16)


def grad_kernel(experts, own_ref, other_ref, x_ref, g_ref, c_ref, *rest):
    outs, rows_ref = rest[:-1], rest[-1]
    latent = rows_ref.shape[1]
    depth = latent // experts
    me = lax.axis_index("expert")
    squares = own_ref[2 * latent :] + other_ref[2 * latent :]
    rscale = lax.rsqrt(jnp.sum(squares.T, axis=0, keepdims=True) / D + 1e-06)
    rows_ref[0] = (own_ref[latent : 2 * latent] + other_ref[latent : 2 * latent]) * rscale
    rows_ref[1] = (own_ref[:latent] + other_ref[:latent]) * rscale
    scaled = (x_ref[...].astype(F32) * g_ref[...].astype(F32)).astype(BF16)
    cot = c_ref[...]
    for offset in range(experts):
        at = pl.ds(pl.multiple_of((me ^ offset) * depth, depth), depth)
        error = rows_ref[0, at, :].astype(BF16)
        hidden = rows_ref[1, at, :].astype(BF16)
        outs[offset][0] = jnp.dot(error, scaled, preferred_element_type=F32).astype(BF16)
        outs[offset][1] = jnp.dot(hidden, cot, preferred_element_type=F32).astype(BF16)


def share_kernel(*refs):
    total = refs[0][...].astype(F32)
    for ref in refs[1:-1]:
        total = total + ref[...].astype(F32)
    refs[-1][...] = total.astype(BF16)


def update_kernel(share_ref, master_ref, moment_ref, second_ref, *rest):
    fresh_ref, peak_ref = rest[-2:]
    grad = share_ref[...].astype(F32)
    first = 0.9 * moment_ref[...].astype(F32) + 0.1 * grad
    secnd = 0.95 * second_ref[...].astype(F32) + 0.05 * grad * grad
    update = first / (1.0 - 0.9**10) / (jnp.sqrt(secnd / (1.0 - 0.95**10)) + 1e-08)
    weights = master_ref[...]
    fresh = weights - 0.01 * (update + 0.1 * weights)
    fresh_ref[...] = fresh
    peak = jnp.max(jnp.abs(fresh), axis=1, keepdims=True)
    for block in range(peak.shape[-1] // LANES):
        peak_ref[:, block : block + 1] = peak[:, :, block * LANES : (block + 1) * LANES]


def code_kernel(group, fresh_ref, *rest):
    peak_refs, code_ref, scale_ref, wide = rest[:-3], rest[-3], rest[-2], rest[-1]
    chunks, _, per, _ = peak_refs[0].shape
    rows_of = len(peak_refs) // group
    mine = lax.axis_index("expert") // group
    wide[...] = jnp.zeros_like(wide)
    for far in range(rows_of):
        top = peak_refs[far * group][...]
        for ref in peak_refs[far * group + 1 : (far + 1) * group]:
            top = jnp.maximum(top, ref[...])
        for side in range(2):
            for chunk in range(chunks):
                wide[side, chunk * per : (chunk + 1) * per, :] = top[chunk, side]
        where = pl.ds(mine ^ far, 1)
        for side in range(2):
            scale_ref[side, where, :] = (
                jnp.max(wide[side].T, axis=0, keepdims=True)[:, : chunks * per] + 1e-06
            )
        if far == 0:
            for side in range(2):
                scale = jnp.broadcast_to(jnp.max(wide[side], axis=1, keepdims=True), wide.shape[1:]) + 1e-06
                inverse = 1.0 / scale
                for block in range(chunks * per):
                    at = slice(block * LANES, (block + 1) * LANES)
                    code_ref[side, :, at] = (fresh_ref[side, :, at] * inverse[block : block + 1]).astype(BF16)


def place_kernel(in_ref, *rest):
    rest[-1][...] = in_ref[...]


ANY = pl.BlockSpec(memory_space=pl.ANY)


def whole(shape):
    return pl.BlockSpec(shape, lambda *_: (0,) * len(shape))


def shards(enter_fwd, enter_rev, cot_rev, gain, proj_down, proj_up, master, moment, second):
    tokens, width = enter_fwd.shape[1:]
    latent = proj_down.shape[2]
    experts = lax.axis_size("expert")
    depth = latent // experts
    blocks = width // LANES
    steps = 4 if blocks % 4 == 0 else 2
    tile = width // steps
    chunks = steps
    part = width // chunks
    head = tokens * 3 // 4
    tail = tokens - head

    def token_tile(rows):
        return pl.BlockSpec((None, rows, tile), lambda i: (0, 0, i))

    def gain_tile(copy):
        return pl.BlockSpec((None, 1, tile), lambda i: (copy, 0, i))

    def weight_tile(copy):
        return pl.BlockSpec((None, None, latent, tile), lambda i: (copy, 0, 0, i))

    packed = pl.pallas_call(
        fwd_latent_kernel,
        grid=(steps,),
        in_specs=[token_tile(tokens), gain_tile(0), weight_tile(0)],
        out_specs=whole((tokens, latent + LANES)),
        out_shape=jax.ShapeDtypeStruct((tokens, latent + LANES), F32),
        cost_estimate=cost(2 * tokens * latent * width, 2 * (tokens + latent) * width),
        name="fwd_latent",
    )(enter_fwd, gain, proj_down)
    fwd_pair = halves_of_sum(packed, "dp")

    packed = pl.pallas_call(
        back_latent_kernel,
        grid=(steps,),
        in_specs=[token_tile(tokens), token_tile(tokens), gain_tile(1), weight_tile(1), weight_tile(1)],
        out_specs=whole((2 * latent + tokens, tokens)),
        out_shape=jax.ShapeDtypeStruct((2 * latent + tokens, tokens), F32),
        cost_estimate=cost(4 * tokens * latent * width, 4 * (tokens + latent) * width),
        name="back_latent",
    )(enter_rev, cot_rev, gain, proj_down, proj_up)
    back_pair = halves_of_sum(packed, "dp")

    def leaving_rows(start, count, *after):
        at = start // count
        latent_rows = pl.BlockSpec((count, latent + LANES), lambda i: (at, 0))
        return pl.pallas_call(
            leaving_kernel,
            grid=(steps,),
            in_specs=[
                latent_rows,
                latent_rows,
                pl.BlockSpec((None, count, tile), lambda i: (0, at, i)),
                weight_tile(0),
            ]
            + [ANY] * len(after),
            out_specs=pl.BlockSpec((count, tile), lambda i: (0, i)),
            out_shape=jax.ShapeDtypeStruct((count, width), BF16),
            scratch_shapes=[pltpu.VMEM((count, latent), BF16)],
            cost_estimate=cost(2 * count * latent * width, 2 * (2 * count + latent) * width),
            name="leaving",
        )(*fwd_pair, enter_fwd, proj_up, *after)

    left_head = shifted(leaving_rows(0, head), "pipe")

    quarters = jax.ShapeDtypeStruct((2, depth, part), BF16)
    sums = []
    for chunk in range(chunks):
        pieces = pl.pallas_call(
            lambda *refs: grad_kernel(experts, *refs),
            grid=(1,),
            in_specs=[
                whole((2 * latent + tokens, tokens)),
                whole((2 * latent + tokens, tokens)),
                pl.BlockSpec((None, tokens, part), lambda i, c=chunk: (0, 0, c)),
                pl.BlockSpec((None, 1, part), lambda i, c=chunk: (1, 0, c)),
                pl.BlockSpec((None, tokens, part), lambda i, c=chunk: (0, 0, c)),
            ],
            out_specs=[whole((2, depth, part))] * experts,
            out_shape=[quarters] * experts,
            scratch_shapes=[pltpu.VMEM((2, latent, tokens), F32)],
            cost_estimate=cost(4 * tokens * latent * part, 4 * (tokens + latent) * part),
            name="grads",
        )(*back_pair, enter_rev, gain, cot_rev)
        sums.append([pieces[0]] + [exchange(pieces[k], "expert", k) for k in range(1, experts)])

    fresh = peaks = None
    shares = []
    for chunk in range(chunks):
        share = pl.pallas_call(
            share_kernel,
            grid=(1,),
            in_specs=[whole((2, depth, part))] * experts,
            out_specs=whole((2, depth, part)),
            out_shape=quarters,
            cost_estimate=cost(0, 2 * 2 * depth * part * (experts + 1)),
            name="share",
        )(*sums[chunk])
        shares.append(share)
    left_tail = shifted(leaving_rows(head, tail, shares[-1]), "pipe")

    for chunk in range(chunks):
        state = pl.BlockSpec((2, None, depth, part), lambda i, c=chunk: (0, 0, 0, c))
        kept = () if fresh is None else (fresh, peaks)
        fresh, peaks = pl.pallas_call(
            update_kernel,
            grid=(1,),
            in_specs=[whole((2, depth, part)), state, state, state] + [ANY] * len(kept),
            out_specs=[
                pl.BlockSpec((2, depth, part), lambda i, c=chunk: (0, 0, c)),
                pl.BlockSpec((None, 2, part // LANES, LANES), lambda i, c=chunk: (c, 0, 0, 0)),
            ],
            out_shape=[
                jax.ShapeDtypeStruct((2, depth, width), F32),
                jax.ShapeDtypeStruct((chunks, 2, part // LANES, LANES), F32),
            ],
            input_output_aliases={4 + k: k for k in range(len(kept))},
            cost_estimate=cost(20 * 2 * depth * part, 14 * 2 * depth * part),
            name="update",
        )(mirrored(shares[chunk], "pipe"), master, moment, second, *kept)

    peak_rows = [peaks] + [exchange(peaks, "expert", k) for k in range(1, experts)]
    group = LANES // depth
    coded, scales = pl.pallas_call(
        lambda *refs: code_kernel(group, *refs),
        grid=(1,),
        in_specs=[whole((2, depth, width))] + [whole(peaks.shape)] * experts,
        out_specs=[
            pl.BlockSpec((2, None, depth, width), lambda i: (0, 0, 0, 0)),
            pl.BlockSpec((2, None, experts // group, blocks), lambda i: (0, 0, 0, 0)),
        ],
        out_shape=[
            jax.ShapeDtypeStruct((2, 1, depth, width), BF16),
            jax.ShapeDtypeStruct((2, 1, experts // group, blocks), F32),
        ],
        scratch_shapes=[pltpu.VMEM((2, LANES, LANES), F32)],
        cost_estimate=cost(2 * 2 * depth * width, 6 * 2 * depth * width),
        name="codes",
    )(fresh, *peak_rows)

    unit = tail
    placed = None
    for start, rows in ((0, left_head), (head, left_tail)):
        kept = () if placed is None else (placed,)
        placed = pl.pallas_call(
            place_kernel,
            grid=(rows.shape[0] // unit,),
            in_specs=[pl.BlockSpec((unit, width), lambda i: (i, 0))] + [ANY] * len(kept),
            out_specs=pl.BlockSpec((None, unit, width), lambda i, s=start // unit: (0, i + s, 0)),
            out_shape=jax.ShapeDtypeStruct((1, tokens, width), BF16),
            input_output_aliases={1 + k: k for k in range(len(kept))},
            cost_estimate=cost(0, 4 * rows.shape[0] * width),
            name="place",
        )(rows, *kept)
    return (placed, coded, scales)


def solution(mesh):
    in_specs = (
        P("pipe", "expert", "dp"),
        P("pipe", "expert", "dp"),
        P("pipe", "expert", "dp"),
        P(None, "pipe", "dp"),
        P(None, "pipe", None, "dp"),
        P(None, "pipe", None, "dp"),
        P(None, "pipe", "expert", "dp"),
        P(None, "pipe", "expert", "dp"),
        P(None, "pipe", "expert", "dp"),
    )
    out_specs = (
        P("pipe", "expert", "dp"),
        P(None, "pipe", "expert", "dp"),
        P(None, "pipe", None, "dp"),
    )
    return jax.shard_map(shards, mesh=mesh, in_specs=in_specs, out_specs=out_specs, check_vma=False)
```

```python
import jax
import jax.numpy as jnp
from jax import lax
from jax.experimental import pallas as pl
from jax.experimental.pallas import tpu as pltpu
from jax.sharding import PartitionSpec as P

D = 7168
LANES = 128
F32 = jnp.float32
BF16 = jnp.bfloat16
BOTH_LAST = (((1,), (1,)), ((), ()))


def exchange(block, axis, offset):
    count = lax.axis_size(axis)
    return lax.ppermute(block, axis, [(i, i ^ offset) for i in range(count)])


def mirrored(block, axis):
    count = lax.axis_size(axis)
    return lax.ppermute(block, axis, [(i, count - 1 - i) for i in range(count)])


def shifted(block, axis):
    count = lax.axis_size(axis)
    return lax.ppermute(block, axis, [(i, i + 1) for i in range(count - 1)])


def halves_of_sum(block, axis):
    count = lax.axis_size(axis)
    offset = 1
    while True:
        other = exchange(block, axis, offset)
        offset *= 2
        if offset >= count:
            return block, other
        block = block + other


ROOM = pltpu.CompilerParams(vmem_limit_bytes=16 << 20)


def cost(flops, nbytes):
    return pl.CostEstimate(flops=flops, bytes_accessed=nbytes, transcendentals=0)


def folded_squares(rows):
    tokens, width = rows.shape
    total = jnp.zeros((tokens, LANES), F32)
    for at in range(0, width, LANES):
        part = rows[:, at : at + LANES]
        total = total + part * part
    return total


def fwd_latent_kernel(x_ref, g_ref, a_ref, out_ref):
    latent = a_ref.shape[0]

    @pl.when(pl.program_id(0) == 0)
    def _():
        out_ref[...] = jnp.zeros_like(out_ref)

    rows = x_ref[...].astype(F32)
    scaled = (rows * g_ref[...].astype(F32)).astype(BF16)
    out_ref[:, :latent] += lax.dot_general(scaled, a_ref[...], BOTH_LAST, preferred_element_type=F32)
    out_ref[:, latent:] += folded_squares(rows)


def back_latent_kernel(x_ref, c_ref, g_ref, a_ref, b_ref, *rest):
    out_ref = rest[-1]
    latent = a_ref.shape[0]

    @pl.when(pl.program_id(0) == 0)
    def _():
        out_ref[...] = jnp.zeros_like(out_ref)

    rows = x_ref[...].astype(F32)
    scaled = (rows * g_ref[...].astype(F32)).astype(BF16)
    out_ref[:latent] += lax.dot_general(a_ref[...], scaled, BOTH_LAST, preferred_element_type=F32)
    out_ref[latent : 2 * latent] += lax.dot_general(b_ref[...], c_ref[...], BOTH_LAST, preferred_element_type=F32)
    out_ref[2 * latent :] += folded_squares(rows)


def leaving_kernel(own_ref, other_ref, x_ref, b_ref, *rest):
    out_ref, hidden = rest[-2], rest[-1]
    latent = b_ref.shape[0]

    @pl.when(pl.program_id(0) == 0)
    def _():
        total = own_ref[...] + other_ref[...]
        squares = jnp.sum(total[:, latent:], axis=1, keepdims=True)
        hidden[...] = (total[:, :latent] * lax.rsqrt(squares / D + 1e-06)).astype(BF16)

    out_ref[...] = (
        x_ref[...].astype(F32) + jnp.dot(hidden[...], b_ref[...], preferred_element_type=F32)
    ).astype(BF16)


def grad_kernel(experts, own_ref, other_ref, x_ref, g_ref, c_ref, *rest):
    outs, rows_ref = rest[-1 - experts : -1], rest[-1]
    latent = rows_ref.shape[1]
    depth = latent // experts
    me = lax.axis_index("expert")
    squares = own_ref[2 * latent :] + other_ref[2 * latent :]
    rscale = lax.rsqrt(jnp.sum(squares.T, axis=0, keepdims=True) / D + 1e-06)
    rows_ref[0] = (own_ref[latent : 2 * latent] + other_ref[latent : 2 * latent]) * rscale
    rows_ref[1] = (own_ref[:latent] + other_ref[:latent]) * rscale
    scaled = (x_ref[...].astype(F32) * g_ref[...].astype(F32)).astype(BF16)
    cot = c_ref[...]
    for offset in range(experts):
        at = pl.ds(pl.multiple_of((me ^ offset) * depth, depth), depth)
        error = rows_ref[0, at, :].astype(BF16)
        hidden = rows_ref[1, at, :].astype(BF16)
        outs[offset][0] = jnp.dot(error, scaled, preferred_element_type=F32).astype(BF16)
        outs[offset][1] = jnp.dot(hidden, cot, preferred_element_type=F32).astype(BF16)


def share_kernel(experts, *refs):
    total = refs[0][...].astype(F32)
    for ref in refs[1:experts]:
        total = total + ref[...].astype(F32)
    refs[-1][...] = total.astype(BF16)


def update_kernel(share_ref, master_ref, moment_ref, second_ref, *rest):
    fresh_ref, peak_ref = rest[-2:]
    grad = share_ref[...].astype(F32)
    first = 0.9 * moment_ref[...].astype(F32) + 0.1 * grad
    secnd = 0.95 * second_ref[...].astype(F32) + 0.05 * grad * grad
    update = first / (1.0 - 0.9**10) / (jnp.sqrt(secnd / (1.0 - 0.95**10)) + 1e-08)
    weights = master_ref[...]
    fresh = weights - 0.01 * (update + 0.1 * weights)
    fresh_ref[...] = fresh
    peak = jnp.max(jnp.abs(fresh), axis=1, keepdims=True)
    for block in range(peak.shape[-1] // LANES):
        peak_ref[:, block : block + 1] = peak[:, :, block * LANES : (block + 1) * LANES]


def code_kernel(group, fresh_ref, *rest):
    peak_refs, code_ref, scale_ref, wide = rest[:-3], rest[-3], rest[-2], rest[-1]
    chunks, _, per, _ = peak_refs[0].shape
    rows_of = len(peak_refs) // group
    mine = lax.axis_index("expert") // group
    wide[...] = jnp.zeros_like(wide)
    for far in range(rows_of):
        top = peak_refs[far * group][...]
        for ref in peak_refs[far * group + 1 : (far + 1) * group]:
            top = jnp.maximum(top, ref[...])
        for side in range(2):
            for chunk in range(chunks):
                wide[side, chunk * per : (chunk + 1) * per, :] = top[chunk, side]
        where = pl.ds(mine ^ far, 1)
        for side in range(2):
            scale_ref[side, where, :] = (
                jnp.max(wide[side].T, axis=0, keepdims=True)[:, : chunks * per] + 1e-06
            )
        if far == 0:
            for side in range(2):
                scale = jnp.broadcast_to(jnp.max(wide[side], axis=1, keepdims=True), wide.shape[1:]) + 1e-06
                inverse = 1.0 / scale
                for block in range(chunks * per):
                    at = slice(block * LANES, (block + 1) * LANES)
                    code_ref[side, :, at] = (fresh_ref[side, :, at] * inverse[block : block + 1]).astype(BF16)


def place_kernel(in_ref, *rest):
    rest[-1][...] = in_ref[...]


ANY = pl.BlockSpec(memory_space=pl.ANY)


def whole(shape):
    return pl.BlockSpec(shape, lambda *_: (0,) * len(shape))


def shards(enter_fwd, enter_rev, cot_rev, gain, proj_down, proj_up, master, moment, second):
    tokens, width = enter_fwd.shape[1:]
    latent = proj_down.shape[2]
    experts = lax.axis_size("expert")
    depth = latent // experts
    blocks = width // LANES
    steps = 4 if blocks % 4 == 0 else 2
    tile = width // steps
    chunks = steps
    part = width // chunks
    head = tokens * 3 // 4
    tail = tokens - head

    def token_tile(rows):
        return pl.BlockSpec((None, rows, tile), lambda i: (0, 0, i))

    def gain_tile(copy):
        return pl.BlockSpec((None, 1, tile), lambda i: (copy, 0, i))

    def weight_tile(copy):
        return pl.BlockSpec((None, None, latent, tile), lambda i: (copy, 0, 0, i))

    packed = pl.pallas_call(
        fwd_latent_kernel,
        grid=(steps,),
        in_specs=[token_tile(tokens), gain_tile(0), weight_tile(0)],
        out_specs=whole((tokens, latent + LANES)),
        out_shape=jax.ShapeDtypeStruct((tokens, latent + LANES), F32),
        compiler_params=ROOM,
        cost_estimate=cost(2 * tokens * latent * width, 2 * (tokens + latent) * width),
        name="fwd_latent",
    )(enter_fwd, gain, proj_down)
    fwd_pair = halves_of_sum(packed, "dp")

    packed = pl.pallas_call(
        back_latent_kernel,
        grid=(steps,),
        in_specs=[token_tile(tokens), token_tile(tokens), gain_tile(1), weight_tile(1), weight_tile(1), ANY],
        out_specs=whole((2 * latent + tokens, tokens)),
        out_shape=jax.ShapeDtypeStruct((2 * latent + tokens, tokens), F32),
        compiler_params=ROOM,
        cost_estimate=cost(4 * tokens * latent * width, 4 * (tokens + latent) * width),
        name="back_latent",
    )(enter_rev, cot_rev, gain, proj_down, proj_up, packed)
    back_pair = halves_of_sum(packed, "dp")

    def leaving_rows(start, count, *after):
        at = start // count
        latent_rows = pl.BlockSpec((count, latent + LANES), lambda i: (at, 0))
        return pl.pallas_call(
            leaving_kernel,
            grid=(steps,),
            in_specs=[
                latent_rows,
                latent_rows,
                pl.BlockSpec((None, count, tile), lambda i: (0, at, i)),
                weight_tile(0),
            ]
            + [ANY] * len(after),
            out_specs=pl.BlockSpec((count, tile), lambda i: (0, i)),
            out_shape=jax.ShapeDtypeStruct((count, width), BF16),
            scratch_shapes=[pltpu.VMEM((count, latent), BF16)],
            compiler_params=ROOM,
        cost_estimate=cost(2 * count * latent * width, 2 * (2 * count + latent) * width),
            name="leaving",
        )(*fwd_pair, enter_fwd, proj_up, *after)

    first_rows = leaving_rows(0, head)
    left_head = shifted(first_rows, "pipe")

    quarters = jax.ShapeDtypeStruct((2, depth, part), BF16)

    def grads(chunk, *after):
        return pl.pallas_call(
            lambda *refs: grad_kernel(experts, *refs),
            grid=(1,),
            in_specs=[
                whole((2 * latent + tokens, tokens)),
                whole((2 * latent + tokens, tokens)),
                pl.BlockSpec((None, tokens, part), lambda i: (0, 0, chunk)),
                pl.BlockSpec((None, 1, part), lambda i: (1, 0, chunk)),
                pl.BlockSpec((None, tokens, part), lambda i: (0, 0, chunk)),
            ]
            + [ANY] * len(after),
            out_specs=[whole((2, depth, part))] * experts,
            out_shape=[quarters] * experts,
            scratch_shapes=[pltpu.VMEM((2, latent, tokens), F32)],
            compiler_params=ROOM,
            cost_estimate=cost(4 * tokens * latent * part, 4 * (tokens + latent) * part),
            name="grads",
        )(*back_pair, enter_rev, gain, cot_rev, *after)

    def summed(pieces, *after):
        others = [exchange(pieces[k], "expert", k) for k in range(1, experts)]
        return pl.pallas_call(
            lambda *refs: share_kernel(experts, *refs),
            grid=(1,),
            in_specs=[whole((2, depth, part))] * experts + [ANY] * len(after),
            out_specs=whole((2, depth, part)),
            out_shape=quarters,
            compiler_params=ROOM,
            cost_estimate=cost(0, 2 * 2 * depth * part * (experts + 1)),
            name="share",
        )(pieces[0], *others, *after)

    shares, arrived = [], [left_head]
    for chunk in range(chunks):
        pieces = grads(chunk, first_rows, *shares[-2:-1])
        shares.append(summed(pieces, *arrived[chunk - 1 : chunk]))
        arrived.append(mirrored(shares[-1], "pipe"))
    fresh = peaks = None
    left_tail = shifted(leaving_rows(head, tail, shares[-1]), "pipe")

    for chunk in range(chunks):
        state = pl.BlockSpec((2, None, depth, part), lambda i, c=chunk: (0, 0, 0, c))
        kept = () if fresh is None else (fresh, peaks)
        fresh, peaks = pl.pallas_call(
            update_kernel,
            grid=(1,),
            in_specs=[whole((2, depth, part)), state, state, state] + [ANY] * len(kept),
            out_specs=[
                pl.BlockSpec((2, depth, part), lambda i, c=chunk: (0, 0, c)),
                pl.BlockSpec((None, 2, part // LANES, LANES), lambda i, c=chunk: (c, 0, 0, 0)),
            ],
            out_shape=[
                jax.ShapeDtypeStruct((2, depth, width), F32),
                jax.ShapeDtypeStruct((chunks, 2, part // LANES, LANES), F32),
            ],
            input_output_aliases={4 + k: k for k in range(len(kept))},
            compiler_params=ROOM,
        cost_estimate=cost(20 * 2 * depth * part, 14 * 2 * depth * part),
            name="update",
        )(arrived[1 + chunk], master, moment, second, *kept)

    peak_rows = [peaks] + [exchange(peaks, "expert", k) for k in range(1, experts)]
    group = LANES // depth
    coded, scales = pl.pallas_call(
        lambda *refs: code_kernel(group, *refs),
        grid=(1,),
        in_specs=[whole((2, depth, width))] + [whole(peaks.shape)] * experts,
        out_specs=[
            pl.BlockSpec((2, None, depth, width), lambda i: (0, 0, 0, 0)),
            pl.BlockSpec((2, None, experts // group, blocks), lambda i: (0, 0, 0, 0)),
        ],
        out_shape=[
            jax.ShapeDtypeStruct((2, 1, depth, width), BF16),
            jax.ShapeDtypeStruct((2, 1, experts // group, blocks), F32),
        ],
        scratch_shapes=[pltpu.VMEM((2, LANES, LANES), F32)],
        compiler_params=ROOM,
        cost_estimate=cost(2 * 2 * depth * width, 6 * 2 * depth * width),
        name="codes",
    )(fresh, *peak_rows)

    unit = tail
    placed = None
    for start, rows in ((0, left_head), (head, left_tail)):
        kept = () if placed is None else (placed,)
        placed = pl.pallas_call(
            place_kernel,
            grid=(rows.shape[0] // unit,),
            in_specs=[pl.BlockSpec((unit, width), lambda i: (i, 0))] + [ANY] * len(kept),
            out_specs=pl.BlockSpec((None, unit, width), lambda i, s=start // unit: (0, i + s, 0)),
            out_shape=jax.ShapeDtypeStruct((1, tokens, width), BF16),
            input_output_aliases={1 + k: k for k in range(len(kept))},
            compiler_params=ROOM,
        cost_estimate=cost(0, 4 * rows.shape[0] * width),
            name="place",
        )(rows, *kept)
    return (placed, coded, scales)


def solution(mesh):
    in_specs = (
        P("pipe", "expert", "dp"),
        P("pipe", "expert", "dp"),
        P("pipe", "expert", "dp"),
        P(None, "pipe", "dp"),
        P(None, "pipe", None, "dp"),
        P(None, "pipe", None, "dp"),
        P(None, "pipe", "expert", "dp"),
        P(None, "pipe", "expert", "dp"),
        P(None, "pipe", "expert", "dp"),
    )
    out_specs = (
        P("pipe", "expert", "dp"),
        P(None, "pipe", "expert", "dp"),
        P(None, "pipe", None, "dp"),
    )
    return jax.shard_map(shards, mesh=mesh, in_specs=in_specs, out_specs=out_specs, check_vma=False)
```

```python
import jax
import jax.numpy as jnp
from jax import lax
from jax.experimental import pallas as pl
from jax.experimental.pallas import tpu as pltpu
from jax.sharding import PartitionSpec as P

D = 7168
LANES = 128
F32 = jnp.float32
BF16 = jnp.bfloat16
BOTH_LAST = (((1,), (1,)), ((), ()))


def exchange(block, axis, offset):
    count = lax.axis_size(axis)
    return lax.ppermute(block, axis, [(i, i ^ offset) for i in range(count)])


def mirrored(block, axis):
    count = lax.axis_size(axis)
    return lax.ppermute(block, axis, [(i, count - 1 - i) for i in range(count)])


def shifted(block, axis):
    count = lax.axis_size(axis)
    return lax.ppermute(block, axis, [(i, i + 1) for i in range(count - 1)])


def halves_of_sum(block, axis):
    count = lax.axis_size(axis)
    offset = 1
    while True:
        other = exchange(block, axis, offset)
        offset *= 2
        if offset >= count:
            return block, other
        block = block + other


ROOM = pltpu.CompilerParams(vmem_limit_bytes=16 << 20)


def cost(flops, nbytes):
    return pl.CostEstimate(flops=flops, bytes_accessed=nbytes, transcendentals=0)


def folded_squares(rows):
    tokens, width = rows.shape
    total = jnp.zeros((tokens, LANES), F32)
    for at in range(0, width, LANES):
        part = rows[:, at : at + LANES]
        total = total + part * part
    return total


def latent_kernel(tiles, x1, a1, x2, c2, a2, b2, gain_ref, out_ref, vx1, va1, vx2, vc2, va2, vb2, sems):
    tokens, width = vx1.shape
    latent = va1.shape[0]
    tile = width // tiles
    jobs = []
    for names in (((x1, vx1), (a1, va1)), ((x2, vx2), (a2, va2)), ((c2, vc2), (b2, vb2))):
        for at in range(tiles):
            cols = pl.ds(at * tile, tile)
            jobs.append([])
            for src, dst in names:
                copy = pltpu.make_async_copy(
                    src.at[:, cols], dst.at[:, cols], sems.at[2 * len(jobs) - 2 + len(jobs[-1])]
                )
                copy.start()
                jobs[-1].append(copy)
    gains = gain_ref[...].astype(F32)

    def product(job, left, right):
        total = None
        squares = jnp.zeros((tokens, LANES), F32)
        for at in range(tiles):
            for copy in jobs[job * tiles + at]:
                copy.wait()
            cols = slice(at * tile, (at + 1) * tile)
            one, two, folded = left(cols), right(cols), None
            if job < 2:
                rows = (vx1, vx2)[job][:, cols].astype(F32)
                squares += folded_squares(rows)
                scaled = (rows * gains[job : job + 1, cols]).astype(BF16)
                one = scaled if one is None else one
                two = scaled if two is None else two
            term = lax.dot_general(one, two, BOTH_LAST, preferred_element_type=F32)
            total = term if total is None else total + term
        return total, squares

    raw, squares = product(0, lambda c: None, lambda c: va1[:, c])
    base = 2 * latent + tokens
    for at in range(latent // LANES):
        out_ref[base + at * tokens : base + (at + 1) * tokens] = raw[:, at * LANES : (at + 1) * LANES]
    out_ref[base + (latent // LANES) * tokens :] = squares
    raw, squares = product(1, lambda c: va2[:, c], lambda c: None)
    out_ref[:latent] = raw
    out_ref[2 * latent : base] = squares
    out_ref[latent : 2 * latent], _ = product(2, lambda c: vb2[:, c], lambda c: vc2[:, c])


def leaving_kernel(own_ref, other_ref, x_ref, b_ref, out_ref, hidden):
    latent = b_ref.shape[0]
    tokens = x_ref.shape[0]

    @pl.when(pl.program_id(0) == 0)
    def _():
        base = own_ref.shape[0] - tokens
        squares = jnp.sum(own_ref[base:] + other_ref[base:], axis=1, keepdims=True)
        rscale = lax.rsqrt(squares / D + 1e-06)
        base -= (latent // LANES) * tokens
        for at in range(latent // LANES):
            rows = slice(base + at * tokens, base + (at + 1) * tokens)
            hidden[:, at * LANES : (at + 1) * LANES] = ((own_ref[rows] + other_ref[rows]) * rscale).astype(BF16)

    out_ref[...] = (
        x_ref[...].astype(F32) + jnp.dot(hidden[...], b_ref[...], preferred_element_type=F32)
    ).astype(BF16)


def grad_kernel(orders, own_ref, other_ref, x_ref, g_ref, c_ref, *rest):
    (down_keep, up_keep, down_send, up_send), rows_ref = rest[-5:-1], rest[-1]
    latent = rows_ref.shape[0]
    experts = len(orders[0])
    depth = latent // experts
    me = lax.axis_index("expert")
    squares = own_ref[2 * latent : 2 * latent + LANES] + other_ref[2 * latent : 2 * latent + LANES]
    rscale = lax.rsqrt(jnp.sum(squares.T, axis=0, keepdims=True) / D + 1e-06)
    scaled = (x_ref[...].astype(F32) * g_ref[1:2].astype(F32)).astype(BF16)
    for base, order, right, keep, send in (
        (latent, orders[0], scaled, down_keep, down_send),
        (0, orders[1], c_ref[...], up_keep, up_send),
    ):
        rows_ref[...] = (own_ref[base : base + latent] + other_ref[base : base + latent]) * rscale
        for half, out in enumerate((keep, send)):
            some = order[half * experts // 2 : (half + 1) * experts // 2]
            left = jnp.concatenate(
                [rows_ref[pl.ds(pl.multiple_of((me ^ offset) * depth, depth), depth), :] for offset in some]
            )
            out[...] = jnp.dot(left.astype(BF16), right, preferred_element_type=F32).astype(BF16)


def fold_kernel(down_keep, down_in, up_keep, up_in, *rest):
    outs = rest[-4:]
    for keep, more, kept, send in ((down_keep, down_in, outs[0], outs[2]), (up_keep, up_in, outs[1], outs[3])):
        total = keep[...].astype(F32) + more[...].astype(F32)
        half = total.shape[0] // 2
        kept[...] = total[:half]
        send[...] = total[half:].astype(BF16)


def share_kernel(down_keep, down_in, up_keep, up_in, *rest):
    out_ref = rest[-1]
    out_ref[0] = (down_keep[...].astype(F32) + down_in[...].astype(F32)).astype(BF16)
    out_ref[1] = (up_keep[...].astype(F32) + up_in[...].astype(F32)).astype(BF16)


def update_kernel(share_ref, master_ref, moment_ref, second_ref, *rest):
    fresh_ref, peak_ref = rest[-2:]
    grad = share_ref[...].astype(F32)
    first = 0.9 * moment_ref[...].astype(F32) + 0.1 * grad
    secnd = 0.95 * second_ref[...].astype(F32) + 0.05 * grad * grad
    update = first / (1.0 - 0.9**10) / (jnp.sqrt(secnd / (1.0 - 0.95**10)) + 1e-08)
    weights = master_ref[...]
    fresh = weights - 0.01 * (update + 0.1 * weights)
    fresh_ref[...] = fresh
    peak = jnp.max(jnp.abs(fresh), axis=1, keepdims=True)
    for block in range(peak.shape[-1] // LANES):
        peak_ref[:, block : block + 1] = peak[:, :, block * LANES : (block + 1) * LANES]


def code_kernel(group, fresh_ref, *rest):
    peak_refs, code_ref, scale_ref, wide = rest[:-3], rest[-3], rest[-2], rest[-1]
    chunks, _, per, _ = peak_refs[0].shape
    rows_of = len(peak_refs) // group
    mine = lax.axis_index("expert") // group
    wide[...] = jnp.zeros_like(wide)
    for far in range(rows_of):
        top = peak_refs[far * group][...]
        for ref in peak_refs[far * group + 1 : (far + 1) * group]:
            top = jnp.maximum(top, ref[...])
        for side in range(2):
            for chunk in range(chunks):
                wide[side, chunk * per : (chunk + 1) * per, :] = top[chunk, side]
        where = pl.ds(mine ^ far, 1)
        for side in range(2):
            scale_ref[side, where, :] = (
                jnp.max(wide[side].T, axis=0, keepdims=True)[:, : chunks * per] + 1e-06
            )
        if far == 0:
            for side in range(2):
                scale = jnp.broadcast_to(jnp.max(wide[side], axis=1, keepdims=True), wide.shape[1:]) + 1e-06
                inverse = 1.0 / scale
                for block in range(chunks * per):
                    at = slice(block * LANES, (block + 1) * LANES)
                    code_ref[side, :, at] = (fresh_ref[side, :, at] * inverse[block : block + 1]).astype(BF16)


ANY = pl.BlockSpec(memory_space=pl.ANY)


def whole(shape):
    return pl.BlockSpec(shape, lambda *_: (0,) * len(shape))


def shards(enter_fwd, enter_rev, cot_rev, gain, proj_down, proj_up, master, moment, second):
    tokens, width = enter_fwd.shape[1:]
    latent = proj_down.shape[2]
    experts = lax.axis_size("expert")
    depth = latent // experts
    blocks = width // LANES
    tiles = 4 if blocks % 4 == 0 else 2
    tile = width // tiles
    chunks = 2
    part = width // chunks
    gains = gain.reshape(2, width)

    def streamed(array):
        return pltpu.with_memory_space_constraint(array, pltpu.HBM)

    pack_rows = 2 * latent + tokens + (latent // LANES + 1) * tokens
    packed = pl.pallas_call(
        lambda x1, x2, c2, down, up, *refs: latent_kernel(
            tiles, x1.at[0], down.at[0, 0], x2.at[0], c2.at[0], down.at[1, 0], up.at[1, 0], *refs
        ),
        in_specs=[ANY] * 5 + [pl.BlockSpec(memory_space=pltpu.VMEM)],
        out_specs=pl.BlockSpec(memory_space=pltpu.VMEM),
        out_shape=jax.ShapeDtypeStruct((pack_rows, LANES), F32),
        scratch_shapes=[
            pltpu.VMEM((tokens, width), BF16),
            pltpu.VMEM((latent, width), BF16),
            pltpu.VMEM((tokens, width), BF16),
            pltpu.VMEM((tokens, width), BF16),
            pltpu.VMEM((latent, width), BF16),
            pltpu.VMEM((latent, width), BF16),
            pltpu.SemaphoreType.DMA((6 * tiles,)),
        ],
        compiler_params=ROOM,
        cost_estimate=cost(6 * tokens * latent * width, 6 * (tokens + latent) * width),
        name="latents",
    )(streamed(enter_fwd), streamed(enter_rev), streamed(cot_rev), streamed(proj_down), streamed(proj_up), gains)
    pair = halves_of_sum(packed, "dp")

    first_rows = pl.pallas_call(
        leaving_kernel,
        grid=(tiles,),
        in_specs=[
            whole((pack_rows, LANES)),
            whole((pack_rows, LANES)),
            pl.BlockSpec((None, tokens, tile), lambda i: (0, 0, i)),
            pl.BlockSpec((None, None, latent, tile), lambda i: (0, 0, 0, i)),
        ],
        out_specs=pl.BlockSpec((tokens, tile), lambda i: (0, i)),
        out_shape=jax.ShapeDtypeStruct((tokens, width), BF16),
        scratch_shapes=[pltpu.VMEM((tokens, latent), BF16)],
        compiler_params=ROOM,
        cost_estimate=cost(2 * tokens * latent * width, 2 * (2 * tokens + latent) * width),
        name="leaving",
    )(*pair, enter_fwd, proj_up)
    left = shifted(first_rows, "pipe")

    levels = experts.bit_length() - 1
    orders = [[sum((i >> k & 1) << (levels - 1 - k) for k in range(levels)) for i in range(experts)], list(range(experts))]

    def split(kernel, rows, keep_type, name, *operands, specs=None, scratch=(), flops=0):
        return pl.pallas_call(
            kernel,
            grid=(1,),
            in_specs=[whole(o.shape) for o in operands] if specs is None else specs,
            out_specs=[whole((rows, part))] * 4,
            out_shape=[jax.ShapeDtypeStruct((rows, part), t) for t in (keep_type, keep_type, BF16, BF16)],
            scratch_shapes=scratch,
            compiler_params=ROOM,
            cost_estimate=cost(flops, 12 * rows * part),
            name=name,
        )(*operands)

    def columns(rows, chunk):
        return pl.BlockSpec((None, rows, part), lambda i: (0, 0, chunk))

    arrived = []
    last = share = first_rows
    for chunk in range(chunks):
        down, up, down_out, up_out = split(
            lambda *refs: grad_kernel(orders, *refs),
            latent // 2,
            BF16,
            "grads",
            *pair,
            enter_rev,
            gains,
            cot_rev,
            last,
            share,
            specs=[
                whole((pack_rows, LANES)),
                whole((pack_rows, LANES)),
                columns(tokens, chunk),
                pl.BlockSpec((2, part), lambda i, c=chunk: (0, c)),
                columns(tokens, chunk),
                ANY,
                ANY,
            ],
            scratch=[pltpu.VMEM((latent, tokens), F32)],
            flops=4 * tokens * latent * part,
        )
        for level in range(levels):
            down_in = exchange(down_out, "expert", 1 << level)
            up_in = exchange(up_out, "expert", 1 << (levels - 1 - level))
            if level < levels - 1:
                down, up, down_out, up_out = split(
                    fold_kernel,
                    latent >> (level + 2),
                    F32,
                    "fold",
                    down,
                    down_in,
                    up,
                    up_in,


                )
        share = pl.pallas_call(
            share_kernel,
            grid=(1,),
            in_specs=[whole((depth, part))] * 4 + [ANY] * len(arrived),
            out_specs=whole((2, depth, part)),
            out_shape=jax.ShapeDtypeStruct((2, depth, part), BF16),
            compiler_params=ROOM,
            cost_estimate=cost(0, 16 * depth * part),
            name="share",
        )(down, down_in, up, up_in, *arrived)
        arrived = arrived + [mirrored(share, "pipe")]
        last = left if chunk == 0 else share

    fresh = peaks = None
    for chunk in range(chunks):
        state = pl.BlockSpec((2, None, depth, part), lambda i, c=chunk: (0, 0, 0, c))
        kept = () if fresh is None else (fresh, peaks)
        fresh, peaks = pl.pallas_call(
            update_kernel,
            grid=(1,),
            in_specs=[whole((2, depth, part)), state, state, state] + [ANY] * len(kept),
            out_specs=[
                pl.BlockSpec((2, depth, part), lambda i, c=chunk: (0, 0, c)),
                pl.BlockSpec((None, 2, part // LANES, LANES), lambda i, c=chunk: (c, 0, 0, 0)),
            ],
            out_shape=[
                jax.ShapeDtypeStruct((2, depth, width), F32),
                jax.ShapeDtypeStruct((chunks, 2, part // LANES, LANES), F32),
            ],
            input_output_aliases={4 + k: k for k in range(len(kept))},
            compiler_params=ROOM,
        cost_estimate=cost(20 * 2 * depth * part, 14 * 2 * depth * part),
            name="update",
        )(arrived[chunk], master, moment, second, *kept)

    peak_rows = [peaks] + [exchange(peaks, "expert", k) for k in range(1, experts)]
    group = LANES // depth
    coded, scales = pl.pallas_call(
        lambda *refs: code_kernel(group, *refs),
        grid=(1,),
        in_specs=[whole((2, depth, width))] + [whole(peaks.shape)] * experts,
        out_specs=[
            pl.BlockSpec((2, None, depth, width), lambda i: (0, 0, 0, 0)),
            pl.BlockSpec((2, None, experts // group, blocks), lambda i: (0, 0, 0, 0)),
        ],
        out_shape=[
            jax.ShapeDtypeStruct((2, 1, depth, width), BF16),
            jax.ShapeDtypeStruct((2, 1, experts // group, blocks), F32),
        ],
        scratch_shapes=[pltpu.VMEM((2, LANES, LANES), F32)],
        compiler_params=ROOM,
        cost_estimate=cost(2 * 2 * depth * width, 6 * 2 * depth * width),
        name="codes",
    )(fresh, *peak_rows)

    return (left[None], coded, scales)


def solution(mesh):
    in_specs = (
        P("pipe", "expert", "dp"),
        P("pipe", "expert", "dp"),
        P("pipe", "expert", "dp"),
        P(None, "pipe", "dp"),
        P(None, "pipe", None, "dp"),
        P(None, "pipe", None, "dp"),
        P(None, "pipe", "expert", "dp"),
        P(None, "pipe", "expert", "dp"),
        P(None, "pipe", "expert", "dp"),
    )
    out_specs = (
        P("pipe", "expert", "dp"),
        P(None, "pipe", "expert", "dp"),
        P(None, "pipe", None, "dp"),
    )
    return jax.shard_map(shards, mesh=mesh, in_specs=in_specs, out_specs=out_specs, check_vma=False)
```

```python
import jax
import jax.numpy as jnp
from jax import lax
from jax.experimental import pallas as pl
from jax.experimental.pallas import tpu as pltpu
from jax.sharding import PartitionSpec as P

D = 7168
LANES = 128
F32 = jnp.float32
BF16 = jnp.bfloat16
BOTH_LAST = (((1,), (1,)), ((), ()))


def exchange(block, axis, offset):
    count = lax.axis_size(axis)
    return lax.ppermute(block, axis, [(i, i ^ offset) for i in range(count)])


def mirrored(block, axis):
    count = lax.axis_size(axis)
    return lax.ppermute(block, axis, [(i, count - 1 - i) for i in range(count)])


def shifted(block, axis):
    count = lax.axis_size(axis)
    return lax.ppermute(block, axis, [(i, (i + 1) % count) for i in range(count)])


def halves_of_sum(block, axis):
    count = lax.axis_size(axis)
    offset = 1
    while True:
        other = exchange(block, axis, offset)
        offset *= 2
        if offset >= count:
            return block, other
        block = block + other


ROOM = pltpu.CompilerParams(vmem_limit_bytes=16 << 20)


def cost(flops, nbytes):
    return pl.CostEstimate(flops=flops, bytes_accessed=nbytes, transcendentals=0)


def folded_squares(rows):
    tokens, width = rows.shape
    total = jnp.zeros((tokens, LANES), F32)
    for at in range(0, width, LANES):
        part = rows[:, at : at + LANES]
        total = total + part * part
    return total


def latent_kernel(tiles, x1, a1, x2, c2, a2, b2, gain, out_ref, vx1, va1, vx2, vc2, va2, vb2, vgain, sems):
    tokens, width = vx1.shape
    latent = va1.shape[0]
    tile = width // tiles
    jobs = [[pltpu.make_async_copy(gain, vgain, sems.at[6 * tiles])]]
    for names in (((x1, vx1), (a1, va1)), ((x2, vx2), (a2, va2)), ((c2, vc2), (b2, vb2))):
        for at in range(tiles):
            cols = pl.ds(at * tile, tile)
            sem = 2 * (len(jobs) - 1)
            jobs.append(
                [pltpu.make_async_copy(s.at[:, cols], d.at[:, cols], sems.at[sem + k]) for k, (s, d) in enumerate(names)]
            )
    ahead = 4
    for job in jobs[:ahead]:
        for copy in job:
            copy.start()

    def arrive(at):
        for copy in jobs[at]:
            copy.wait()
        if at + ahead < len(jobs):
            for copy in jobs[at + ahead]:
                copy.start()

    arrive(0)
    gains = vgain[...].astype(F32)

    def product(job, left, right):
        total = None
        squares = jnp.zeros((tokens, LANES), F32)
        for at in range(tiles):
            arrive(1 + job * tiles + at)
            cols = slice(at * tile, (at + 1) * tile)
            one, two = left(cols), right(cols)
            if job < 2:
                rows = (vx1, vx2)[job][:, cols].astype(F32)
                squares += folded_squares(rows)
                scaled = (rows * gains[job : job + 1, cols]).astype(BF16)
                one = scaled if one is None else one
                two = scaled if two is None else two
            term = lax.dot_general(one, two, BOTH_LAST, preferred_element_type=F32)
            total = term if total is None else total + term
        return total, squares

    raw, squares = product(0, lambda c: None, lambda c: va1[:, c])
    base = 2 * latent + tokens
    for at in range(latent // LANES):
        out_ref[base + at * tokens : base + (at + 1) * tokens] = raw[:, at * LANES : (at + 1) * LANES]
    out_ref[base + (latent // LANES) * tokens :] = squares
    raw, squares = product(1, lambda c: va2[:, c], lambda c: None)
    out_ref[:latent] = raw
    out_ref[2 * latent : base] = squares
    out_ref[latent : 2 * latent], _ = product(2, lambda c: vb2[:, c], lambda c: vc2[:, c])


def leaving_kernel(start, own_ref, other_ref, x_ref, b_ref, *rest):
    out_ref = rest[-1]
    latent = b_ref.shape[0]
    count = out_ref.shape[0]
    tokens = x_ref.shape[0]

    def summed(at):
        rows = slice(at + start, at + start + count)
        return own_ref[rows] + other_ref[rows]

    base = own_ref.shape[0] - tokens
    rscale = lax.rsqrt(jnp.sum(summed(base), axis=1, keepdims=True) / D + 1e-06)
    base -= (latent // LANES) * tokens
    hidden = jnp.concatenate([summed(base + at * tokens) * rscale for at in range(latent // LANES)], axis=1).astype(BF16)
    last = lax.axis_index("pipe") == lax.axis_size("pipe") - 1
    width = out_ref.shape[1]
    step = width // (4 if width % 512 == 0 else 2)
    for at in range(0, width, step):
        cols = slice(at, at + step)
        rows = x_ref[start : start + count, cols].astype(F32)
        rows += jnp.dot(hidden, b_ref[:, cols], preferred_element_type=F32)
        out_ref[:, cols] = jnp.where(last, 0.0, rows).astype(BF16)


def grad_kernel(experts, own_ref, other_ref, x_ref, g_ref, c_ref, *rest):
    outs, rows_ref = rest[-1 - experts : -1], rest[-1]
    latent = rows_ref.shape[1]
    depth = latent // experts
    me = lax.axis_index("expert")
    squares = own_ref[2 * latent : 2 * latent + LANES] + other_ref[2 * latent : 2 * latent + LANES]
    rscale = lax.rsqrt(jnp.sum(squares.T, axis=0, keepdims=True) / D + 1e-06)
    rows_ref[0] = (own_ref[latent : 2 * latent] + other_ref[latent : 2 * latent]) * rscale
    rows_ref[1] = (own_ref[:latent] + other_ref[:latent]) * rscale
    scaled = (x_ref[...].astype(F32) * g_ref[1:2].astype(F32)).astype(BF16)
    for side, right in enumerate((scaled, c_ref[...])):
        left = jnp.concatenate(
            [rows_ref[side, pl.ds(pl.multiple_of((me ^ k) * depth, depth), depth), :] for k in range(experts)]
        )
        both = jnp.dot(left.astype(BF16), right, preferred_element_type=F32).astype(BF16)
        for k in range(experts):
            outs[k][side] = both[k * depth : (k + 1) * depth]


def share_kernel(experts, *refs):
    total = refs[0][...].astype(F32)
    for ref in refs[1:experts]:
        total = total + ref[...].astype(F32)
    refs[-1][...] = total.astype(BF16)


def update_kernel(share_ref, master_ref, moment_ref, second_ref, *rest):
    fresh_ref, peak_ref = rest[-2:]
    grad = share_ref[...].astype(F32)
    first = 0.9 * moment_ref[...].astype(F32) + 0.1 * grad
    secnd = 0.95 * second_ref[...].astype(F32) + 0.05 * grad * grad
    update = first / (1.0 - 0.9**10) / (jnp.sqrt(secnd / (1.0 - 0.95**10)) + 1e-08)
    weights = master_ref[...]
    fresh = weights - 0.01 * (update + 0.1 * weights)
    fresh_ref[...] = fresh
    peak = jnp.max(jnp.abs(fresh), axis=1, keepdims=True)
    for block in range(peak.shape[-1] // LANES):
        peak_ref[:, block : block + 1] = peak[:, :, block * LANES : (block + 1) * LANES]


def code_kernel(group, fresh_ref, *rest):
    peak_refs, code_ref, scale_ref, wide = rest[:-3], rest[-3], rest[-2], rest[-1]
    chunks, _, per, _ = peak_refs[0].shape
    mine = lax.axis_index("expert") // group
    wide[...] = jnp.zeros_like(wide)
    for far, top in enumerate(peak_refs):
        for side in range(2):
            for chunk in range(chunks):
                wide[side, chunk * per : (chunk + 1) * per, :] = top[chunk, side]
        where = pl.ds(mine ^ far, 1)
        for side in range(2):
            scale_ref[side, where, :] = (
                jnp.max(wide[side].T, axis=0, keepdims=True)[:, : chunks * per] + 1e-06
            )
        if far == 0:
            for side in range(2):
                scale = jnp.broadcast_to(jnp.max(wide[side], axis=1, keepdims=True), wide.shape[1:]) + 1e-06
                inverse = 1.0 / scale
                for block in range(chunks * per):
                    at = slice(block * LANES, (block + 1) * LANES)
                    code_ref[side, :, at] = (fresh_ref[side, :, at] * inverse[block : block + 1]).astype(BF16)


def place_kernel(start, in_ref, *rest):
    out_ref, sem = rest[-2:]
    copy = pltpu.make_async_copy(in_ref, out_ref.at[0, pl.ds(start, in_ref.shape[0])], sem)
    copy.start()
    copy.wait()


ANY = pl.BlockSpec(memory_space=pl.ANY)


def whole(shape):
    return pl.BlockSpec(shape, lambda *_: (0,) * len(shape))


def shards(enter_fwd, enter_rev, cot_rev, gain, proj_down, proj_up, master, moment, second):
    tokens, width = enter_fwd.shape[1:]
    latent = proj_down.shape[2]
    experts = lax.axis_size("expert")
    depth = latent // experts
    blocks = width // LANES
    tiles = 4 if blocks % 4 == 0 else 2
    tile = width // tiles
    chunks = tiles
    part = width // chunks
    gains = gain.reshape(2, width)

    def streamed(array):
        return pltpu.with_memory_space_constraint(array, pltpu.HBM)

    pack_rows = 2 * latent + tokens + (latent // LANES + 1) * tokens
    packed = pl.pallas_call(
        lambda x1, x2, c2, down, up, *refs: latent_kernel(
            tiles, x1.at[0], down.at[0, 0], x2.at[0], c2.at[0], down.at[1, 0], up.at[1, 0], *refs
        ),
        in_specs=[ANY] * 6,
        out_specs=pl.BlockSpec(memory_space=pltpu.VMEM),
        out_shape=jax.ShapeDtypeStruct((pack_rows, LANES), F32),
        scratch_shapes=[
            pltpu.VMEM((tokens, width), BF16),
            pltpu.VMEM((latent, width), BF16),
            pltpu.VMEM((tokens, width), BF16),
            pltpu.VMEM((tokens, width), BF16),
            pltpu.VMEM((latent, width), BF16),
            pltpu.VMEM((latent, width), BF16),
            pltpu.VMEM((2, width), BF16),
            pltpu.SemaphoreType.DMA((6 * tiles + 1,)),
        ],
        compiler_params=ROOM,
        cost_estimate=cost(6 * tokens * latent * width, 6 * (tokens + latent) * width),
        name="latents",
    )(streamed(enter_fwd), streamed(enter_rev), streamed(cot_rev), streamed(proj_down), streamed(proj_up), streamed(gains))
    pair = halves_of_sum(packed, "dp")

    def leaving(start, count, *after):
        return pl.pallas_call(
            lambda *refs: leaving_kernel(start, *refs),
            grid=(1,),
            in_specs=[
                whole((pack_rows, LANES)),
                whole((pack_rows, LANES)),
                pl.BlockSpec((None, tokens, width), lambda i: (0, 0, 0)),
                pl.BlockSpec((None, None, latent, width), lambda i: (0, 0, 0, 0)),
            ]
            + [ANY] * len(after),
            out_specs=whole((count, width)),
            out_shape=jax.ShapeDtypeStruct((count, width), BF16),
            compiler_params=ROOM,
            cost_estimate=cost(2 * count * latent * width, 2 * (2 * count + latent) * width),
            name="leaving",
        )(*pair, enter_fwd, proj_up, *after)

    head = tokens * 5 // 8
    first_rows = leaving(0, head)
    left_head = shifted(first_rows, "pipe")

    def grads(chunk, *after):
        def columns():
            return pl.BlockSpec((None, tokens, part), lambda i: (0, 0, chunk))

        return pl.pallas_call(
            lambda *refs: grad_kernel(experts, *refs),
            grid=(1,),
            in_specs=[
                whole((pack_rows, LANES)),
                whole((pack_rows, LANES)),
                columns(),
                pl.BlockSpec((2, part), lambda i: (0, chunk)),
                columns(),
            ]
            + [ANY] * len(after),
            out_specs=[whole((2, depth, part))] * experts,
            out_shape=[jax.ShapeDtypeStruct((2, depth, part), BF16)] * experts,
            scratch_shapes=[pltpu.VMEM((2, latent, tokens), F32)],
            compiler_params=ROOM,
            cost_estimate=cost(4 * tokens * latent * part, 4 * (tokens + latent) * part),
            name="grads",
        )(*pair, enter_rev, gains, cot_rev, *after)

    def summed(own, others, *after):
        return pl.pallas_call(
            lambda *refs: share_kernel(experts, *refs),
            grid=(1,),
            in_specs=[whole((2, depth, part))] * experts + [ANY] * len(after),
            out_specs=whole((2, depth, part)),
            out_shape=jax.ShapeDtypeStruct((2, depth, part), BF16),
            compiler_params=ROOM,
            cost_estimate=cost(0, 4 * depth * part * (experts + 1)),
            name="share",
        )(own, *others, *after)

    shares, arrived, others = [], [], []
    for chunk in range(chunks):
        after = [first_rows, *shares[-2:-1], *([own] if chunk == 1 else [])]
        own, *pieces = grads(chunk, *after)
        others.append([exchange(piece, "expert", 1 + k) for k, piece in enumerate(pieces)])
        after = [left_head] if chunk == 1 else arrived[chunk - 2 : chunk - 1] if chunk else []
        shares.append(summed(own, others[-1], *after))
        arrived.append(mirrored(shares[-1], "pipe"))
    left_tail = shifted(leaving(head, tokens - head, shares[-1]), "pipe")

    def place(start, rows, *kept):
        return pl.pallas_call(
            lambda *refs: place_kernel(start, *refs),
            in_specs=[ANY] * (1 + len(kept)),
            out_specs=ANY,
            out_shape=jax.ShapeDtypeStruct((1, tokens, width), BF16),
            scratch_shapes=[pltpu.SemaphoreType.DMA],
            input_output_aliases={1 + k: k for k in range(len(kept))},
            compiler_params=ROOM,
            cost_estimate=cost(0, 4 * rows.shape[0] * width),
            name="place",
        )(rows, *kept)

    placed = place(0, left_head)

    fresh = peaks = None
    for chunk in range(chunks):
        state = pl.BlockSpec((2, None, depth, part), lambda i, c=chunk: (0, 0, 0, c))
        kept = () if fresh is None else (fresh, peaks)
        after = (placed,) if chunk == 2 else ()
        fresh, peaks = pl.pallas_call(
            update_kernel,
            grid=(1,),
            in_specs=[whole((2, depth, part)), state, state, state] + [ANY] * (len(kept) + len(after)),
            out_specs=[
                pl.BlockSpec((2, depth, part), lambda i, c=chunk: (0, 0, c)),
                pl.BlockSpec((None, 2, part // LANES, LANES), lambda i, c=chunk: (c, 0, 0, 0)),
            ],
            out_shape=[
                jax.ShapeDtypeStruct((2, depth, width), F32),
                jax.ShapeDtypeStruct((chunks, 2, part // LANES, LANES), F32),
            ],
            input_output_aliases={4 + k: k for k in range(len(kept))},
            compiler_params=ROOM,
            cost_estimate=cost(20 * 2 * depth * part, 14 * 2 * depth * part),
            name="update",
        )(arrived[chunk], master, moment, second, *kept, *after)

    group = LANES // depth
    for level in range(group.bit_length() - 1):
        peaks = jnp.maximum(peaks, exchange(peaks, "expert", 1 << level))
    peak_rows = [peaks] + [exchange(peaks, "expert", k * group) for k in range(1, experts // group)]
    coded, scales = pl.pallas_call(
        lambda *refs: code_kernel(group, *refs),
        grid=(1,),
        in_specs=[whole((2, depth, width))] + [whole(peaks.shape)] * len(peak_rows),
        out_specs=[
            pl.BlockSpec((2, None, depth, width), lambda i: (0, 0, 0, 0)),
            pl.BlockSpec((2, None, experts // group, blocks), lambda i: (0, 0, 0, 0)),
        ],
        out_shape=[
            jax.ShapeDtypeStruct((2, 1, depth, width), BF16),
            jax.ShapeDtypeStruct((2, 1, experts // group, blocks), F32),
        ],
        scratch_shapes=[pltpu.VMEM((2, LANES, LANES), F32)],
        compiler_params=ROOM,
        cost_estimate=cost(2 * 2 * depth * width, 6 * 2 * depth * width),
        name="codes",
    )(fresh, *peak_rows)

    return (place(head, left_tail, placed), coded, scales)


def solution(mesh):
    in_specs = (
        P("pipe", "expert", "dp"),
        P("pipe", "expert", "dp"),
        P("pipe", "expert", "dp"),
        P(None, "pipe", "dp"),
        P(None, "pipe", None, "dp"),
        P(None, "pipe", None, "dp"),
        P(None, "pipe", "expert", "dp"),
        P(None, "pipe", "expert", "dp"),
        P(None, "pipe", "expert", "dp"),
    )
    out_specs = (
        P("pipe", "expert", "dp"),
        P(None, "pipe", "expert", "dp"),
        P(None, "pipe", None, "dp"),
    )
    return jax.shard_map(shards, mesh=mesh, in_specs=in_specs, out_specs=out_specs, check_vma=False)
```

```python
import jax
import jax.numpy as jnp
from jax import lax
from jax.experimental import pallas as pl
from jax.experimental.pallas import tpu as pltpu
from jax.sharding import PartitionSpec as P

D = 7168
LANES = 128
F32 = jnp.float32
BF16 = jnp.bfloat16
BOTH_LAST = (((1,), (1,)), ((), ()))
ROOM = pltpu.CompilerParams(vmem_limit_bytes=16 << 20)
ANY = pl.BlockSpec(memory_space=pl.ANY)
VMEM = pl.BlockSpec(memory_space=pltpu.VMEM)


def exchange(block, axis, offset):
    count = lax.axis_size(axis)
    return lax.ppermute(block, axis, [(i, i ^ offset) for i in range(count)])


def mirrored(block, axis):
    count = lax.axis_size(axis)
    return lax.ppermute(block, axis, [(i, count - 1 - i) for i in range(count)])


def turned(block, axis):
    count = lax.axis_size(axis)
    return lax.ppermute(block, axis, [(i, (i + 1) % count) for i in range(count)])


def halves_of_sum(block, axis):
    count = lax.axis_size(axis)
    offset = 1
    while True:
        other = exchange(block, axis, offset)
        offset *= 2
        if offset >= count:
            return block, other
        block = block + other


def shape(dims, dtype):
    return jax.ShapeDtypeStruct(dims, dtype)


def call(kernel, name, outs, *operands, read, scratch=(), flops=0):
    many = isinstance(outs, list)
    nbytes = sum(o.size * o.dtype.itemsize for o in operands[:read])
    return pl.pallas_call(
        kernel,
        in_specs=[VMEM] * read + [ANY] * (len(operands) - read),
        out_specs=[VMEM] * len(outs) if many else VMEM,
        out_shape=outs,
        scratch_shapes=list(scratch),
        compiler_params=ROOM,
        cost_estimate=pl.CostEstimate(flops=flops, bytes_accessed=nbytes, transcendentals=0),
        name=name,
    )(*operands)


def folded_squares(rows):
    tokens, width = rows.shape
    total = jnp.zeros((tokens, LANES), F32)
    for at in range(0, width, LANES):
        part = rows[:, at : at + LANES]
        total = total + part * part
    return total


def latent_kernel(tiles, x1, x2, c2, down, up, gain, out_ref, vx1, scaled2, vc2, va1, vx2, va2, vb2, vgain, sems):
    tokens, width = vx1.shape
    latent = va1.shape[0]
    tile = width // tiles
    pairs = (
        ((x1.at[0], vx1), (down.at[0, 0], va1)),
        ((x2.at[0], vx2), (down.at[1, 0], va2)),
        ((c2.at[0], vc2), (up.at[1, 0], vb2)),
    )
    jobs = [[pltpu.make_async_copy(gain, vgain, sems.at[6 * tiles])]]
    for pair in pairs:
        for at in range(tiles):
            cols = pl.ds(at * tile, tile)
            sem = 2 * (len(jobs) - 1)
            jobs.append(
                [pltpu.make_async_copy(s.at[:, cols], d.at[:, cols], sems.at[sem + k]) for k, (s, d) in enumerate(pair)]
            )
    for job in jobs:
        for copy in job:
            copy.start()

    def arrive(at):
        for copy in jobs[at]:
            copy.wait()

    arrive(0)
    gains = vgain[...].astype(F32)

    def product(job):
        total = None
        squares = jnp.zeros((tokens, LANES), F32)
        for at in range(tiles):
            arrive(1 + job * tiles + at)
            cols = slice(at * tile, (at + 1) * tile)
            if job < 2:
                rows = (vx1, vx2)[job][:, cols].astype(F32)
                squares += folded_squares(rows)
                right = (rows * gains[job : job + 1, cols]).astype(BF16)
            if job == 0:
                left, right = right, va1[:, cols]
            elif job == 1:
                scaled2[:, cols] = right
                left = va2[:, cols]
            else:
                left, right = vb2[:, cols], vc2[:, cols]
            term = lax.dot_general(left, right, BOTH_LAST, preferred_element_type=F32)
            total = term if total is None else total + term
        return total, squares

    raw, squares = product(0)
    base = 2 * latent + tokens
    for at in range(latent // LANES):
        out_ref[base + at * tokens : base + (at + 1) * tokens] = raw[:, at * LANES : (at + 1) * LANES]
    out_ref[base + (latent // LANES) * tokens :] = squares
    raw, squares = product(1)
    out_ref[:latent] = raw
    out_ref[2 * latent : base] = squares
    out_ref[latent : 2 * latent], _ = product(2)


def fetch_kernel(in_ref, *rest):
    out_ref, sem = rest[-2:]
    copy = pltpu.make_async_copy(in_ref.at[0, 0], out_ref, sem)
    copy.start()
    copy.wait()


def leaving_kernel(start, own_ref, other_ref, x_ref, b_ref, *rest):
    out_ref = rest[-1]
    latent = b_ref.shape[0]
    count, width = out_ref.shape
    tokens = x_ref.shape[0]

    def summed(at):
        rows = slice(at + start, at + start + count)
        return own_ref[rows] + other_ref[rows]

    base = own_ref.shape[0] - tokens
    rscale = lax.rsqrt(jnp.sum(summed(base), axis=1, keepdims=True) / D + 1e-06)
    base -= (latent // LANES) * tokens
    hidden = jnp.concatenate([summed(base + at * tokens) * rscale for at in range(latent // LANES)], axis=1).astype(BF16)
    last = lax.axis_index("pipe") == lax.axis_size("pipe") - 1
    step = width // (4 if width % (4 * LANES) == 0 else 2)
    for at in range(0, width, step):
        cols = slice(at, at + step)
        rows = x_ref[start : start + count, cols].astype(F32)
        rows += jnp.dot(hidden, b_ref[:, cols], preferred_element_type=F32)
        out_ref[:, cols] = jnp.where(last, 0.0, rows).astype(BF16)


def grad_kernel(experts, start, own_ref, other_ref, x_ref, c_ref, *rest):
    outs, rows_ref = rest[-1 - experts : -1], rest[-1]
    latent = rows_ref.shape[1]
    depth = latent // experts
    cols = slice(start, start + outs[0].shape[2])
    me = lax.axis_index("expert")
    squares = own_ref[2 * latent : 2 * latent + LANES] + other_ref[2 * latent : 2 * latent + LANES]
    rscale = lax.rsqrt(jnp.sum(squares.T, axis=0, keepdims=True) / D + 1e-06)
    rows_ref[0] = (own_ref[latent : 2 * latent] + other_ref[latent : 2 * latent]) * rscale
    rows_ref[1] = (own_ref[:latent] + other_ref[:latent]) * rscale
    for side, right in enumerate((x_ref[:, cols], c_ref[:, cols])):
        left = jnp.concatenate(
            [rows_ref[side, pl.ds(pl.multiple_of((me ^ k) * depth, depth), depth), :] for k in range(experts)]
        )
        both = jnp.dot(left.astype(BF16), right, preferred_element_type=F32).astype(BF16)
        for k in range(experts):
            outs[k][side] = both[k * depth : (k + 1) * depth]


def share_kernel(experts, *refs):
    total = refs[0][...].astype(F32)
    for ref in refs[1:experts]:
        total = total + ref[...].astype(F32)
    refs[-1][...] = total.astype(BF16)


def update_kernel(start, share_ref, master_ref, moment_ref, second_ref, *rest):
    fresh_ref, peak_ref, wide = rest[-3:]
    cols = slice(start, start + share_ref.shape[2])
    grad = share_ref[...].astype(F32)
    first = 0.9 * moment_ref[:, 0, :, cols].astype(F32) + 0.1 * grad
    secnd = 0.95 * second_ref[:, 0, :, cols].astype(F32) + 0.05 * grad * grad
    update = first / (1.0 - 0.9**10) / (jnp.sqrt(secnd / (1.0 - 0.95**10)) + 1e-08)
    weights = master_ref[:, 0, :, cols]
    fresh = weights - 0.01 * (update + 0.1 * weights)
    fresh_ref[...] = fresh
    peak_ref[...] = jnp.zeros_like(peak_ref) if start == 0 else rest[0][...]
    wide[...] = jnp.zeros_like(wide)
    for side in range(2):
        peak = jnp.max(jnp.abs(fresh[side]), axis=0, keepdims=True)
        for at in range(0, peak.shape[1], LANES):
            block = (start + at) // LANES
            wide[side, block : block + 1, :] = peak[:, at : at + LANES]
        peak_ref[side : side + 1, :] = jnp.maximum(
            peak_ref[side : side + 1, :], jnp.max(wide[side].T, axis=0, keepdims=True)
        )


def code_kernel(group, peak_refs, fresh_refs, code_ref, scale_ref):
    blocks = scale_ref.shape[3]
    mine = lax.axis_index("expert") // group
    for far, ref in enumerate(peak_refs):
        for side in range(2):
            scale_ref[side, 0, pl.ds(mine ^ far, 1), :] = ref[side : side + 1, :blocks] + 1e-06
    column = (1.0 / (peak_refs[0][...] + 1e-06)).T
    for side in range(2):
        inverse = jnp.broadcast_to(column[:, side : side + 1], (LANES, LANES))
        block = 0
        for ref in fresh_refs:
            for at in range(0, ref.shape[2], LANES):
                code_ref[side, 0, :, block * LANES : (block + 1) * LANES] = (
                    ref[side, :, at : at + LANES] * inverse[block : block + 1]
                ).astype(BF16)
                block += 1


def place_kernel(start, in_ref, *rest):
    out_ref, sem = rest[-2:]
    copy = pltpu.make_async_copy(in_ref, out_ref.at[0, pl.ds(start, in_ref.shape[0])], sem)
    copy.start()
    copy.wait()


def shards(enter_fwd, enter_rev, cot_rev, gain, proj_down, proj_up, master, moment, second):
    tokens, width = enter_fwd.shape[1:]
    latent = proj_down.shape[2]
    experts = lax.axis_size("expert")
    depth = latent // experts
    blocks = width // LANES
    tiles = 2
    weights = [8, 8, 7, 5]
    edges = [blocks * sum(weights[:k]) // sum(weights) * LANES for k in range(len(weights) + 1)]
    chunks = list(zip(edges[:-1], edges[1:]))

    def streamed(array):
        return pltpu.with_memory_space_constraint(array, pltpu.HBM)

    pack_rows = 2 * latent + tokens + (latent // LANES + 1) * tokens
    held = pltpu.VMEM((tokens, width), BF16)
    packed, rows1, scaled2, cot2 = pl.pallas_call(
        lambda *refs: latent_kernel(tiles, *refs),
        in_specs=[ANY] * 6,
        out_specs=[VMEM] * 4,
        out_shape=[pltpu.VMEM((pack_rows, LANES), F32), held, held, held],
        scratch_shapes=[
            pltpu.VMEM((latent, width), BF16),
            pltpu.VMEM((tokens, width), BF16),
            pltpu.VMEM((latent, width), BF16),
            pltpu.VMEM((latent, width), BF16),
            pltpu.VMEM((2, width), BF16),
            pltpu.SemaphoreType.DMA((6 * tiles + 1,)),
        ],
        compiler_params=ROOM,
        cost_estimate=pl.CostEstimate(
            flops=6 * tokens * latent * width, bytes_accessed=6 * (tokens + latent) * width, transcendentals=0
        ),
        name="latents",
    )(*(streamed(a) for a in (enter_fwd, enter_rev, cot_rev, proj_down, proj_up, gain.reshape(2, width))))
    own_up = pl.pallas_call(
        fetch_kernel,
        in_specs=[ANY] * 2,
        out_specs=VMEM,
        out_shape=pltpu.VMEM((latent, width), BF16),
        scratch_shapes=[pltpu.SemaphoreType.DMA],
        compiler_params=ROOM,
        cost_estimate=pl.CostEstimate(flops=0, bytes_accessed=2 * latent * width, transcendentals=0),
        name="fetch",
    )(streamed(proj_up), packed)
    pair = halves_of_sum(packed, "dp")

    def leaving(start, count, *after):
        return call(
            lambda *refs: leaving_kernel(start, *refs),
            "leaving",
            shape((count, width), BF16),
            *pair,
            rows1,
            own_up,
            *after,
            read=4,
            flops=2 * count * latent * width,
        )

    def grads(chunk, *after):
        start, stop = chunks[chunk]
        return call(
            lambda *refs: grad_kernel(experts, start, *refs),
            "grads",
            [shape((2, depth, stop - start), BF16)] * experts,
            *pair,
            scaled2,
            cot2,
            *after,
            read=4,
            scratch=[pltpu.VMEM((2, latent, tokens), F32)],
            flops=4 * tokens * latent * (stop - start),
        )

    head = 128
    first_rows = leaving(0, head)
    left_head = turned(first_rows, "pipe")
    first = grads(0, first_rows)
    shares, arrived, others = [], [], []
    for chunk in range(len(chunks)):
        own, *pieces = grads(chunk, *shares[-2:-1], *others[-1][:1]) if chunk else first
        others.append([exchange(piece, "expert", 1 + k) for k, piece in enumerate(pieces)])
        after = [left_head] if chunk == 1 else arrived[chunk - 2 : chunk - 1] if chunk > 1 else []
        shares.append(
            call(
                lambda *refs: share_kernel(experts, *refs),
                "share",
                shape(own.shape, BF16),
                own,
                *others[-1],
                *shares[-1:],
                *after,
                read=experts,
            )
        )
        arrived.append(mirrored(shares[-1], "pipe"))
    left_tail = None

    def place(start, rows, *kept):
        return pl.pallas_call(
            lambda *refs: place_kernel(start, *refs),
            in_specs=[ANY] * (1 + len(kept)),
            out_specs=ANY,
            out_shape=shape((1, tokens, width), BF16),
            scratch_shapes=[pltpu.SemaphoreType.DMA],
            input_output_aliases={1 + k: k for k in range(len(kept))},
            compiler_params=ROOM,
            cost_estimate=pl.CostEstimate(flops=0, bytes_accessed=4 * rows.shape[0] * width, transcendentals=0),
            name="place",
        )(rows, *kept)

    placed = place(0, left_head)

    fresh, peaks = [], None
    for chunk, (start, stop) in enumerate(chunks):
        kept = () if peaks is None else (peaks,)
        after = (placed,) if chunk == len(chunks) - 1 else ()
        some, peaks = call(
            lambda *refs: update_kernel(start, *refs),
            "update",
            [shape((2, depth, stop - start), F32), shape((8, LANES), F32)],
            arrived[chunk],
            master,
            moment,
            second,
            *kept,
            *after,
            read=4 + len(kept),
            scratch=[pltpu.VMEM((2, LANES, LANES), F32)],
            flops=40 * depth * (stop - start),
        )
        fresh.append(some)

    group = LANES // depth
    for level in range(group.bit_length() - 1):
        peaks = jnp.maximum(peaks, exchange(peaks, "expert", 1 << level))
    peak_rows = [peaks] + [exchange(peaks, "expert", k * group) for k in range(1, experts // group)]
    count = len(peak_rows)
    coded, scales = call(
        lambda *refs: code_kernel(group, refs[:count], refs[count:-2], *refs[-2:]),
        "codes",
        [shape((2, 1, depth, width), BF16), shape((2, 1, experts // group, blocks), F32)],
        *peak_rows,
        *fresh,
        read=count + len(fresh),
        flops=4 * depth * width,
    )
    return (placed, coded, scales)


def solution(mesh):
    in_specs = (
        P("pipe", "expert", "dp"),
        P("pipe", "expert", "dp"),
        P("pipe", "expert", "dp"),
        P(None, "pipe", "dp"),
        P(None, "pipe", None, "dp"),
        P(None, "pipe", None, "dp"),
        P(None, "pipe", "expert", "dp"),
        P(None, "pipe", "expert", "dp"),
        P(None, "pipe", "expert", "dp"),
    )
    out_specs = (
        P("pipe", "expert", "dp"),
        P(None, "pipe", "expert", "dp"),
        P(None, "pipe", None, "dp"),
    )
    return jax.shard_map(shards, mesh=mesh, in_specs=in_specs, out_specs=out_specs, check_vma=False)
```

```python
import jax
import jax.numpy as jnp
from jax import lax
from jax.experimental import pallas as pl
from jax.experimental.pallas import tpu as pltpu
from jax.sharding import PartitionSpec as P

D = 7168
LANES = 128
F32 = jnp.float32
BF16 = jnp.bfloat16
BOTH_LAST = (((1,), (1,)), ((), ()))
ROOM = pltpu.CompilerParams(vmem_limit_bytes=16 << 20)
ANY = pl.BlockSpec(memory_space=pl.ANY)
VMEM = pl.BlockSpec(memory_space=pltpu.VMEM)


def exchange(block, axis, offset):
    count = lax.axis_size(axis)
    return lax.ppermute(block, axis, [(i, i ^ offset) for i in range(count)])


def mirrored(block, axis):
    count = lax.axis_size(axis)
    return lax.ppermute(block, axis, [(i, count - 1 - i) for i in range(count)])


def turned(block, axis):
    count = lax.axis_size(axis)
    return lax.ppermute(block, axis, [(i, (i + 1) % count) for i in range(count)])


def halves_of_sum(block, axis):
    count = lax.axis_size(axis)
    offset = 1
    while True:
        other = exchange(block, axis, offset)
        offset *= 2
        if offset >= count:
            return block, other
        block = block + other


def shape(dims, dtype):
    return jax.ShapeDtypeStruct(dims, dtype)


def call(kernel, name, outs, *operands, read, scratch=(), flops=0):
    many = isinstance(outs, list)
    nbytes = sum(o.size * o.dtype.itemsize for o in operands[:read])
    return pl.pallas_call(
        kernel,
        in_specs=[VMEM] * read + [ANY] * (len(operands) - read),
        out_specs=[VMEM] * len(outs) if many else VMEM,
        out_shape=outs,
        scratch_shapes=list(scratch),
        compiler_params=ROOM,
        cost_estimate=pl.CostEstimate(flops=flops, bytes_accessed=nbytes, transcendentals=0),
        name=name,
    )(*operands)


def folded_squares(rows):
    tokens, width = rows.shape
    total = jnp.zeros((tokens, LANES), F32)
    for at in range(0, width, LANES):
        part = rows[:, at : at + LANES]
        total = total + part * part
    return total


def latent_kernel(tiles, x1, x2, c2, down, up, gain, out_ref, vx1, scaled2, vc2, va1, vx2, va2, vb2, vgain, sems):
    tokens, width = vx1.shape
    latent = va1.shape[0]
    tile = width // tiles
    groups = (
        ((x1.at[0], vx1), (down.at[0, 0], va1)),
        ((x2.at[0], vx2), (down.at[1, 0], va2)),
        ((c2.at[0], vc2), (up.at[1, 0], vb2)),
    )

    def copies(job, at):
        cols = pl.ds(at * tile, tile)
        return [
            pltpu.make_async_copy(src.at[:, cols], dst.at[:, cols], sems.at[job, k, at])
            for k, (src, dst) in enumerate(groups[job])
        ]

    whole_gain = pltpu.make_async_copy(gain, vgain, sems.at[len(groups), 0, 0])
    whole_gain.start()
    for job in range(len(groups)):
        for at in range(tiles):
            for copy in copies(job, at):
                copy.start()
    base = 2 * latent + tokens
    out_ref[...] = jnp.zeros_like(out_ref)
    whole_gain.wait()

    def step(job, at):
        for copy in copies(job, at):
            copy.wait()
        cols = pl.ds(pl.multiple_of(at * tile, LANES), tile)
        if job < 2:
            rows = (vx1, vx2)[job][:, cols].astype(F32)
            right = (rows * vgain[job : job + 1, cols].astype(F32)).astype(BF16)
            squares = folded_squares(rows)
        if job == 0:
            raw = lax.dot_general(right, va1[:, cols], BOTH_LAST, preferred_element_type=F32)
            for piece in range(latent // LANES):
                out_ref[base + piece * tokens : base + (piece + 1) * tokens] += raw[:, piece * LANES : (piece + 1) * LANES]
            out_ref[base + (latent // LANES) * tokens :] += squares
        elif job == 1:
            scaled2[:, cols] = right
            out_ref[:latent] += lax.dot_general(va2[:, cols], right, BOTH_LAST, preferred_element_type=F32)
            out_ref[2 * latent : base] += squares
        else:
            out_ref[latent : 2 * latent] += lax.dot_general(
                vb2[:, cols], vc2[:, cols], BOTH_LAST, preferred_element_type=F32
            )

    for job in range(len(groups)):
        lax.fori_loop(0, tiles, lambda at, _, job=job: step(job, at) or 0, 0)


def fetch_kernel(in_ref, *rest):
    out_ref, sem = rest[-2:]
    copy = pltpu.make_async_copy(in_ref.at[0, 0], out_ref, sem)
    copy.start()
    copy.wait()


def leaving_kernel(start, own_ref, other_ref, x_ref, b_ref, *rest):
    out_ref = rest[-1]
    latent = b_ref.shape[0]
    count, width = out_ref.shape
    tokens = x_ref.shape[0]

    def summed(at):
        rows = slice(at + start, at + start + count)
        return own_ref[rows] + other_ref[rows]

    base = own_ref.shape[0] - tokens
    rscale = lax.rsqrt(jnp.sum(summed(base), axis=1, keepdims=True) / D + 1e-06)
    base -= (latent // LANES) * tokens
    hidden = jnp.concatenate([summed(base + at * tokens) * rscale for at in range(latent // LANES)], axis=1).astype(BF16)
    last = lax.axis_index("pipe") == lax.axis_size("pipe") - 1
    step = width // (4 if width % (4 * LANES) == 0 else 2)
    for at in range(0, width, step):
        cols = slice(at, at + step)
        rows = x_ref[start : start + count, cols].astype(F32)
        rows += jnp.dot(hidden, b_ref[:, cols], preferred_element_type=F32)
        out_ref[:, cols] = jnp.where(last, 0.0, rows).astype(BF16)


def grad_kernel(experts, start, own_ref, other_ref, x_ref, c_ref, *rest):
    outs, rows_ref = rest[-1 - experts : -1], rest[-1]
    latent = rows_ref.shape[1]
    depth = latent // experts
    cols = slice(start, start + outs[0].shape[2])
    me = lax.axis_index("expert")
    squares = own_ref[2 * latent : 2 * latent + LANES] + other_ref[2 * latent : 2 * latent + LANES]
    rscale = lax.rsqrt(jnp.sum(squares.T, axis=0, keepdims=True) / D + 1e-06)
    rows_ref[0] = (own_ref[latent : 2 * latent] + other_ref[latent : 2 * latent]) * rscale
    rows_ref[1] = (own_ref[:latent] + other_ref[:latent]) * rscale
    for side, right in enumerate((x_ref[:, cols], c_ref[:, cols])):
        left = jnp.concatenate(
            [rows_ref[side, pl.ds(pl.multiple_of((me ^ k) * depth, depth), depth), :] for k in range(experts)]
        )
        both = jnp.dot(left.astype(BF16), right, preferred_element_type=F32).astype(BF16)
        for k in range(experts):
            outs[k][side] = both[k * depth : (k + 1) * depth]


def share_kernel(experts, *refs):
    total = refs[0][...].astype(F32)
    for ref in refs[1:experts]:
        total = total + ref[...].astype(F32)
    refs[-1][...] = total.astype(BF16)


def update_kernel(start, share_ref, master_ref, moment_ref, second_ref, *rest):
    fresh_ref, peak_ref, wide = rest[-3:]
    cols = slice(start, start + share_ref.shape[2])
    grad = share_ref[...].astype(F32)
    first = 0.9 * moment_ref[:, 0, :, cols].astype(F32) + 0.1 * grad
    secnd = 0.95 * second_ref[:, 0, :, cols].astype(F32) + 0.05 * grad * grad
    update = first / (1.0 - 0.9**10) / (jnp.sqrt(secnd / (1.0 - 0.95**10)) + 1e-08)
    weights = master_ref[:, 0, :, cols]
    fresh = weights - 0.01 * (update + 0.1 * weights)
    fresh_ref[...] = fresh
    peak_ref[...] = jnp.zeros_like(peak_ref) if start == 0 else rest[0][...]
    wide[...] = jnp.zeros_like(wide)
    for side in range(2):
        peak = jnp.max(jnp.abs(fresh[side]), axis=0, keepdims=True)
        for at in range(0, peak.shape[1], LANES):
            block = (start + at) // LANES
            wide[side, block : block + 1, :] = peak[:, at : at + LANES]
        peak_ref[side : side + 1, :] = jnp.maximum(
            peak_ref[side : side + 1, :], jnp.max(wide[side].T, axis=0, keepdims=True)
        )


def code_kernel(group, peak_refs, fresh_refs, code_ref, scale_ref):
    blocks = scale_ref.shape[3]
    mine = lax.axis_index("expert") // group
    tops = []
    for far in range(len(peak_refs) // group):
        top = peak_refs[far * group][...]
        for ref in peak_refs[far * group + 1 : (far + 1) * group]:
            top = jnp.maximum(top, ref[...])
        tops.append(top + 1e-06)
        for side in range(2):
            scale_ref[side, 0, pl.ds(mine ^ far, 1), :] = tops[far][side : side + 1, :blocks]
    column = (1.0 / tops[0]).T
    for side in range(2):
        inverse = jnp.broadcast_to(column[:, side : side + 1], (LANES, LANES))
        block = 0
        for ref in fresh_refs:
            for at in range(0, ref.shape[2], LANES):
                code_ref[side, 0, :, block * LANES : (block + 1) * LANES] = (
                    ref[side, :, at : at + LANES] * inverse[block : block + 1]
                ).astype(BF16)
                block += 1


def place_kernel(start, in_ref, *rest):
    out_ref, sem = rest[-2:]
    copy = pltpu.make_async_copy(in_ref, out_ref.at[0, pl.ds(start, in_ref.shape[0])], sem)
    copy.start()
    copy.wait()


def shards(enter_fwd, enter_rev, cot_rev, gain, proj_down, proj_up, master, moment, second):
    tokens, width = enter_fwd.shape[1:]
    latent = proj_down.shape[2]
    experts = lax.axis_size("expert")
    depth = latent // experts
    blocks = width // LANES
    tiles = 2
    weights = [8, 8, 7, 5]
    edges = [blocks * sum(weights[:k]) // sum(weights) * LANES for k in range(len(weights) + 1)]
    chunks = list(zip(edges[:-1], edges[1:]))

    def streamed(array):
        return pltpu.with_memory_space_constraint(array, pltpu.HBM)

    pack_rows = 2 * latent + tokens + (latent // LANES + 1) * tokens
    held = pltpu.VMEM((tokens, width), BF16)
    packed, rows1, scaled2, cot2 = pl.pallas_call(
        lambda *refs: latent_kernel(tiles, *refs),
        in_specs=[ANY] * 6,
        out_specs=[VMEM] * 4,
        out_shape=[pltpu.VMEM((pack_rows, LANES), F32), held, held, held],
        scratch_shapes=[
            pltpu.VMEM((latent, width), BF16),
            pltpu.VMEM((tokens, width), BF16),
            pltpu.VMEM((latent, width), BF16),
            pltpu.VMEM((latent, width), BF16),
            pltpu.VMEM((2, width), BF16),
            pltpu.SemaphoreType.DMA((4, 2, tiles)),
        ],
        compiler_params=ROOM,
        cost_estimate=pl.CostEstimate(
            flops=6 * tokens * latent * width, bytes_accessed=6 * (tokens + latent) * width, transcendentals=0
        ),
        name="latents",
    )(*(streamed(a) for a in (enter_fwd, enter_rev, cot_rev, proj_down, proj_up, gain.reshape(2, width))))
    own_up = pl.pallas_call(
        fetch_kernel,
        in_specs=[ANY] * 2,
        out_specs=VMEM,
        out_shape=pltpu.VMEM((latent, width), BF16),
        scratch_shapes=[pltpu.SemaphoreType.DMA],
        compiler_params=ROOM,
        cost_estimate=pl.CostEstimate(flops=0, bytes_accessed=2 * latent * width, transcendentals=0),
        name="fetch",
    )(streamed(proj_up), packed)
    pair = halves_of_sum(packed, "dp")

    def leaving(start, count, *after):
        return call(
            lambda *refs: leaving_kernel(start, *refs),
            "leaving",
            shape((count, width), BF16),
            *pair,
            rows1,
            own_up,
            *after,
            read=4,
            flops=2 * count * latent * width,
        )

    def grads(chunk, *after):
        start, stop = chunks[chunk]
        return call(
            lambda *refs: grad_kernel(experts, start, *refs),
            "grads",
            [shape((2, depth, stop - start), BF16)] * experts,
            *pair,
            scaled2,
            cot2,
            *after,
            read=4,
            scratch=[pltpu.VMEM((2, latent, tokens), F32)],
            flops=4 * tokens * latent * (stop - start),
        )

    head = 128
    first_rows = leaving(0, head)
    left_head = turned(first_rows, "pipe")
    first = grads(0, first_rows)
    shares, arrived, others = [], [], []
    for chunk in range(len(chunks)):
        own, *pieces = grads(chunk, *shares[-2:-1], *others[-1][:1]) if chunk else first
        others.append([exchange(piece, "expert", 1 + k) for k, piece in enumerate(pieces)])
        after = [left_head] if chunk == 1 else arrived[chunk - 2 : chunk - 1] if chunk > 1 else []
        shares.append(
            call(
                lambda *refs: share_kernel(experts, *refs),
                "share",
                shape(own.shape, BF16),
                own,
                *others[-1],
                *shares[-1:],
                *after,
                read=experts,
            )
        )
        arrived.append(mirrored(shares[-1], "pipe"))
    left_tail = None

    def place(start, rows, *kept):
        return pl.pallas_call(
            lambda *refs: place_kernel(start, *refs),
            in_specs=[ANY] * (1 + len(kept)),
            out_specs=ANY,
            out_shape=shape((1, tokens, width), BF16),
            scratch_shapes=[pltpu.SemaphoreType.DMA],
            input_output_aliases={1 + k: k for k in range(len(kept))},
            compiler_params=ROOM,
            cost_estimate=pl.CostEstimate(flops=0, bytes_accessed=4 * rows.shape[0] * width, transcendentals=0),
            name="place",
        )(rows, *kept)

    placed = place(0, left_head)

    fresh, peaks = [], None
    for chunk, (start, stop) in enumerate(chunks):
        kept = () if peaks is None else (peaks,)
        after = (placed,) if chunk == len(chunks) - 1 else ()
        some, peaks = call(
            lambda *refs: update_kernel(start, *refs),
            "update",
            [shape((2, depth, stop - start), F32), shape((8, LANES), F32)],
            arrived[chunk],
            master,
            moment,
            second,
            *kept,
            *after,
            read=4 + len(kept),
            scratch=[pltpu.VMEM((2, LANES, LANES), F32)],
            flops=40 * depth * (stop - start),
        )
        fresh.append(some)

    group = LANES // depth
    peak_rows = [peaks] + [exchange(peaks, "expert", k) for k in range(1, experts)]
    count = len(peak_rows)
    coded, scales = call(
        lambda *refs: code_kernel(group, refs[:count], refs[count:-2], *refs[-2:]),
        "codes",
        [shape((2, 1, depth, width), BF16), shape((2, 1, experts // group, blocks), F32)],
        *peak_rows,
        *fresh,
        read=count + len(fresh),
        flops=4 * depth * width,
    )
    return (placed, coded, scales)


def solution(mesh):
    in_specs = (
        P("pipe", "expert", "dp"),
        P("pipe", "expert", "dp"),
        P("pipe", "expert", "dp"),
        P(None, "pipe", "dp"),
        P(None, "pipe", None, "dp"),
        P(None, "pipe", None, "dp"),
        P(None, "pipe", "expert", "dp"),
        P(None, "pipe", "expert", "dp"),
        P(None, "pipe", "expert", "dp"),
    )
    out_specs = (
        P("pipe", "expert", "dp"),
        P(None, "pipe", "expert", "dp"),
        P(None, "pipe", None, "dp"),
    )
    return jax.shard_map(shards, mesh=mesh, in_specs=in_specs, out_specs=out_specs, check_vma=False)
```

```python
import jax
import jax.numpy as jnp
from jax import lax
from jax.experimental import pallas as pl
from jax.experimental.pallas import tpu as pltpu
from jax.sharding import PartitionSpec as P

D = 7168
LANES = 128
F32 = jnp.float32
BF16 = jnp.bfloat16
BOTH_LAST = (((1,), (1,)), ((), ()))
ROOM = pltpu.CompilerParams(vmem_limit_bytes=16 << 20)
ANY = pl.BlockSpec(memory_space=pl.ANY)
VMEM = pl.BlockSpec(memory_space=pltpu.VMEM)


def exchange(block, axis, offset):
    count = lax.axis_size(axis)
    return lax.ppermute(block, axis, [(i, i ^ offset) for i in range(count)])


def mirrored(block, axis):
    count = lax.axis_size(axis)
    return lax.ppermute(block, axis, [(i, count - 1 - i) for i in range(count)])


def turned(block, axis):
    count = lax.axis_size(axis)
    return lax.ppermute(block, axis, [(i, (i + 1) % count) for i in range(count)])


def halves_of_sum(block, axis):
    count = lax.axis_size(axis)
    offset = 1
    while True:
        other = exchange(block, axis, offset)
        offset *= 2
        if offset >= count:
            return block, other
        block = block + other


def shape(dims, dtype):
    return jax.ShapeDtypeStruct(dims, dtype)


def call(kernel, name, outs, *operands, read, scratch=(), flops=0):
    many = isinstance(outs, list)
    nbytes = sum(o.size * o.dtype.itemsize for o in operands[:read])
    return pl.pallas_call(
        kernel,
        in_specs=[VMEM] * read + [ANY] * (len(operands) - read),
        out_specs=[VMEM] * len(outs) if many else VMEM,
        out_shape=outs,
        scratch_shapes=list(scratch),
        compiler_params=ROOM,
        cost_estimate=pl.CostEstimate(flops=flops, bytes_accessed=nbytes, transcendentals=0),
        name=name,
    )(*operands)


def folded_squares(rows):
    tokens, width = rows.shape
    total = jnp.zeros((tokens, LANES), F32)
    for at in range(0, width, LANES):
        part = rows[:, at : at + LANES]
        total = total + part * part
    return total


def latent_kernel(tiles, x1, x2, c2, down, up, gain, out_ref, vx1, scaled2, vc2, va1, vx2, va2, vb2, vgain, sems):
    tokens, width = vx1.shape
    latent = va1.shape[0]
    tile = width // tiles
    groups = (
        ((x1.at[0], vx1), (down.at[0, 0], va1)),
        ((x2.at[0], vx2), (down.at[1, 0], va2)),
        ((c2.at[0], vc2), (up.at[1, 0], vb2)),
    )

    def copies(job, at):
        cols = pl.ds(at * tile, tile)
        return [
            pltpu.make_async_copy(src.at[:, cols], dst.at[:, cols], sems.at[job, k, at])
            for k, (src, dst) in enumerate(groups[job])
        ]

    whole_gain = pltpu.make_async_copy(gain, vgain, sems.at[len(groups), 0, 0])
    whole_gain.start()
    for job in range(len(groups)):
        for at in range(tiles):
            for copy in copies(job, at):
                copy.start()
    base = 2 * latent + tokens
    out_ref[...] = jnp.zeros_like(out_ref)
    whole_gain.wait()

    def step(job, at):
        for copy in copies(job, at):
            copy.wait()
        cols = pl.ds(pl.multiple_of(at * tile, LANES), tile)
        if job < 2:
            rows = (vx1, vx2)[job][:, cols].astype(F32)
            right = (rows * vgain[job : job + 1, cols].astype(F32)).astype(BF16)
            squares = folded_squares(rows)
        if job == 0:
            raw = lax.dot_general(right, va1[:, cols], BOTH_LAST, preferred_element_type=F32)
            for piece in range(latent // LANES):
                out_ref[base + piece * tokens : base + (piece + 1) * tokens] += raw[:, piece * LANES : (piece + 1) * LANES]
            out_ref[base + (latent // LANES) * tokens :] += squares
        elif job == 1:
            scaled2[:, cols] = right
            out_ref[:latent] += lax.dot_general(va2[:, cols], right, BOTH_LAST, preferred_element_type=F32)
            out_ref[2 * latent : base] += squares
        else:
            out_ref[latent : 2 * latent] += lax.dot_general(
                vb2[:, cols], vc2[:, cols], BOTH_LAST, preferred_element_type=F32
            )

    for job in range(len(groups)):
        lax.fori_loop(0, tiles, lambda at, _, job=job: step(job, at) or 0, 0)


def fetch_kernel(in_ref, *rest):
    out_ref, sem = rest[-2:]
    copy = pltpu.make_async_copy(in_ref.at[0, 0], out_ref, sem)
    copy.start()
    copy.wait()


def leaving_kernel(start, own_ref, other_ref, x_ref, b_ref, *rest):
    out_ref = rest[-1]
    latent = b_ref.shape[0]
    count, width = out_ref.shape
    tokens = x_ref.shape[0]

    def summed(at):
        rows = slice(at + start, at + start + count)
        return own_ref[rows] + other_ref[rows]

    base = own_ref.shape[0] - tokens
    rscale = lax.rsqrt(jnp.sum(summed(base), axis=1, keepdims=True) / D + 1e-06)
    base -= (latent // LANES) * tokens
    hidden = jnp.concatenate([summed(base + at * tokens) * rscale for at in range(latent // LANES)], axis=1).astype(BF16)
    last = lax.axis_index("pipe") == lax.axis_size("pipe") - 1
    step = width // (4 if width % (4 * LANES) == 0 else 2)
    for at in range(0, width, step):
        cols = slice(at, at + step)
        rows = x_ref[start : start + count, cols].astype(F32)
        rows += jnp.dot(hidden, b_ref[:, cols], preferred_element_type=F32)
        out_ref[:, cols] = jnp.where(last, 0.0, rows).astype(BF16)


def grad_kernel(experts, start, own_ref, other_ref, x_ref, c_ref, *rest):
    outs, rows_ref = rest[-1 - experts : -1], rest[-1]
    latent = rows_ref.shape[1]
    depth = latent // experts
    cols = slice(start, start + outs[0].shape[2])
    me = lax.axis_index("expert")
    squares = own_ref[2 * latent : 2 * latent + LANES] + other_ref[2 * latent : 2 * latent + LANES]
    rscale = lax.rsqrt(jnp.sum(squares.T, axis=0, keepdims=True) / D + 1e-06)
    rows_ref[0] = (own_ref[latent : 2 * latent] + other_ref[latent : 2 * latent]) * rscale
    rows_ref[1] = (own_ref[:latent] + other_ref[:latent]) * rscale
    for side, right in enumerate((x_ref[:, cols], c_ref[:, cols])):
        left = jnp.concatenate(
            [rows_ref[side, pl.ds(pl.multiple_of((me ^ k) * depth, depth), depth), :] for k in range(experts)]
        )
        both = jnp.dot(left.astype(BF16), right, preferred_element_type=F32).astype(BF16)
        for k in range(experts):
            outs[k][side] = both[k * depth : (k + 1) * depth]


def share_kernel(experts, *refs):
    total = refs[0][...].astype(F32)
    for ref in refs[1:experts]:
        total = total + ref[...].astype(F32)
    refs[-1][...] = total.astype(BF16)


def update_kernel(start, share_ref, master_ref, moment_ref, second_ref, *rest):
    fresh_ref, peak_ref, wide = rest[-3:]
    cols = slice(start, start + share_ref.shape[2])
    grad = share_ref[...].astype(F32)
    first = 0.9 * moment_ref[:, 0, :, cols].astype(F32) + 0.1 * grad
    secnd = 0.95 * second_ref[:, 0, :, cols].astype(F32) + 0.05 * grad * grad
    update = first / (1.0 - 0.9**10) / (jnp.sqrt(secnd / (1.0 - 0.95**10)) + 1e-08)
    weights = master_ref[:, 0, :, cols]
    fresh = weights - 0.01 * (update + 0.1 * weights)
    fresh_ref[...] = fresh
    peak_ref[...] = jnp.zeros_like(peak_ref) if start == 0 else rest[0][...]
    wide[...] = jnp.zeros_like(wide)
    for side in range(2):
        peak = jnp.max(jnp.abs(fresh[side]), axis=0, keepdims=True)
        for at in range(0, peak.shape[1], LANES):
            block = (start + at) // LANES
            wide[side, block : block + 1, :] = peak[:, at : at + LANES]
        peak_ref[side : side + 1, :] = jnp.maximum(
            peak_ref[side : side + 1, :], jnp.max(wide[side].T, axis=0, keepdims=True)
        )


def merged(refs):
    top = refs[0][...]
    for ref in refs[1:]:
        top = jnp.maximum(top, ref[...])
    return top + 1e-06


def code_kernel(group, *refs):
    peak_refs, fresh_refs, code_ref = refs[:group], refs[group:-1], refs[-1]
    column = (1.0 / merged(peak_refs)).T
    for side in range(2):
        inverse = jnp.broadcast_to(column[:, side : side + 1], (LANES, LANES))
        block = 0
        for ref in fresh_refs:
            for at in range(0, ref.shape[2], LANES):
                code_ref[side, 0, :, block * LANES : (block + 1) * LANES] = (
                    ref[side, :, at : at + LANES] * inverse[block : block + 1]
                ).astype(BF16)
                block += 1


def scale_kernel(group, experts, *refs):
    peak_refs, scale_ref = refs[:experts], refs[-1]
    blocks = scale_ref.shape[3]
    mine = lax.axis_index("expert") // group
    for far in range(len(peak_refs) // group):
        top = merged(peak_refs[far * group : (far + 1) * group])
        for side in range(2):
            scale_ref[side, 0, pl.ds(mine ^ far, 1), :] = top[side : side + 1, :blocks]


def place_kernel(start, in_ref, *rest):
    out_ref, sem = rest[-2:]
    copy = pltpu.make_async_copy(in_ref, out_ref.at[0, pl.ds(start, in_ref.shape[0])], sem)
    copy.start()
    copy.wait()


def shards(enter_fwd, enter_rev, cot_rev, gain, proj_down, proj_up, master, moment, second):
    tokens, width = enter_fwd.shape[1:]
    latent = proj_down.shape[2]
    experts = lax.axis_size("expert")
    depth = latent // experts
    blocks = width // LANES
    tiles = 2
    weights = [8, 7, 7, 6]
    edges = [blocks * sum(weights[:k]) // sum(weights) * LANES for k in range(len(weights) + 1)]
    chunks = list(zip(edges[:-1], edges[1:]))

    def streamed(array):
        return pltpu.with_memory_space_constraint(array, pltpu.HBM)

    pack_rows = 2 * latent + tokens + (latent // LANES + 1) * tokens
    held = pltpu.VMEM((tokens, width), BF16)
    packed, rows1, scaled2, cot2 = pl.pallas_call(
        lambda *refs: latent_kernel(tiles, *refs),
        in_specs=[ANY] * 6,
        out_specs=[VMEM] * 4,
        out_shape=[pltpu.VMEM((pack_rows, LANES), F32), held, held, held],
        scratch_shapes=[
            pltpu.VMEM((latent, width), BF16),
            pltpu.VMEM((tokens, width), BF16),
            pltpu.VMEM((latent, width), BF16),
            pltpu.VMEM((latent, width), BF16),
            pltpu.VMEM((2, width), BF16),
            pltpu.SemaphoreType.DMA((4, 2, tiles)),
        ],
        compiler_params=ROOM,
        cost_estimate=pl.CostEstimate(
            flops=6 * tokens * latent * width, bytes_accessed=6 * (tokens + latent) * width, transcendentals=0
        ),
        name="latents",
    )(*(streamed(a) for a in (enter_fwd, enter_rev, cot_rev, proj_down, proj_up, gain.reshape(2, width))))
    own_up = pl.pallas_call(
        fetch_kernel,
        in_specs=[ANY] * 2,
        out_specs=VMEM,
        out_shape=pltpu.VMEM((latent, width), BF16),
        scratch_shapes=[pltpu.SemaphoreType.DMA],
        compiler_params=ROOM,
        cost_estimate=pl.CostEstimate(flops=0, bytes_accessed=2 * latent * width, transcendentals=0),
        name="fetch",
    )(streamed(proj_up), packed)
    pair = halves_of_sum(packed, "dp")

    def leaving(start, count, *after):
        return call(
            lambda *refs: leaving_kernel(start, *refs),
            "leaving",
            shape((count, width), BF16),
            *pair,
            rows1,
            own_up,
            *after,
            read=4,
            flops=2 * count * latent * width,
        )

    def grads(chunk, *after):
        start, stop = chunks[chunk]
        return call(
            lambda *refs: grad_kernel(experts, start, *refs),
            "grads",
            [shape((2, depth, stop - start), BF16)] * experts,
            *pair,
            scaled2,
            cot2,
            *after,
            read=4,
            scratch=[pltpu.VMEM((2, latent, tokens), F32)],
            flops=4 * tokens * latent * (stop - start),
        )

    head = 112
    first_rows = leaving(0, head)
    left_head = turned(first_rows, "pipe")
    first = grads(0, first_rows)
    shares, arrived, others = [], [], []
    for chunk in range(len(chunks)):
        own, *pieces = grads(chunk, *shares[-2:-1], *others[-1][:1]) if chunk else first
        others.append([exchange(piece, "expert", 1 + k) for k, piece in enumerate(pieces)])
        after = [left_head] if chunk == 1 else arrived[chunk - 2 : chunk - 1] if chunk > 1 else []
        shares.append(
            call(
                lambda *refs: share_kernel(experts, *refs),
                "share",
                shape(own.shape, BF16),
                own,
                *others[-1],
                *after,
                read=experts,
            )
        )
        arrived.append(mirrored(shares[-1], "pipe"))
    left_tail = turned(leaving(head, tokens - head, arrived[-2]), "pipe")

    def place(start, rows, kept=(), after=()):
        return pl.pallas_call(
            lambda *refs: place_kernel(start, *refs),
            in_specs=[ANY] * (1 + len(kept) + len(after)),
            out_specs=ANY,
            out_shape=shape((1, tokens, width), BF16),
            scratch_shapes=[pltpu.SemaphoreType.DMA],
            input_output_aliases={1 + k: k for k in range(len(kept))},
            compiler_params=ROOM,
            cost_estimate=pl.CostEstimate(flops=0, bytes_accessed=4 * rows.shape[0] * width, transcendentals=0),
            name="place",
        )(rows, *kept, *after)

    placed = place(0, left_head)

    fresh, peaks = [], None
    for chunk, (start, stop) in enumerate(chunks):
        kept = () if peaks is None else (peaks,)
        after = (placed,) if chunk == len(chunks) - 1 else ()
        some, peaks = call(
            lambda *refs: update_kernel(start, *refs),
            "update",
            [shape((2, depth, stop - start), F32), shape((8, LANES), F32)],
            arrived[chunk],
            master,
            moment,
            second,
            *kept,
            *after,
            read=4 + len(kept),
            scratch=[pltpu.VMEM((2, LANES, LANES), F32)],
            flops=40 * depth * (stop - start),
        )
        fresh.append(some)

    group = LANES // depth
    peak_rows = [peaks] + [exchange(peaks, "expert", k) for k in range(1, experts)]
    coded = call(
        lambda *refs: code_kernel(group, *refs),
        "codes",
        shape((2, 1, depth, width), BF16),
        *peak_rows[:group],
        *fresh,
        read=group + len(fresh),
        flops=4 * depth * width,
    )
    scales = call(
        lambda *refs: scale_kernel(group, experts, *refs),
        "scales",
        shape((2, 1, experts // group, blocks), F32),
        *peak_rows,
        coded,
        read=experts,
    )
    return (place(head, left_tail, (placed,), (coded,)), coded, scales)


def solution(mesh):
    in_specs = (
        P("pipe", "expert", "dp"),
        P("pipe", "expert", "dp"),
        P("pipe", "expert", "dp"),
        P(None, "pipe", "dp"),
        P(None, "pipe", None, "dp"),
        P(None, "pipe", None, "dp"),
        P(None, "pipe", "expert", "dp"),
        P(None, "pipe", "expert", "dp"),
        P(None, "pipe", "expert", "dp"),
    )
    out_specs = (
        P("pipe", "expert", "dp"),
        P(None, "pipe", "expert", "dp"),
        P(None, "pipe", None, "dp"),
    )
    return jax.shard_map(shards, mesh=mesh, in_specs=in_specs, out_specs=out_specs, check_vma=False)
```

```python
import jax
import jax.numpy as jnp
from jax import lax
from jax.experimental import pallas as pl
from jax.experimental.pallas import tpu as pltpu
from jax.sharding import PartitionSpec as P

D = 7168
LANES = 128
F32 = jnp.float32
BF16 = jnp.bfloat16
BOTH_LAST = (((1,), (1,)), ((), ()))
ROOM = pltpu.CompilerParams(vmem_limit_bytes=16 << 20)
ANY = pl.BlockSpec(memory_space=pl.ANY)
VMEM = pl.BlockSpec(memory_space=pltpu.VMEM)


def exchange(block, axis, offset):
    count = lax.axis_size(axis)
    return lax.ppermute(block, axis, [(i, i ^ offset) for i in range(count)])


def mirrored(block, axis):
    count = lax.axis_size(axis)
    return lax.ppermute(block, axis, [(i, count - 1 - i) for i in range(count)])


def turned(block, axis):
    count = lax.axis_size(axis)
    return lax.ppermute(block, axis, [(i, (i + 1) % count) for i in range(count)])


def halves_of_sum(block, axis):
    count = lax.axis_size(axis)
    offset = 1
    while True:
        other = exchange(block, axis, offset)
        offset *= 2
        if offset >= count:
            return block, other
        block = block + other


def shape(dims, dtype):
    return jax.ShapeDtypeStruct(dims, dtype)


def call(kernel, name, outs, *operands, read, scratch=(), flops=0):
    many = isinstance(outs, list)
    nbytes = sum(o.size * o.dtype.itemsize for o in operands[:read])
    return pl.pallas_call(
        kernel,
        in_specs=[VMEM] * read + [ANY] * (len(operands) - read),
        out_specs=[VMEM] * len(outs) if many else VMEM,
        out_shape=outs,
        scratch_shapes=list(scratch),
        compiler_params=ROOM,
        cost_estimate=pl.CostEstimate(flops=flops, bytes_accessed=nbytes, transcendentals=0),
        name=name,
    )(*operands)


def folded_squares(rows):
    tokens, width = rows.shape
    total = jnp.zeros((tokens, LANES), F32)
    for at in range(0, width, LANES):
        part = rows[:, at : at + LANES]
        total = total + part * part
    return total


def latent_kernel(tiles, x1, x2, c2, down, up, gain, out_ref, vx1, scaled2, vc2, va1, vx2, va2, vb2, vgain, sems):
    tokens, width = vx1.shape
    latent = va1.shape[0]
    tile = width // tiles
    groups = (
        ((x1.at[0], vx1), (down.at[0, 0], va1)),
        ((x2.at[0], vx2), (down.at[1, 0], va2)),
        ((c2.at[0], vc2), (up.at[1, 0], vb2)),
    )

    def copies(job, at):
        cols = pl.ds(at * tile, tile)
        return [
            pltpu.make_async_copy(src.at[:, cols], dst.at[:, cols], sems.at[job, k, at])
            for k, (src, dst) in enumerate(groups[job])
        ]

    whole_gain = pltpu.make_async_copy(gain, vgain, sems.at[len(groups), 0, 0])
    whole_gain.start()
    for job in range(len(groups)):
        for at in range(tiles):
            for copy in copies(job, at):
                copy.start()
    base = 2 * latent + tokens
    out_ref[...] = jnp.zeros_like(out_ref)
    whole_gain.wait()

    def step(job, at):
        for copy in copies(job, at):
            copy.wait()
        cols = pl.ds(pl.multiple_of(at * tile, LANES), tile)
        if job < 2:
            rows = (vx1, vx2)[job][:, cols].astype(F32)
            right = (rows * vgain[job : job + 1, cols].astype(F32)).astype(BF16)
            squares = folded_squares(rows)
        if job == 0:
            raw = lax.dot_general(right, va1[:, cols], BOTH_LAST, preferred_element_type=F32)
            for piece in range(latent // LANES):
                out_ref[base + piece * tokens : base + (piece + 1) * tokens] += raw[:, piece * LANES : (piece + 1) * LANES]
            out_ref[base + (latent // LANES) * tokens :] += squares
        elif job == 1:
            scaled2[:, cols] = right
            out_ref[:latent] += lax.dot_general(va2[:, cols], right, BOTH_LAST, preferred_element_type=F32)
            out_ref[2 * latent : base] += squares
        else:
            out_ref[latent : 2 * latent] += lax.dot_general(
                vb2[:, cols], vc2[:, cols], BOTH_LAST, preferred_element_type=F32
            )

    for job in range(len(groups)):
        lax.fori_loop(0, tiles, lambda at, _, job=job: step(job, at) or 0, 0)


def fetch_kernel(in_ref, *rest):
    out_ref, sem = rest[-2:]
    copy = pltpu.make_async_copy(in_ref.at[0, 0], out_ref, sem)
    copy.start()
    copy.wait()


def leaving_kernel(start, own_ref, other_ref, x_ref, b_ref, *rest):
    out_ref = rest[-1]
    latent = b_ref.shape[0]
    count, width = out_ref.shape
    tokens = x_ref.shape[0]

    def summed(at):
        rows = slice(at + start, at + start + count)
        return own_ref[rows] + other_ref[rows]

    base = own_ref.shape[0] - tokens
    rscale = lax.rsqrt(jnp.sum(summed(base), axis=1, keepdims=True) / D + 1e-06)
    base -= (latent // LANES) * tokens
    hidden = jnp.concatenate([summed(base + at * tokens) * rscale for at in range(latent // LANES)], axis=1).astype(BF16)
    last = lax.axis_index("pipe") == lax.axis_size("pipe") - 1
    step = width // (4 if width % (4 * LANES) == 0 else 2)
    for at in range(0, width, step):
        cols = slice(at, at + step)
        rows = x_ref[start : start + count, cols].astype(F32)
        rows += jnp.dot(hidden, b_ref[:, cols], preferred_element_type=F32)
        out_ref[:, cols] = jnp.where(last, 0.0, rows).astype(BF16)


def grad_kernel(experts, start, own_ref, other_ref, x_ref, c_ref, *rest):
    outs, rows_ref = rest[-1 - experts : -1], rest[-1]
    latent = rows_ref.shape[1]
    depth = latent // experts
    cols = slice(start, start + outs[0].shape[2])
    me = lax.axis_index("expert")
    squares = own_ref[2 * latent : 2 * latent + LANES] + other_ref[2 * latent : 2 * latent + LANES]
    rscale = lax.rsqrt(jnp.sum(squares.T, axis=0, keepdims=True) / D + 1e-06)
    rows_ref[0] = (own_ref[latent : 2 * latent] + other_ref[latent : 2 * latent]) * rscale
    rows_ref[1] = (own_ref[:latent] + other_ref[:latent]) * rscale
    for side, right in enumerate((x_ref[:, cols], c_ref[:, cols])):
        left = jnp.concatenate(
            [rows_ref[side, pl.ds(pl.multiple_of((me ^ k) * depth, depth), depth), :] for k in range(experts)]
        )
        both = jnp.dot(left.astype(BF16), right, preferred_element_type=F32).astype(BF16)
        for k in range(experts):
            outs[k][side] = both[k * depth : (k + 1) * depth]


def share_kernel(experts, *refs):
    total = refs[0][...].astype(F32)
    for ref in refs[1:experts]:
        total = total + ref[...].astype(F32)
    refs[-1][...] = total.astype(BF16)


def update_kernel(start, share_ref, master_ref, moment_ref, second_ref, *rest):
    fresh_ref, peak_ref, wide = rest[-3:]
    cols = slice(start, start + share_ref.shape[2])
    grad = share_ref[...].astype(F32)
    first = 0.9 * moment_ref[:, 0, :, cols].astype(F32) + 0.1 * grad
    secnd = 0.95 * second_ref[:, 0, :, cols].astype(F32) + 0.05 * grad * grad
    update = first / (1.0 - 0.9**10) / (jnp.sqrt(secnd / (1.0 - 0.95**10)) + 1e-08)
    weights = master_ref[:, 0, :, cols]
    fresh = weights - 0.01 * (update + 0.1 * weights)
    fresh_ref[...] = fresh
    peak_ref[...] = jnp.zeros_like(peak_ref) if start == 0 else rest[0][...]
    wide[...] = jnp.zeros_like(wide)
    for side in range(2):
        peak = jnp.max(jnp.abs(fresh[side]), axis=0, keepdims=True)
        for at in range(0, peak.shape[1], LANES):
            block = (start + at) // LANES
            wide[side, block : block + 1, :] = peak[:, at : at + LANES]
        peak_ref[side : side + 1, :] = jnp.maximum(
            peak_ref[side : side + 1, :], jnp.max(wide[side].T, axis=0, keepdims=True)
        )


def merged(refs):
    top = refs[0][...]
    for ref in refs[1:]:
        top = jnp.maximum(top, ref[...])
    return top + 1e-06


def code_kernel(group, *refs):
    peak_refs, fresh_refs, (code_ref, token_ref) = refs[:group], refs[group:-2], refs[-2:]
    token_ref[...] = jnp.zeros_like(token_ref)
    column = (1.0 / merged(peak_refs)).T
    for side in range(2):
        inverse = jnp.broadcast_to(column[:, side : side + 1], (LANES, LANES))
        block = 0
        for ref in fresh_refs:
            for at in range(0, ref.shape[2], LANES):
                code_ref[side, 0, :, block * LANES : (block + 1) * LANES] = (
                    ref[side, :, at : at + LANES] * inverse[block : block + 1]
                ).astype(BF16)
                block += 1


def scale_kernel(group, experts, *refs):
    peak_refs, scale_ref = refs[:experts], refs[-1]
    blocks = scale_ref.shape[3]
    mine = lax.axis_index("expert") // group
    for far in range(len(peak_refs) // group):
        top = merged(peak_refs[far * group : (far + 1) * group])
        for side in range(2):
            scale_ref[side, 0, pl.ds(mine ^ far, 1), :] = top[side : side + 1, :blocks]


def place_kernel(start, in_ref, *rest):
    out_ref, token_ref, sem = rest[-3:]
    copy = pltpu.make_async_copy(in_ref, out_ref.at[0, pl.ds(start, in_ref.shape[0])], sem)
    copy.start()
    token_ref[...] = jnp.zeros_like(token_ref)
    copy.wait()


def shards(enter_fwd, enter_rev, cot_rev, gain, proj_down, proj_up, master, moment, second):
    tokens, width = enter_fwd.shape[1:]
    latent = proj_down.shape[2]
    experts = lax.axis_size("expert")
    depth = latent // experts
    blocks = width // LANES
    tiles = 2
    weights = [8, 7, 7, 6]
    edges = [blocks * sum(weights[:k]) // sum(weights) * LANES for k in range(len(weights) + 1)]
    chunks = list(zip(edges[:-1], edges[1:]))

    def streamed(array):
        return pltpu.with_memory_space_constraint(array, pltpu.HBM)

    pack_rows = 2 * latent + tokens + (latent // LANES + 1) * tokens
    held = pltpu.VMEM((tokens, width), BF16)
    packed, rows1, scaled2, cot2 = pl.pallas_call(
        lambda *refs: latent_kernel(tiles, *refs),
        in_specs=[ANY] * 6,
        out_specs=[VMEM] * 4,
        out_shape=[pltpu.VMEM((pack_rows, LANES), F32), held, held, held],
        scratch_shapes=[
            pltpu.VMEM((latent, width), BF16),
            pltpu.VMEM((tokens, width), BF16),
            pltpu.VMEM((latent, width), BF16),
            pltpu.VMEM((latent, width), BF16),
            pltpu.VMEM((2, width), BF16),
            pltpu.SemaphoreType.DMA((4, 2, tiles)),
        ],
        compiler_params=ROOM,
        cost_estimate=pl.CostEstimate(
            flops=6 * tokens * latent * width, bytes_accessed=6 * (tokens + latent) * width, transcendentals=0
        ),
        name="latents",
    )(*(streamed(a) for a in (enter_fwd, enter_rev, cot_rev, proj_down, proj_up, gain.reshape(2, width))))
    own_up = pl.pallas_call(
        fetch_kernel,
        in_specs=[ANY] * 2,
        out_specs=VMEM,
        out_shape=pltpu.VMEM((latent, width), BF16),
        scratch_shapes=[pltpu.SemaphoreType.DMA],
        compiler_params=ROOM,
        cost_estimate=pl.CostEstimate(flops=0, bytes_accessed=2 * latent * width, transcendentals=0),
        name="fetch",
    )(streamed(proj_up), packed)
    pair = halves_of_sum(packed, "dp")

    def leaving(start, count, *after):
        return call(
            lambda *refs: leaving_kernel(start, *refs),
            "leaving",
            shape((count, width), BF16),
            *pair,
            rows1,
            own_up,
            *after,
            read=4,
            flops=2 * count * latent * width,
        )

    def grads(chunk, *after):
        start, stop = chunks[chunk]
        return call(
            lambda *refs: grad_kernel(experts, start, *refs),
            "grads",
            [shape((2, depth, stop - start), BF16)] * experts,
            *pair,
            scaled2,
            cot2,
            *after,
            read=4,
            scratch=[pltpu.VMEM((2, latent, tokens), F32)],
            flops=4 * tokens * latent * (stop - start),
        )

    head = 112
    first_rows = leaving(0, head)
    left_head = turned(first_rows, "pipe")
    first = grads(0, first_rows)
    shares, arrived, others = [], [], []
    for chunk in range(len(chunks)):
        own, *pieces = grads(chunk, *shares[-2:-1], *others[-1][:1]) if chunk else first
        others.append([exchange(piece, "expert", 1 + k) for k, piece in enumerate(pieces)])
        after = [left_head] if chunk == 1 else arrived[chunk - 2 : chunk - 1] if chunk > 1 else []
        shares.append(
            call(
                lambda *refs: share_kernel(experts, *refs),
                "share",
                shape(own.shape, BF16),
                own,
                *others[-1],
                *after,
                read=experts,
            )
        )
        arrived.append(mirrored(shares[-1], "pipe"))

    def place(start, rows, kept=(), after=()):
        return pl.pallas_call(
            lambda *refs: place_kernel(start, *refs),
            in_specs=[ANY] * (1 + len(kept) + len(after)),
            out_specs=[ANY, VMEM],
            out_shape=[shape((1, tokens, width), BF16), shape((8, LANES), F32)],
            scratch_shapes=[pltpu.SemaphoreType.DMA],
            input_output_aliases={1 + k: k for k in range(len(kept))},
            compiler_params=ROOM,
            cost_estimate=pl.CostEstimate(flops=0, bytes_accessed=4 * rows.shape[0] * width, transcendentals=0),
            name="place",
        )(rows, *kept, *after)

    placed, token = place(0, left_head)

    fresh, peaks, steps = [], None, []
    for chunk, (start, stop) in enumerate(chunks):
        kept = () if peaks is None else (peaks,)
        after = (token,) if chunk == 1 else ()
        some, peaks = call(
            lambda *refs: update_kernel(start, *refs),
            "update",
            [shape((2, depth, stop - start), F32), shape((8, LANES), F32)],
            arrived[chunk],
            master,
            moment,
            second,
            *kept,
            *after,
            read=4 + len(kept),
            scratch=[pltpu.VMEM((2, LANES, LANES), F32)],
            flops=40 * depth * (stop - start),
        )
        fresh.append(some)
        steps.append(peaks)

    left_tail = turned(leaving(head, tokens - head, steps[-2]), "pipe")

    group = LANES // depth
    peak_rows = [peaks] + [exchange(peaks, "expert", k) for k in range(1, experts)]
    coded, token = call(
        lambda *refs: code_kernel(group, *refs),
        "codes",
        [shape((2, 1, depth, width), BF16), shape((8, LANES), F32)],
        *peak_rows[:group],
        *fresh,
        read=group + len(fresh),
        flops=4 * depth * width,
    )
    scales = call(
        lambda *refs: scale_kernel(group, experts, *refs),
        "scales",
        shape((2, 1, experts // group, blocks), F32),
        *peak_rows,
        token,
        read=experts,
    )
    left, _ = place(head, left_tail, (placed,), (token,))
    return (left, coded, scales)


def solution(mesh):
    in_specs = (
        P("pipe", "expert", "dp"),
        P("pipe", "expert", "dp"),
        P("pipe", "expert", "dp"),
        P(None, "pipe", "dp"),
        P(None, "pipe", None, "dp"),
        P(None, "pipe", None, "dp"),
        P(None, "pipe", "expert", "dp"),
        P(None, "pipe", "expert", "dp"),
        P(None, "pipe", "expert", "dp"),
    )
    out_specs = (
        P("pipe", "expert", "dp"),
        P(None, "pipe", "expert", "dp"),
        P(None, "pipe", None, "dp"),
    )
    return jax.shard_map(shards, mesh=mesh, in_specs=in_specs, out_specs=out_specs, check_vma=False)
```

```python
import jax
import jax.numpy as jnp
from jax import lax
from jax.experimental import pallas as pl
from jax.experimental.pallas import tpu as pltpu
from jax.sharding import PartitionSpec as P

D = 7168
LANES = 128
F32 = jnp.float32
BF16 = jnp.bfloat16
BOTH_LAST = (((1,), (1,)), ((), ()))
ROOM = pltpu.CompilerParams(vmem_limit_bytes=16 << 20)
ANY = pl.BlockSpec(memory_space=pl.ANY)
VMEM = pl.BlockSpec(memory_space=pltpu.VMEM)


def exchange(block, axis, offset):
    count = lax.axis_size(axis)
    return lax.ppermute(block, axis, [(i, i ^ offset) for i in range(count)])


def mirrored(block, axis):
    count = lax.axis_size(axis)
    return lax.ppermute(block, axis, [(i, count - 1 - i) for i in range(count)])


def turned(block, axis):
    count = lax.axis_size(axis)
    return lax.ppermute(block, axis, [(i, (i + 1) % count) for i in range(count)])


def halves_of_sum(block, axis):
    count = lax.axis_size(axis)
    offset = 1
    while True:
        other = exchange(block, axis, offset)
        offset *= 2
        if offset >= count:
            return block, other
        block = block + other


def shape(dims, dtype):
    return jax.ShapeDtypeStruct(dims, dtype)


def call(kernel, name, outs, *operands, read, scratch=(), flops=0):
    many = isinstance(outs, list)
    nbytes = sum(o.size * o.dtype.itemsize for o in operands[:read])
    return pl.pallas_call(
        kernel,
        in_specs=[VMEM] * read + [ANY] * (len(operands) - read),
        out_specs=[VMEM] * len(outs) if many else VMEM,
        out_shape=outs,
        scratch_shapes=list(scratch),
        compiler_params=ROOM,
        cost_estimate=pl.CostEstimate(flops=flops, bytes_accessed=nbytes, transcendentals=0),
        name=name,
    )(*operands)


def folded_squares(rows):
    tokens, width = rows.shape
    total = jnp.zeros((tokens, LANES), F32)
    for at in range(0, width, LANES):
        part = rows[:, at : at + LANES]
        total = total + part * part
    return total


def latent_kernel(tiles, x1, x2, c2, down, up, gain, out_ref, vx1, scaled2, vc2, va1, vx2, va2, vb2, vgain, sems):
    tokens, width = vx1.shape
    latent = va1.shape[0]
    tile = width // tiles
    groups = (
        ((x1.at[0], vx1), (down.at[0, 0], va1)),
        ((x2.at[0], vx2), (down.at[1, 0], va2)),
        ((c2.at[0], vc2), (up.at[1, 0], vb2)),
    )

    def copies(job, at):
        cols = pl.ds(at * tile, tile)
        return [
            pltpu.make_async_copy(src.at[:, cols], dst.at[:, cols], sems.at[job, k, at])
            for k, (src, dst) in enumerate(groups[job])
        ]

    whole_gain = pltpu.make_async_copy(gain, vgain, sems.at[len(groups), 0, 0])
    whole_gain.start()
    for job in range(len(groups)):
        for at in range(tiles):
            for copy in copies(job, at):
                copy.start()
    base = 2 * latent + tokens
    out_ref[...] = jnp.zeros_like(out_ref)
    whole_gain.wait()

    def step(job, at):
        for copy in copies(job, at):
            copy.wait()
        cols = pl.ds(pl.multiple_of(at * tile, LANES), tile)
        if job < 2:
            rows = (vx1, vx2)[job][:, cols].astype(F32)
            right = (rows * vgain[job : job + 1, cols].astype(F32)).astype(BF16)
            squares = folded_squares(rows)
        if job == 0:
            raw = lax.dot_general(right, va1[:, cols], BOTH_LAST, preferred_element_type=F32)
            for piece in range(latent // LANES):
                out_ref[base + piece * tokens : base + (piece + 1) * tokens] += raw[:, piece * LANES : (piece + 1) * LANES]
            out_ref[base + (latent // LANES) * tokens :] += squares
        elif job == 1:
            scaled2[:, cols] = right
            out_ref[:latent] += lax.dot_general(va2[:, cols], right, BOTH_LAST, preferred_element_type=F32)
            out_ref[2 * latent : base] += squares
        else:
            out_ref[latent : 2 * latent] += lax.dot_general(
                vb2[:, cols], vc2[:, cols], BOTH_LAST, preferred_element_type=F32
            )

    for job in range(len(groups)):
        lax.fori_loop(0, tiles, lambda at, _, job=job: step(job, at) or 0, 0)


def fetch_kernel(in_ref, *rest):
    out_ref, sems = rest[-2:]
    step = out_ref.shape[0] // sems.shape[0]
    copies = []
    for k in range(sems.shape[0]):
        rows = pl.ds(k * step, step)
        copies.append(pltpu.make_async_copy(in_ref.at[0, 0, rows], out_ref.at[rows], sems.at[k]))
    for copy in copies:
        copy.start()
    for copy in copies:
        copy.wait()


def leaving_kernel(start, own_ref, other_ref, x_ref, b_ref, *rest):
    out_ref = rest[-1]
    latent = b_ref.shape[0]
    count, width = out_ref.shape
    tokens = x_ref.shape[0]

    def summed(at):
        rows = slice(at + start, at + start + count)
        return own_ref[rows] + other_ref[rows]

    base = own_ref.shape[0] - tokens
    rscale = lax.rsqrt(jnp.sum(summed(base), axis=1, keepdims=True) / D + 1e-06)
    base -= (latent // LANES) * tokens
    hidden = jnp.concatenate([summed(base + at * tokens) * rscale for at in range(latent // LANES)], axis=1).astype(BF16)
    last = lax.axis_index("pipe") == lax.axis_size("pipe") - 1
    step = width // (4 if width % (4 * LANES) == 0 else 2)
    for at in range(0, width, step):
        cols = slice(at, at + step)
        rows = x_ref[start : start + count, cols].astype(F32)
        rows += jnp.dot(hidden, b_ref[:, cols], preferred_element_type=F32)
        out_ref[:, cols] = jnp.where(last, 0.0, rows).astype(BF16)


def grad_kernel(experts, start, own_ref, other_ref, x_ref, c_ref, *rest):
    outs, rows_ref = rest[-1 - experts : -1], rest[-1]
    latent = rows_ref.shape[1]
    depth = latent // experts
    cols = slice(start, start + outs[0].shape[2])
    me = lax.axis_index("expert")
    squares = own_ref[2 * latent : 2 * latent + LANES] + other_ref[2 * latent : 2 * latent + LANES]
    rscale = lax.rsqrt(jnp.sum(squares.T, axis=0, keepdims=True) / D + 1e-06)
    rows_ref[0] = (own_ref[latent : 2 * latent] + other_ref[latent : 2 * latent]) * rscale
    rows_ref[1] = (own_ref[:latent] + other_ref[:latent]) * rscale
    for side, right in enumerate((x_ref[:, cols], c_ref[:, cols])):
        left = jnp.concatenate(
            [rows_ref[side, pl.ds(pl.multiple_of((me ^ k) * depth, depth), depth), :] for k in range(experts)]
        )
        both = jnp.dot(left.astype(BF16), right, preferred_element_type=F32).astype(BF16)
        for k in range(experts):
            outs[k][side] = both[k * depth : (k + 1) * depth]


def share_kernel(experts, *refs):
    total = refs[0][...].astype(F32)
    for ref in refs[1:experts]:
        total = total + ref[...].astype(F32)
    refs[-1][...] = total.astype(BF16)


def update_kernel(start, share_ref, master_ref, moment_ref, second_ref, *rest):
    fresh_ref, peak_ref, wide = rest[-3:]
    cols = slice(start, start + share_ref.shape[2])
    grad = share_ref[...].astype(F32)
    first = 0.9 * moment_ref[:, 0, :, cols].astype(F32) + 0.1 * grad
    secnd = 0.95 * second_ref[:, 0, :, cols].astype(F32) + 0.05 * grad * grad
    update = first / (1.0 - 0.9**10) / (jnp.sqrt(secnd / (1.0 - 0.95**10)) + 1e-08)
    weights = master_ref[:, 0, :, cols]
    fresh = weights - 0.01 * (update + 0.1 * weights)
    fresh_ref[...] = fresh
    peak_ref[...] = jnp.zeros_like(peak_ref) if start == 0 else rest[0][...]
    wide[...] = jnp.zeros_like(wide)
    for side in range(2):
        peak = jnp.max(jnp.abs(fresh[side]), axis=0, keepdims=True)
        for at in range(0, peak.shape[1], LANES):
            block = (start + at) // LANES
            wide[side, block : block + 1, :] = peak[:, at : at + LANES]
        peak_ref[side : side + 1, :] = jnp.maximum(
            peak_ref[side : side + 1, :], jnp.max(wide[side].T, axis=0, keepdims=True)
        )


def code_kernel(peak_ref, *refs):
    fresh_refs, (code_ref, token_ref) = refs[:-2], refs[-2:]
    token_ref[...] = jnp.zeros_like(token_ref)
    column = (1.0 / (peak_ref[...] + 1e-06)).T
    for side in range(2):
        inverse = jnp.broadcast_to(column[:, side : side + 1], (LANES, LANES))
        block = 0
        for ref in fresh_refs:
            for at in range(0, ref.shape[2], LANES):
                code_ref[side, 0, :, block * LANES : (block + 1) * LANES] = (
                    ref[side, :, at : at + LANES] * inverse[block : block + 1]
                ).astype(BF16)
                block += 1


def finish_kernel(start, group, tail_ref, placed_ref, token_ref, *refs):
    peak_refs, (left_ref, scale_ref, sem) = refs[:-3], refs[-3:]
    copy = pltpu.make_async_copy(tail_ref, left_ref.at[0, pl.ds(start, tail_ref.shape[0])], sem)
    copy.start()
    blocks = scale_ref.shape[3]
    mine = lax.axis_index("expert") // group
    for far, ref in enumerate(peak_refs):
        for side in range(2):
            scale_ref[side, 0, pl.ds(mine ^ far, 1), :] = ref[side : side + 1, :blocks] + 1e-06
    copy.wait()


def place_kernel(in_ref, out_ref, token_ref, sem):
    copy = pltpu.make_async_copy(in_ref, out_ref.at[0, pl.ds(0, in_ref.shape[0])], sem)
    copy.start()
    token_ref[...] = jnp.zeros_like(token_ref)
    copy.wait()


def shards(enter_fwd, enter_rev, cot_rev, gain, proj_down, proj_up, master, moment, second):
    tokens, width = enter_fwd.shape[1:]
    latent = proj_down.shape[2]
    experts = lax.axis_size("expert")
    depth = latent // experts
    blocks = width // LANES
    tiles = 2
    weights = [8, 7, 7, 6]
    edges = [blocks * sum(weights[:k]) // sum(weights) * LANES for k in range(len(weights) + 1)]
    chunks = list(zip(edges[:-1], edges[1:]))

    def streamed(array):
        return pltpu.with_memory_space_constraint(array, pltpu.HBM)

    pack_rows = 2 * latent + tokens + (latent // LANES + 1) * tokens
    held = pltpu.VMEM((tokens, width), BF16)
    packed, rows1, scaled2, cot2 = pl.pallas_call(
        lambda *refs: latent_kernel(tiles, *refs),
        in_specs=[ANY] * 6,
        out_specs=[VMEM] * 4,
        out_shape=[pltpu.VMEM((pack_rows, LANES), F32), held, held, held],
        scratch_shapes=[
            pltpu.VMEM((latent, width), BF16),
            pltpu.VMEM((tokens, width), BF16),
            pltpu.VMEM((latent, width), BF16),
            pltpu.VMEM((latent, width), BF16),
            pltpu.VMEM((2, width), BF16),
            pltpu.SemaphoreType.DMA((4, 2, tiles)),
        ],
        compiler_params=ROOM,
        cost_estimate=pl.CostEstimate(
            flops=6 * tokens * latent * width, bytes_accessed=6 * (tokens + latent) * width, transcendentals=0
        ),
        name="latents",
    )(*(streamed(a) for a in (enter_fwd, enter_rev, cot_rev, proj_down, proj_up, gain.reshape(2, width))))
    own_up = pl.pallas_call(
        fetch_kernel,
        in_specs=[ANY] * 2,
        out_specs=VMEM,
        out_shape=pltpu.VMEM((latent, width), BF16),
        scratch_shapes=[pltpu.SemaphoreType.DMA((4,))],
        compiler_params=ROOM,
        cost_estimate=pl.CostEstimate(flops=0, bytes_accessed=2 * latent * width, transcendentals=0),
        name="fetch",
    )(streamed(proj_up), packed)
    pair = halves_of_sum(packed, "dp")

    def leaving(start, count, *after):
        return call(
            lambda *refs: leaving_kernel(start, *refs),
            "leaving",
            shape((count, width), BF16),
            *pair,
            rows1,
            own_up,
            *after,
            read=4,
            flops=2 * count * latent * width,
        )

    def grads(chunk, *after):
        start, stop = chunks[chunk]
        return call(
            lambda *refs: grad_kernel(experts, start, *refs),
            "grads",
            [shape((2, depth, stop - start), BF16)] * experts,
            *pair,
            scaled2,
            cot2,
            *after,
            read=4,
            scratch=[pltpu.VMEM((2, latent, tokens), F32)],
            flops=4 * tokens * latent * (stop - start),
        )

    head = 112
    first_rows = leaving(0, head)
    left_head = turned(first_rows, "pipe")
    first = grads(0, first_rows)
    shares, arrived, others = [], [], []
    for chunk in range(len(chunks)):
        own, *pieces = grads(chunk, *shares[-2:-1], *others[-1][:1]) if chunk else first
        others.append([exchange(piece, "expert", 1 + k) for k, piece in enumerate(pieces)])
        after = [left_head] if chunk == 1 else arrived[chunk - 2 : chunk - 1] if chunk > 1 else []
        shares.append(
            call(
                lambda *refs: share_kernel(experts, *refs),
                "share",
                shape(own.shape, BF16),
                own,
                *others[-1],
                *after,
                read=experts,
            )
        )
        arrived.append(mirrored(shares[-1], "pipe"))

    placed, token = pl.pallas_call(
        place_kernel,
        in_specs=[ANY],
        out_specs=[ANY, VMEM],
        out_shape=[shape((1, tokens, width), BF16), shape((8, LANES), F32)],
        scratch_shapes=[pltpu.SemaphoreType.DMA],
        compiler_params=ROOM,
        cost_estimate=pl.CostEstimate(flops=0, bytes_accessed=4 * head * width, transcendentals=0),
        name="place",
    )(left_head)

    fresh, peaks, steps = [], None, []
    for chunk, (start, stop) in enumerate(chunks):
        kept = () if peaks is None else (peaks,)
        after = (token,) if chunk == 1 else ()
        some, peaks = call(
            lambda *refs: update_kernel(start, *refs),
            "update",
            [shape((2, depth, stop - start), F32), shape((8, LANES), F32)],
            arrived[chunk],
            master,
            moment,
            second,
            *kept,
            *after,
            read=4 + len(kept),
            scratch=[pltpu.VMEM((2, LANES, LANES), F32)],
            flops=40 * depth * (stop - start),
        )
        fresh.append(some)
        steps.append(peaks)

    left_tail = turned(leaving(head, tokens - head, steps[-2]), "pipe")

    group = LANES // depth
    for level in range(group.bit_length() - 1):
        peaks = jnp.maximum(peaks, exchange(peaks, "expert", 1 << level))
    peak_rows = [peaks] + [exchange(peaks, "expert", k * group) for k in range(1, experts // group)]
    coded, token = call(
        code_kernel,
        "codes",
        [shape((2, 1, depth, width), BF16), shape((8, LANES), F32)],
        peaks,
        *fresh,
        read=1 + len(fresh),
        flops=4 * depth * width,
    )
    left, scales = pl.pallas_call(
        lambda *refs: finish_kernel(head, group, *refs),
        in_specs=[ANY] * 3 + [VMEM] * len(peak_rows),
        out_specs=[ANY, VMEM],
        out_shape=[shape((1, tokens, width), BF16), shape((2, 1, experts // group, blocks), F32)],
        scratch_shapes=[pltpu.SemaphoreType.DMA],
        input_output_aliases={1: 0},
        compiler_params=ROOM,
        cost_estimate=pl.CostEstimate(flops=0, bytes_accessed=4 * (tokens - head) * width, transcendentals=0),
        name="finish",
    )(left_tail, placed, token, *peak_rows)
    return (left, coded, scales)


def solution(mesh):
    in_specs = (
        P("pipe", "expert", "dp"),
        P("pipe", "expert", "dp"),
        P("pipe", "expert", "dp"),
        P(None, "pipe", "dp"),
        P(None, "pipe", None, "dp"),
        P(None, "pipe", None, "dp"),
        P(None, "pipe", "expert", "dp"),
        P(None, "pipe", "expert", "dp"),
        P(None, "pipe", "expert", "dp"),
    )
    out_specs = (
        P("pipe", "expert", "dp"),
        P(None, "pipe", "expert", "dp"),
        P(None, "pipe", None, "dp"),
    )
    return jax.shard_map(shards, mesh=mesh, in_specs=in_specs, out_specs=out_specs, check_vma=False)
```

```python
import jax
import jax.numpy as jnp
from jax import lax
from jax.experimental import pallas as pl
from jax.experimental.pallas import tpu as pltpu
from jax.sharding import PartitionSpec as P

D = 7168
LANES = 128
F32 = jnp.float32
BF16 = jnp.bfloat16
BOTH_LAST = (((1,), (1,)), ((), ()))
ROOM = pltpu.CompilerParams(vmem_limit_bytes=16 << 20)
ANY = pl.BlockSpec(memory_space=pl.ANY)
VMEM = pl.BlockSpec(memory_space=pltpu.VMEM)


def exchange(block, axis, offset):
    count = lax.axis_size(axis)
    return lax.ppermute(block, axis, [(i, i ^ offset) for i in range(count)])


def mirrored(block, axis):
    count = lax.axis_size(axis)
    return lax.ppermute(block, axis, [(i, count - 1 - i) for i in range(count)])


def turned(block, axis):
    count = lax.axis_size(axis)
    return lax.ppermute(block, axis, [(i, (i + 1) % count) for i in range(count)])


def shifted(block, axis):
    count = lax.axis_size(axis)
    return lax.ppermute(block, axis, [(i, i + 1) for i in range(count - 1)])


def halves_of_sum(block, axis):
    count = lax.axis_size(axis)
    offset = 1
    while True:
        other = exchange(block, axis, offset)
        offset *= 2
        if offset >= count:
            return block, other
        block = block + other


def shape(dims, dtype):
    return jax.ShapeDtypeStruct(dims, dtype)


def call(kernel, name, outs, *operands, read, scratch=(), flops=0):
    many = isinstance(outs, list)
    nbytes = sum(o.size * o.dtype.itemsize for o in operands[:read])
    return pl.pallas_call(
        kernel,
        in_specs=[VMEM] * read + [ANY] * (len(operands) - read),
        out_specs=[VMEM] * len(outs) if many else VMEM,
        out_shape=outs,
        scratch_shapes=list(scratch),
        compiler_params=ROOM,
        cost_estimate=pl.CostEstimate(flops=flops, bytes_accessed=nbytes, transcendentals=0),
        name=name,
    )(*operands)


def folded_squares(rows):
    tokens, width = rows.shape
    total = jnp.zeros((tokens, LANES), F32)
    for at in range(0, width, LANES):
        part = rows[:, at : at + LANES]
        total = total + part * part
    return total


def latent_kernel(tiles, x1, x2, c2, down, up, gain, out_ref, vx1, scaled2, vc2, va1, vx2, va2, vb2, vgain, sems):
    tokens, width = vx1.shape
    latent = va1.shape[0]
    tile = width // tiles
    groups = (
        ((x1.at[0], vx1), (down.at[0, 0], va1)),
        ((x2.at[0], vx2), (down.at[1, 0], va2)),
        ((c2.at[0], vc2), (up.at[1, 0], vb2)),
    )

    def copies(job, at):
        cols = pl.ds(at * tile, tile)
        return [
            pltpu.make_async_copy(src.at[:, cols], dst.at[:, cols], sems.at[job, k, at])
            for k, (src, dst) in enumerate(groups[job])
        ]

    whole_gain = pltpu.make_async_copy(gain, vgain, sems.at[len(groups), 0, 0])
    whole_gain.start()
    for job in range(len(groups)):
        for at in range(tiles):
            for copy in copies(job, at):
                copy.start()
    base = 2 * latent + tokens
    out_ref[...] = jnp.zeros_like(out_ref)
    whole_gain.wait()

    def step(job, at):
        for copy in copies(job, at):
            copy.wait()
        cols = pl.ds(pl.multiple_of(at * tile, LANES), tile)
        if job < 2:
            rows = (vx1, vx2)[job][:, cols].astype(F32)
            right = (rows * vgain[job : job + 1, cols].astype(F32)).astype(BF16)
            squares = folded_squares(rows)
        if job == 0:
            raw = lax.dot_general(right, va1[:, cols], BOTH_LAST, preferred_element_type=F32)
            for piece in range(latent // LANES):
                out_ref[base + piece * tokens : base + (piece + 1) * tokens] += raw[:, piece * LANES : (piece + 1) * LANES]
            out_ref[base + (latent // LANES) * tokens :] += squares
        elif job == 1:
            scaled2[:, cols] = right
            out_ref[:latent] += lax.dot_general(va2[:, cols], right, BOTH_LAST, preferred_element_type=F32)
            out_ref[2 * latent : base] += squares
        else:
            out_ref[latent : 2 * latent] += lax.dot_general(
                vb2[:, cols], vc2[:, cols], BOTH_LAST, preferred_element_type=F32
            )

    for job in range(len(groups)):
        lax.fori_loop(0, tiles, lambda at, _, job=job: step(job, at) or 0, 0)


def fetch_kernel(in_ref, *rest):
    out_ref, sems = rest[-2:]
    step = out_ref.shape[0] // sems.shape[0]
    copies = []
    for k in range(sems.shape[0]):
        rows = pl.ds(k * step, step)
        copies.append(pltpu.make_async_copy(in_ref.at[0, 0, rows], out_ref.at[rows], sems.at[k]))
    for copy in copies:
        copy.start()
    for copy in copies:
        copy.wait()


def leaving_kernel(start, own_ref, other_ref, x_ref, b_ref, *rest):
    out_ref = rest[-1]
    latent = b_ref.shape[0]
    count, width = out_ref.shape
    tokens = x_ref.shape[0]

    def summed(at):
        rows = slice(at + start, at + start + count)
        return own_ref[rows] + other_ref[rows]

    base = own_ref.shape[0] - tokens
    rscale = lax.rsqrt(jnp.sum(summed(base), axis=1, keepdims=True) / D + 1e-06)
    base -= (latent // LANES) * tokens
    hidden = jnp.concatenate([summed(base + at * tokens) * rscale for at in range(latent // LANES)], axis=1).astype(BF16)
    last = lax.axis_index("pipe") == lax.axis_size("pipe") - 1
    step = width // (4 if width % (4 * LANES) == 0 else 2)
    for at in range(0, width, step):
        cols = slice(at, at + step)
        rows = x_ref[start : start + count, cols].astype(F32)
        rows += jnp.dot(hidden, b_ref[:, cols], preferred_element_type=F32)
        out_ref[:, cols] = jnp.where(last, 0.0, rows).astype(BF16)


def grad_kernel(experts, start, own_ref, other_ref, x_ref, c_ref, *rest):
    outs, rows_ref = rest[-1 - experts : -1], rest[-1]
    latent = rows_ref.shape[1]
    depth = latent // experts
    cols = slice(start, start + outs[0].shape[2])
    me = lax.axis_index("expert")
    squares = own_ref[2 * latent : 2 * latent + LANES] + other_ref[2 * latent : 2 * latent + LANES]
    rscale = lax.rsqrt(jnp.sum(squares.T, axis=0, keepdims=True) / D + 1e-06)
    rows_ref[0] = (own_ref[latent : 2 * latent] + other_ref[latent : 2 * latent]) * rscale
    rows_ref[1] = (own_ref[:latent] + other_ref[:latent]) * rscale
    for side, right in enumerate((x_ref[:, cols], c_ref[:, cols])):
        left = jnp.concatenate(
            [rows_ref[side, pl.ds(pl.multiple_of((me ^ k) * depth, depth), depth), :] for k in range(experts)]
        )
        both = jnp.dot(left.astype(BF16), right, preferred_element_type=F32).astype(BF16)
        for k in range(experts):
            outs[k][side] = both[k * depth : (k + 1) * depth]


def share_kernel(experts, *refs):
    total = refs[0][...].astype(F32)
    for ref in refs[1:experts]:
        total = total + ref[...].astype(F32)
    refs[-1][...] = total.astype(BF16)


def update_kernel(start, share_ref, master_ref, moment_ref, second_ref, *rest):
    fresh_ref, peak_ref, wide = rest[-3:]
    cols = slice(start, start + share_ref.shape[2])
    grad = share_ref[...].astype(F32)
    first = 0.9 * moment_ref[:, 0, :, cols].astype(F32) + 0.1 * grad
    secnd = 0.95 * second_ref[:, 0, :, cols].astype(F32) + 0.05 * grad * grad
    update = first / (1.0 - 0.9**10) / (jnp.sqrt(secnd / (1.0 - 0.95**10)) + 1e-08)
    weights = master_ref[:, 0, :, cols]
    fresh = weights - 0.01 * (update + 0.1 * weights)
    fresh_ref[...] = fresh
    peak_ref[...] = jnp.zeros_like(peak_ref) if start == 0 else rest[0][...]
    wide[...] = jnp.zeros_like(wide)
    for side in range(2):
        peak = jnp.max(jnp.abs(fresh[side]), axis=0, keepdims=True)
        for at in range(0, peak.shape[1], LANES):
            block = (start + at) // LANES
            wide[side, block : block + 1, :] = peak[:, at : at + LANES]
        peak_ref[side : side + 1, :] = jnp.maximum(
            peak_ref[side : side + 1, :], jnp.max(wide[side].T, axis=0, keepdims=True)
        )


def code_kernel(peak_ref, *refs):
    fresh_refs, (code_ref, token_ref) = refs[:-2], refs[-2:]
    token_ref[...] = jnp.zeros_like(token_ref)
    column = (1.0 / (peak_ref[...] + 1e-06)).T
    for side in range(2):
        inverse = jnp.broadcast_to(column[:, side : side + 1], (LANES, LANES))
        block = 0
        for ref in fresh_refs:
            for at in range(0, ref.shape[2], LANES):
                code_ref[side, 0, :, block * LANES : (block + 1) * LANES] = (
                    ref[side, :, at : at + LANES] * inverse[block : block + 1]
                ).astype(BF16)
                block += 1


def finish_kernel(start, group, tail_ref, placed_ref, token_ref, *refs):
    peak_refs, (left_ref, scale_ref, sem) = refs[:-3], refs[-3:]
    copy = pltpu.make_async_copy(tail_ref, left_ref.at[0, pl.ds(start, tail_ref.shape[0])], sem)
    copy.start()
    blocks = scale_ref.shape[3]
    mine = lax.axis_index("expert") // group
    for far, ref in enumerate(peak_refs):
        for side in range(2):
            scale_ref[side, 0, pl.ds(mine ^ far, 1), :] = ref[side : side + 1, :blocks] + 1e-06
    copy.wait()


def place_kernel(*refs):
    in_refs, (out_ref, token_ref, sems) = refs[:-3], refs[-3:]
    copies, start = [], 0
    for k, ref in enumerate(in_refs):
        copies.append(pltpu.make_async_copy(ref, out_ref.at[0, pl.ds(start, ref.shape[0])], sems.at[k]))
        start += ref.shape[0]
    for copy in copies:
        copy.start()
    token_ref[...] = jnp.zeros_like(token_ref)
    for copy in copies:
        copy.wait()


def shards(enter_fwd, enter_rev, cot_rev, gain, proj_down, proj_up, master, moment, second):
    tokens, width = enter_fwd.shape[1:]
    latent = proj_down.shape[2]
    experts = lax.axis_size("expert")
    depth = latent // experts
    blocks = width // LANES
    tiles = 2
    weights = [8, 7, 7, 6]
    edges = [blocks * sum(weights[:k]) // sum(weights) * LANES for k in range(len(weights) + 1)]
    chunks = list(zip(edges[:-1], edges[1:]))

    def streamed(array):
        return pltpu.with_memory_space_constraint(array, pltpu.HBM)

    pack_rows = 2 * latent + tokens + (latent // LANES + 1) * tokens
    held = pltpu.VMEM((tokens, width), BF16)
    packed, rows1, scaled2, cot2 = pl.pallas_call(
        lambda *refs: latent_kernel(tiles, *refs),
        in_specs=[ANY] * 6,
        out_specs=[VMEM] * 4,
        out_shape=[pltpu.VMEM((pack_rows, LANES), F32), held, held, held],
        scratch_shapes=[
            pltpu.VMEM((latent, width), BF16),
            pltpu.VMEM((tokens, width), BF16),
            pltpu.VMEM((latent, width), BF16),
            pltpu.VMEM((latent, width), BF16),
            pltpu.VMEM((2, width), BF16),
            pltpu.SemaphoreType.DMA((4, 2, tiles)),
        ],
        compiler_params=ROOM,
        cost_estimate=pl.CostEstimate(
            flops=6 * tokens * latent * width, bytes_accessed=6 * (tokens + latent) * width, transcendentals=0
        ),
        name="latents",
    )(*(streamed(a) for a in (enter_fwd, enter_rev, cot_rev, proj_down, proj_up, gain.reshape(2, width))))
    own_up = pl.pallas_call(
        fetch_kernel,
        in_specs=[ANY] * 2,
        out_specs=VMEM,
        out_shape=pltpu.VMEM((latent, width), BF16),
        scratch_shapes=[pltpu.SemaphoreType.DMA((4,))],
        compiler_params=ROOM,
        cost_estimate=pl.CostEstimate(flops=0, bytes_accessed=2 * latent * width, transcendentals=0),
        name="fetch",
    )(streamed(proj_up), packed)
    pair = halves_of_sum(packed, "dp")

    def leaving(start, count, *after):
        return call(
            lambda *refs: leaving_kernel(start, *refs),
            "leaving",
            shape((count, width), BF16),
            *pair,
            rows1,
            own_up,
            *after,
            read=4,
            flops=2 * count * latent * width,
        )

    def grads(chunk, *after):
        start, stop = chunks[chunk]
        return call(
            lambda *refs: grad_kernel(experts, start, *refs),
            "grads",
            [shape((2, depth, stop - start), BF16)] * experts,
            *pair,
            scaled2,
            cot2,
            *after,
            read=4,
            scratch=[pltpu.VMEM((2, latent, tokens), F32)],
            flops=4 * tokens * latent * (stop - start),
        )

    pieces_of = (48, 64, 16)
    head = pieces_of[0] + pieces_of[1]
    first_rows = leaving(0, pieces_of[0])
    left_first = turned(first_rows, "pipe")
    first = grads(0, first_rows)
    left_second = shifted(leaving(pieces_of[0], pieces_of[1], first[0]), "pipe")
    shares, arrived, others = [], [], []
    for chunk in range(len(chunks)):
        own, *pieces = grads(chunk, *shares[-2:-1], *others[-1][:2], *([left_first] if chunk == 1 else [])) if chunk else first
        others.append([exchange(piece, "expert", 1 + k) for k, piece in enumerate(pieces)])
        after = [left_second] if chunk == 1 else arrived[chunk - 2 : chunk - 1] if chunk > 1 else []
        shares.append(
            call(
                lambda *refs: share_kernel(experts, *refs),
                "share",
                shape(own.shape, BF16),
                own,
                *others[-1],
                *after,
                read=experts,
            )
        )
        arrived.append(mirrored(shares[-1], "pipe"))

    placed, token = pl.pallas_call(
        place_kernel,
        in_specs=[ANY] * 2,
        out_specs=[ANY, VMEM],
        out_shape=[shape((1, tokens, width), BF16), shape((8, LANES), F32)],
        scratch_shapes=[pltpu.SemaphoreType.DMA((2,))],
        compiler_params=ROOM,
        cost_estimate=pl.CostEstimate(flops=0, bytes_accessed=4 * head * width, transcendentals=0),
        name="place",
    )(left_first, left_second)

    fresh, peaks, steps = [], None, []
    for chunk, (start, stop) in enumerate(chunks):
        kept = () if peaks is None else (peaks,)
        after = (token,) if chunk == 1 else ()
        some, peaks = call(
            lambda *refs: update_kernel(start, *refs),
            "update",
            [shape((2, depth, stop - start), F32), shape((8, LANES), F32)],
            arrived[chunk],
            master,
            moment,
            second,
            *kept,
            *after,
            read=4 + len(kept),
            scratch=[pltpu.VMEM((2, LANES, LANES), F32)],
            flops=40 * depth * (stop - start),
        )
        fresh.append(some)
        steps.append(peaks)

    left_tail = turned(leaving(head, tokens - head, steps[-2]), "pipe")

    group = LANES // depth
    for level in range(group.bit_length() - 1):
        peaks = jnp.maximum(peaks, exchange(peaks, "expert", 1 << level))
    peak_rows = [peaks] + [exchange(peaks, "expert", k * group) for k in range(1, experts // group)]
    coded, token = call(
        code_kernel,
        "codes",
        [shape((2, 1, depth, width), BF16), shape((8, LANES), F32)],
        peaks,
        *fresh,
        read=1 + len(fresh),
        flops=4 * depth * width,
    )
    left, scales = pl.pallas_call(
        lambda *refs: finish_kernel(head, group, *refs),
        in_specs=[ANY] * 3 + [VMEM] * len(peak_rows),
        out_specs=[ANY, VMEM],
        out_shape=[shape((1, tokens, width), BF16), shape((2, 1, experts // group, blocks), F32)],
        scratch_shapes=[pltpu.SemaphoreType.DMA],
        input_output_aliases={1: 0},
        compiler_params=ROOM,
        cost_estimate=pl.CostEstimate(flops=0, bytes_accessed=4 * (tokens - head) * width, transcendentals=0),
        name="finish",
    )(left_tail, placed, token, *peak_rows)
    return (left, coded, scales)


def solution(mesh):
    in_specs = (
        P("pipe", "expert", "dp"),
        P("pipe", "expert", "dp"),
        P("pipe", "expert", "dp"),
        P(None, "pipe", "dp"),
        P(None, "pipe", None, "dp"),
        P(None, "pipe", None, "dp"),
        P(None, "pipe", "expert", "dp"),
        P(None, "pipe", "expert", "dp"),
        P(None, "pipe", "expert", "dp"),
    )
    out_specs = (
        P("pipe", "expert", "dp"),
        P(None, "pipe", "expert", "dp"),
        P(None, "pipe", None, "dp"),
    )
    return jax.shard_map(shards, mesh=mesh, in_specs=in_specs, out_specs=out_specs, check_vma=False)
```

```python
import jax
import jax.numpy as jnp
from jax import lax
from jax.experimental import pallas as pl
from jax.experimental.pallas import tpu as pltpu
from jax.sharding import PartitionSpec as P

D = 7168
LANES = 128
F32 = jnp.float32
BF16 = jnp.bfloat16
BOTH_LAST = (((1,), (1,)), ((), ()))
ROOM = pltpu.CompilerParams(vmem_limit_bytes=16 << 20)
ANY = pl.BlockSpec(memory_space=pl.ANY)
VMEM = pl.BlockSpec(memory_space=pltpu.VMEM)


def exchange(block, axis, offset):
    count = lax.axis_size(axis)
    return lax.ppermute(block, axis, [(i, i ^ offset) for i in range(count)])


def mirrored(block, axis):
    count = lax.axis_size(axis)
    return lax.ppermute(block, axis, [(i, count - 1 - i) for i in range(count)])


def turned(block, axis):
    count = lax.axis_size(axis)
    return lax.ppermute(block, axis, [(i, (i + 1) % count) for i in range(count)])


def shifted(block, axis):
    count = lax.axis_size(axis)
    return lax.ppermute(block, axis, [(i, i + 1) for i in range(count - 1)])


def halves_of_sum(block, axis):
    count = lax.axis_size(axis)
    offset = 1
    while True:
        other = exchange(block, axis, offset)
        offset *= 2
        if offset >= count:
            return block, other
        block = block + other


def shape(dims, dtype):
    return jax.ShapeDtypeStruct(dims, dtype)


def call(kernel, name, outs, *operands, read, scratch=(), flops=0):
    many = isinstance(outs, list)
    nbytes = sum(o.size * o.dtype.itemsize for o in operands[:read])
    return pl.pallas_call(
        kernel,
        in_specs=[VMEM] * read + [ANY] * (len(operands) - read),
        out_specs=[VMEM] * len(outs) if many else VMEM,
        out_shape=outs,
        scratch_shapes=list(scratch),
        compiler_params=ROOM,
        cost_estimate=pl.CostEstimate(flops=flops, bytes_accessed=nbytes, transcendentals=0),
        name=name,
    )(*operands)


def folded_squares(rows):
    tokens, width = rows.shape
    total = jnp.zeros((tokens, LANES), F32)
    for at in range(0, width, LANES):
        part = rows[:, at : at + LANES]
        total = total + part * part
    return total


def latent_kernel(tiles, x1, x2, c2, down, up, gain, out_ref, vx1, scaled2, vc2, va1, vx2, va2, vb2, vgain, sems):
    tokens, width = vx1.shape
    latent = va1.shape[0]
    tile = width // tiles
    groups = (
        ((x1.at[0], vx1), (down.at[0, 0], va1)),
        ((x2.at[0], vx2), (down.at[1, 0], va2)),
        ((c2.at[0], vc2), (up.at[1, 0], vb2)),
    )

    def copies(job, at):
        cols = pl.ds(at * tile, tile)
        return [
            pltpu.make_async_copy(src.at[:, cols], dst.at[:, cols], sems.at[job, k, at])
            for k, (src, dst) in enumerate(groups[job])
        ]

    whole_gain = pltpu.make_async_copy(gain, vgain, sems.at[len(groups), 0, 0])
    whole_gain.start()
    for job in range(len(groups)):
        for at in range(tiles):
            for copy in copies(job, at):
                copy.start()
    base = 2 * latent + tokens
    out_ref[...] = jnp.zeros_like(out_ref)
    whole_gain.wait()

    def step(job, at):
        for copy in copies(job, at):
            copy.wait()
        cols = pl.ds(pl.multiple_of(at * tile, LANES), tile)
        if job < 2:
            rows = (vx1, vx2)[job][:, cols].astype(F32)
            right = (rows * vgain[job : job + 1, cols].astype(F32)).astype(BF16)
            squares = folded_squares(rows)
        if job == 0:
            raw = lax.dot_general(right, va1[:, cols], BOTH_LAST, preferred_element_type=F32)
            for piece in range(latent // LANES):
                out_ref[base + piece * tokens : base + (piece + 1) * tokens] += raw[:, piece * LANES : (piece + 1) * LANES]
            out_ref[base + (latent // LANES) * tokens :] += squares
        elif job == 1:
            scaled2[:, cols] = right
            out_ref[:latent] += lax.dot_general(va2[:, cols], right, BOTH_LAST, preferred_element_type=F32)
            out_ref[2 * latent : base] += squares
        else:
            out_ref[latent : 2 * latent] += lax.dot_general(
                vb2[:, cols], vc2[:, cols], BOTH_LAST, preferred_element_type=F32
            )

    for job in range(len(groups)):
        lax.fori_loop(0, tiles, lambda at, _, job=job: step(job, at) or 0, 0)


def fetch_kernel(in_ref, *rest):
    out_ref, sem = rest[-2:]
    copy = pltpu.make_async_copy(in_ref.at[0, 0], out_ref, sem)
    copy.start()
    copy.wait()


def leaving_kernel(start, own_ref, other_ref, x_ref, b_ref, *rest):
    out_ref = rest[-1]
    latent = b_ref.shape[0]
    count, width = out_ref.shape
    tokens = x_ref.shape[0]

    def summed(at):
        rows = slice(at + start, at + start + count)
        return own_ref[rows] + other_ref[rows]

    base = own_ref.shape[0] - tokens
    rscale = lax.rsqrt(jnp.sum(summed(base), axis=1, keepdims=True) / D + 1e-06)
    base -= (latent // LANES) * tokens
    hidden = jnp.concatenate([summed(base + at * tokens) * rscale for at in range(latent // LANES)], axis=1).astype(BF16)
    last = lax.axis_index("pipe") == lax.axis_size("pipe") - 1
    step = width // (4 if width % (4 * LANES) == 0 else 2)
    for at in range(0, width, step):
        cols = slice(at, at + step)
        rows = x_ref[start : start + count, cols].astype(F32)
        rows += jnp.dot(hidden, b_ref[:, cols], preferred_element_type=F32)
        out_ref[:, cols] = jnp.where(last, 0.0, rows).astype(BF16)


def grad_kernel(experts, start, own_ref, other_ref, x_ref, c_ref, *rest):
    outs, rows_ref = rest[-1 - experts : -1], rest[-1]
    latent = rows_ref.shape[1]
    depth = latent // experts
    cols = slice(start, start + outs[0].shape[2])
    me = lax.axis_index("expert")
    squares = own_ref[2 * latent : 2 * latent + LANES] + other_ref[2 * latent : 2 * latent + LANES]
    rscale = lax.rsqrt(jnp.sum(squares.T, axis=0, keepdims=True) / D + 1e-06)
    rows_ref[0] = (own_ref[latent : 2 * latent] + other_ref[latent : 2 * latent]) * rscale
    rows_ref[1] = (own_ref[:latent] + other_ref[:latent]) * rscale
    for side, right in enumerate((x_ref[:, cols], c_ref[:, cols])):
        left = jnp.concatenate(
            [rows_ref[side, pl.ds(pl.multiple_of((me ^ k) * depth, depth), depth), :] for k in range(experts)]
        )
        both = jnp.dot(left.astype(BF16), right, preferred_element_type=F32).astype(BF16)
        for k in range(experts):
            outs[k][side] = both[k * depth : (k + 1) * depth]


def share_kernel(experts, *refs):
    total = refs[0][...].astype(F32)
    for ref in refs[1:experts]:
        total = total + ref[...].astype(F32)
    refs[-1][...] = total.astype(BF16)


def update_kernel(start, share_ref, master_ref, moment_ref, second_ref, *rest):
    fresh_ref, peak_ref, wide = rest[-3:]
    cols = slice(start, start + share_ref.shape[2])
    grad = share_ref[...].astype(F32)
    first = 0.9 * moment_ref[:, 0, :, cols].astype(F32) + 0.1 * grad
    secnd = 0.95 * second_ref[:, 0, :, cols].astype(F32) + 0.05 * grad * grad
    update = first / (1.0 - 0.9**10) / (jnp.sqrt(secnd / (1.0 - 0.95**10)) + 1e-08)
    weights = master_ref[:, 0, :, cols]
    fresh = weights - 0.01 * (update + 0.1 * weights)
    fresh_ref[...] = fresh
    peak_ref[...] = jnp.zeros_like(peak_ref) if start == 0 else rest[0][...]
    wide[...] = jnp.zeros_like(wide)
    for side in range(2):
        peak = jnp.max(jnp.abs(fresh[side]), axis=0, keepdims=True)
        for at in range(0, peak.shape[1], LANES):
            block = (start + at) // LANES
            wide[side, block : block + 1, :] = peak[:, at : at + LANES]
        peak_ref[side : side + 1, :] = jnp.maximum(
            peak_ref[side : side + 1, :], jnp.max(wide[side].T, axis=0, keepdims=True)
        )


def merged(refs):
    top = refs[0][...]
    for ref in refs[1:]:
        top = jnp.maximum(top, ref[...])
    return top + 1e-06


def code_kernel(group, *refs):
    peak_refs, fresh_refs, (code_ref, token_ref) = refs[:group], refs[group:-2], refs[-2:]
    token_ref[...] = jnp.zeros_like(token_ref)
    column = (1.0 / merged(peak_refs)).T
    for side in range(2):
        inverse = jnp.broadcast_to(column[:, side : side + 1], (LANES, LANES))
        block = 0
        for ref in fresh_refs:
            for at in range(0, ref.shape[2], LANES):
                code_ref[side, 0, :, block * LANES : (block + 1) * LANES] = (
                    ref[side, :, at : at + LANES] * inverse[block : block + 1]
                ).astype(BF16)
                block += 1


def scale_kernel(group, experts, *refs):
    peak_refs, scale_ref = refs[:experts], refs[-1]
    blocks = scale_ref.shape[3]
    mine = lax.axis_index("expert") // group
    for far in range(len(peak_refs) // group):
        top = merged(peak_refs[far * group : (far + 1) * group])
        for side in range(2):
            scale_ref[side, 0, pl.ds(mine ^ far, 1), :] = top[side : side + 1, :blocks]


def place_kernel(start, in_ref, *rest):
    out_ref, token_ref, sem = rest[-3:]
    copy = pltpu.make_async_copy(in_ref, out_ref.at[0, pl.ds(start, in_ref.shape[0])], sem)
    copy.start()
    token_ref[...] = jnp.zeros_like(token_ref)
    copy.wait()


def shards(enter_fwd, enter_rev, cot_rev, gain, proj_down, proj_up, master, moment, second):
    tokens, width = enter_fwd.shape[1:]
    latent = proj_down.shape[2]
    experts = lax.axis_size("expert")
    depth = latent // experts
    blocks = width // LANES
    tiles = 2
    weights = [8, 7, 7, 6]
    edges = [blocks * sum(weights[:k]) // sum(weights) * LANES for k in range(len(weights) + 1)]
    chunks = list(zip(edges[:-1], edges[1:]))

    def streamed(array):
        return pltpu.with_memory_space_constraint(array, pltpu.HBM)

    pack_rows = 2 * latent + tokens + (latent // LANES + 1) * tokens
    held = pltpu.VMEM((tokens, width), BF16)
    packed, rows1, scaled2, cot2 = pl.pallas_call(
        lambda *refs: latent_kernel(tiles, *refs),
        in_specs=[ANY] * 6,
        out_specs=[VMEM] * 4,
        out_shape=[pltpu.VMEM((pack_rows, LANES), F32), held, held, held],
        scratch_shapes=[
            pltpu.VMEM((latent, width), BF16),
            pltpu.VMEM((tokens, width), BF16),
            pltpu.VMEM((latent, width), BF16),
            pltpu.VMEM((latent, width), BF16),
            pltpu.VMEM((2, width), BF16),
            pltpu.SemaphoreType.DMA((4, 2, tiles)),
        ],
        compiler_params=ROOM,
        cost_estimate=pl.CostEstimate(
            flops=6 * tokens * latent * width, bytes_accessed=6 * (tokens + latent) * width, transcendentals=0
        ),
        name="latents",
    )(*(streamed(a) for a in (enter_fwd, enter_rev, cot_rev, proj_down, proj_up, gain.reshape(2, width))))
    own_up = pl.pallas_call(
        fetch_kernel,
        in_specs=[ANY] * 2,
        out_specs=VMEM,
        out_shape=pltpu.VMEM((latent, width), BF16),
        scratch_shapes=[pltpu.SemaphoreType.DMA],
        compiler_params=ROOM,
        cost_estimate=pl.CostEstimate(flops=0, bytes_accessed=2 * latent * width, transcendentals=0),
        name="fetch",
    )(streamed(proj_up), packed)
    pair = halves_of_sum(packed, "dp")

    def leaving(start, count, *after):
        return call(
            lambda *refs: leaving_kernel(start, *refs),
            "leaving",
            shape((count, width), BF16),
            *pair,
            rows1,
            own_up,
            *after,
            read=4,
            flops=2 * count * latent * width,
        )

    def grads(chunk, *after):
        start, stop = chunks[chunk]
        return call(
            lambda *refs: grad_kernel(experts, start, *refs),
            "grads",
            [shape((2, depth, stop - start), BF16)] * experts,
            *pair,
            scaled2,
            cot2,
            *after,
            read=4,
            scratch=[pltpu.VMEM((2, latent, tokens), F32)],
            flops=4 * tokens * latent * (stop - start),
        )

    head = 112
    first_rows = leaving(0, head)
    left_head = turned(first_rows, "pipe")
    first = grads(0, first_rows)
    shares, arrived, others = [], [], []
    for chunk in range(len(chunks)):
        own, *pieces = grads(chunk, *shares[-2:-1], *others[-1][:1]) if chunk else first
        others.append([exchange(piece, "expert", 1 + k) for k, piece in enumerate(pieces)])
        after = [left_head] if chunk == 1 else arrived[chunk - 2 : chunk - 1] if chunk > 1 else []
        shares.append(
            call(
                lambda *refs: share_kernel(experts, *refs),
                "share",
                shape(own.shape, BF16),
                own,
                *others[-1],
                *after,
                read=experts,
            )
        )
        arrived.append(mirrored(shares[-1], "pipe"))

    def place(start, rows, kept=(), after=()):
        return pl.pallas_call(
            lambda *refs: place_kernel(start, *refs),
            in_specs=[ANY] * (1 + len(kept) + len(after)),
            out_specs=[ANY, VMEM],
            out_shape=[shape((1, tokens, width), BF16), shape((8, LANES), F32)],
            scratch_shapes=[pltpu.SemaphoreType.DMA],
            input_output_aliases={1 + k: k for k in range(len(kept))},
            compiler_params=ROOM,
            cost_estimate=pl.CostEstimate(flops=0, bytes_accessed=4 * rows.shape[0] * width, transcendentals=0),
            name="place",
        )(rows, *kept, *after)

    placed, token = place(0, left_head)

    fresh, peaks, steps = [], None, []
    for chunk, (start, stop) in enumerate(chunks):
        kept = () if peaks is None else (peaks,)
        after = (token,) if chunk == 1 else ()
        some, peaks = call(
            lambda *refs: update_kernel(start, *refs),
            "update",
            [shape((2, depth, stop - start), F32), shape((8, LANES), F32)],
            arrived[chunk],
            master,
            moment,
            second,
            *kept,
            *after,
            read=4 + len(kept),
            scratch=[pltpu.VMEM((2, LANES, LANES), F32)],
            flops=40 * depth * (stop - start),
        )
        fresh.append(some)
        steps.append(peaks)

    left_tail = shifted(leaving(head, tokens - head, steps[-2]), "pipe")

    group = LANES // depth
    peak_rows = [peaks] + [exchange(peaks, "expert", k) for k in range(1, experts)]
    coded, token = call(
        lambda *refs: code_kernel(group, *refs),
        "codes",
        [shape((2, 1, depth, width), BF16), shape((8, LANES), F32)],
        *peak_rows[:group],
        *fresh,
        read=group + len(fresh),
        flops=4 * depth * width,
    )
    scales = call(
        lambda *refs: scale_kernel(group, experts, *refs),
        "scales",
        shape((2, 1, experts // group, blocks), F32),
        *peak_rows,
        token,
        read=experts,
    )
    left, _ = place(head, left_tail, (placed,), (token,))
    return (left, coded, scales)


def solution(mesh):
    in_specs = (
        P("pipe", "expert", "dp"),
        P("pipe", "expert", "dp"),
        P("pipe", "expert", "dp"),
        P(None, "pipe", "dp"),
        P(None, "pipe", None, "dp"),
        P(None, "pipe", None, "dp"),
        P(None, "pipe", "expert", "dp"),
        P(None, "pipe", "expert", "dp"),
        P(None, "pipe", "expert", "dp"),
    )
    out_specs = (
        P("pipe", "expert", "dp"),
        P(None, "pipe", "expert", "dp"),
        P(None, "pipe", None, "dp"),
    )
    return jax.shard_map(shards, mesh=mesh, in_specs=in_specs, out_specs=out_specs, check_vma=False)
```

```python
import jax
import jax.numpy as jnp
from jax import lax
from jax.experimental import pallas as pl
from jax.experimental.pallas import tpu as pltpu
from jax.sharding import PartitionSpec as P

D = 7168
LANES = 128
F32 = jnp.float32
BF16 = jnp.bfloat16
BOTH_LAST = (((1,), (1,)), ((), ()))
ROOM = pltpu.CompilerParams(vmem_limit_bytes=16 << 20)
ANY = pl.BlockSpec(memory_space=pl.ANY)
VMEM = pl.BlockSpec(memory_space=pltpu.VMEM)


def exchange(block, axis, offset):
    count = lax.axis_size(axis)
    return lax.ppermute(block, axis, [(i, i ^ offset) for i in range(count)])


def mirrored(block, axis):
    count = lax.axis_size(axis)
    return lax.ppermute(block, axis, [(i, count - 1 - i) for i in range(count)])


def turned(block, axis):
    count = lax.axis_size(axis)
    return lax.ppermute(block, axis, [(i, (i + 1) % count) for i in range(count)])


def shifted(block, axis):
    count = lax.axis_size(axis)
    return lax.ppermute(block, axis, [(i, i + 1) for i in range(count - 1)])


def halves_of_sum(block, axis):
    count = lax.axis_size(axis)
    offset = 1
    while True:
        other = exchange(block, axis, offset)
        offset *= 2
        if offset >= count:
            return block, other
        block = block + other


def shape(dims, dtype):
    return jax.ShapeDtypeStruct(dims, dtype)


def call(kernel, name, outs, *operands, read, scratch=(), flops=0):
    many = isinstance(outs, list)
    nbytes = sum(o.size * o.dtype.itemsize for o in operands[:read])
    return pl.pallas_call(
        kernel,
        in_specs=[VMEM] * read + [ANY] * (len(operands) - read),
        out_specs=[VMEM] * len(outs) if many else VMEM,
        out_shape=outs,
        scratch_shapes=list(scratch),
        compiler_params=ROOM,
        cost_estimate=pl.CostEstimate(flops=flops, bytes_accessed=nbytes, transcendentals=0),
        name=name,
    )(*operands)


def folded_squares(rows):
    tokens, width = rows.shape
    total = jnp.zeros((tokens, LANES), F32)
    for at in range(0, width, LANES):
        part = rows[:, at : at + LANES]
        total = total + part * part
    return total


def latent_kernel(tiles, x1, x2, c2, down, up, gain, out_ref, vx1, scaled2, vc2, va1, vx2, va2, vb2, vgain, sems):
    tokens, width = vx1.shape
    latent = va1.shape[0]
    tile = width // tiles
    groups = (
        ((x1.at[0], vx1), (down.at[0, 0], va1)),
        ((x2.at[0], vx2), (down.at[1, 0], va2)),
        ((c2.at[0], vc2), (up.at[1, 0], vb2)),
    )

    def copies(job, at):
        cols = pl.ds(at * tile, tile)
        return [
            pltpu.make_async_copy(src.at[:, cols], dst.at[:, cols], sems.at[job, k, at])
            for k, (src, dst) in enumerate(groups[job])
        ]

    whole_gain = pltpu.make_async_copy(gain, vgain, sems.at[len(groups), 0, 0])
    whole_gain.start()
    for job in range(len(groups)):
        for at in range(tiles):
            for copy in copies(job, at):
                copy.start()
    base = 2 * latent + tokens
    out_ref[...] = jnp.zeros_like(out_ref)
    whole_gain.wait()

    def step(job, at):
        for copy in copies(job, at):
            copy.wait()
        cols = pl.ds(pl.multiple_of(at * tile, LANES), tile)
        if job < 2:
            rows = (vx1, vx2)[job][:, cols].astype(F32)
            right = (rows * vgain[job : job + 1, cols].astype(F32)).astype(BF16)
            squares = folded_squares(rows)
        if job == 0:
            raw = lax.dot_general(right, va1[:, cols], BOTH_LAST, preferred_element_type=F32)
            for piece in range(latent // LANES):
                out_ref[base + piece * tokens : base + (piece + 1) * tokens] += raw[:, piece * LANES : (piece + 1) * LANES]
            out_ref[base + (latent // LANES) * tokens :] += squares
        elif job == 1:
            scaled2[:, cols] = right
            out_ref[:latent] += lax.dot_general(va2[:, cols], right, BOTH_LAST, preferred_element_type=F32)
            out_ref[2 * latent : base] += squares
        else:
            out_ref[latent : 2 * latent] += lax.dot_general(
                vb2[:, cols], vc2[:, cols], BOTH_LAST, preferred_element_type=F32
            )

    for job in range(len(groups)):
        lax.fori_loop(0, tiles, lambda at, _, job=job: step(job, at) or 0, 0)


def fetch_kernel(in_ref, *rest):
    out_ref, sem = rest[-2:]
    copy = pltpu.make_async_copy(in_ref.at[0, 0], out_ref, sem)
    copy.start()
    copy.wait()


def leaving_kernel(start, own_ref, other_ref, x_ref, b_ref, *rest):
    out_ref = rest[-1]
    latent = b_ref.shape[0]
    count, width = out_ref.shape
    tokens = x_ref.shape[0]

    def summed(at):
        rows = slice(at + start, at + start + count)
        return own_ref[rows] + other_ref[rows]

    base = own_ref.shape[0] - tokens
    rscale = lax.rsqrt(jnp.sum(summed(base), axis=1, keepdims=True) / D + 1e-06)
    base -= (latent // LANES) * tokens
    hidden = jnp.concatenate([summed(base + at * tokens) * rscale for at in range(latent // LANES)], axis=1).astype(BF16)
    last = lax.axis_index("pipe") == lax.axis_size("pipe") - 1
    step = width // (4 if width % (4 * LANES) == 0 else 2)
    for at in range(0, width, step):
        cols = slice(at, at + step)
        rows = x_ref[start : start + count, cols].astype(F32)
        rows += jnp.dot(hidden, b_ref[:, cols], preferred_element_type=F32)
        out_ref[:, cols] = jnp.where(last, 0.0, rows).astype(BF16)


def grad_kernel(experts, start, own_ref, other_ref, x_ref, c_ref, *rest):
    outs, rows_ref = rest[-1 - experts : -1], rest[-1]
    latent = rows_ref.shape[1]
    depth = latent // experts
    cols = slice(start, start + outs[0].shape[2])
    me = lax.axis_index("expert")
    squares = own_ref[2 * latent : 2 * latent + LANES] + other_ref[2 * latent : 2 * latent + LANES]
    rscale = lax.rsqrt(jnp.sum(squares.T, axis=0, keepdims=True) / D + 1e-06)
    rows_ref[0] = (own_ref[latent : 2 * latent] + other_ref[latent : 2 * latent]) * rscale
    rows_ref[1] = (own_ref[:latent] + other_ref[:latent]) * rscale
    for side, right in enumerate((x_ref[:, cols], c_ref[:, cols])):
        left = jnp.concatenate(
            [rows_ref[side, pl.ds(pl.multiple_of((me ^ k) * depth, depth), depth), :] for k in range(experts)]
        )
        both = jnp.dot(left.astype(BF16), right, preferred_element_type=F32).astype(BF16)
        for k in range(experts):
            outs[k][side] = both[k * depth : (k + 1) * depth]


def share_kernel(experts, *refs):
    total = refs[0][...].astype(F32)
    for ref in refs[1:experts]:
        total = total + ref[...].astype(F32)
    refs[-1][...] = total.astype(BF16)


def update_kernel(start, share_ref, master_ref, moment_ref, second_ref, *rest):
    fresh_ref, peak_ref, wide = rest[-3:]
    cols = slice(start, start + share_ref.shape[2])
    grad = share_ref[...].astype(F32)
    first = 0.9 * moment_ref[:, 0, :, cols].astype(F32) + 0.1 * grad
    secnd = 0.95 * second_ref[:, 0, :, cols].astype(F32) + 0.05 * grad * grad
    update = first / (1.0 - 0.9**10) / (jnp.sqrt(secnd / (1.0 - 0.95**10)) + 1e-08)
    weights = master_ref[:, 0, :, cols]
    fresh = weights - 0.01 * (update + 0.1 * weights)
    fresh_ref[...] = fresh
    peak_ref[...] = jnp.zeros_like(peak_ref) if start == 0 else rest[0][...]
    wide[...] = jnp.zeros_like(wide)
    for side in range(2):
        peak = jnp.max(jnp.abs(fresh[side]), axis=0, keepdims=True)
        for at in range(0, peak.shape[1], LANES):
            block = (start + at) // LANES
            wide[side, block : block + 1, :] = peak[:, at : at + LANES]
        peak_ref[side : side + 1, :] = jnp.maximum(
            peak_ref[side : side + 1, :], jnp.max(wide[side].T, axis=0, keepdims=True)
        )


def merged(refs):
    top = refs[0][...]
    for ref in refs[1:]:
        top = jnp.maximum(top, ref[...])
    return top + 1e-06


def code_kernel(group, *refs):
    peak_refs, fresh_refs, (code_ref, token_ref) = refs[:group], refs[group:-2], refs[-2:]
    token_ref[...] = jnp.zeros_like(token_ref)
    column = (1.0 / merged(peak_refs)).T
    for side in range(2):
        inverse = jnp.broadcast_to(column[:, side : side + 1], (LANES, LANES))
        block = 0
        for ref in fresh_refs:
            for at in range(0, ref.shape[2], LANES):
                code_ref[side, 0, :, block * LANES : (block + 1) * LANES] = (
                    ref[side, :, at : at + LANES] * inverse[block : block + 1]
                ).astype(BF16)
                block += 1


def scale_kernel(group, experts, *refs):
    peak_refs, scale_ref = refs[:experts], refs[-1]
    blocks = scale_ref.shape[3]
    mine = lax.axis_index("expert") // group
    for far in range(len(peak_refs) // group):
        top = merged(peak_refs[far * group : (far + 1) * group])
        for side in range(2):
            scale_ref[side, 0, pl.ds(mine ^ far, 1), :] = top[side : side + 1, :blocks]


def place_kernel(start, in_ref, *rest):
    out_ref, token_ref, sem = rest[-3:]
    copy = pltpu.make_async_copy(in_ref, out_ref.at[0, pl.ds(start, in_ref.shape[0])], sem)
    copy.start()
    token_ref[...] = jnp.zeros_like(token_ref)
    copy.wait()


def shards(enter_fwd, enter_rev, cot_rev, gain, proj_down, proj_up, master, moment, second):
    tokens, width = enter_fwd.shape[1:]
    latent = proj_down.shape[2]
    experts = lax.axis_size("expert")
    depth = latent // experts
    blocks = width // LANES
    tiles = 2
    weights = [8, 7, 7, 6]
    edges = [blocks * sum(weights[:k]) // sum(weights) * LANES for k in range(len(weights) + 1)]
    chunks = list(zip(edges[:-1], edges[1:]))

    def streamed(array):
        return pltpu.with_memory_space_constraint(array, pltpu.HBM)

    pack_rows = 2 * latent + tokens + (latent // LANES + 1) * tokens
    held = pltpu.VMEM((tokens, width), BF16)
    packed, rows1, scaled2, cot2 = pl.pallas_call(
        lambda *refs: latent_kernel(tiles, *refs),
        in_specs=[ANY] * 6,
        out_specs=[VMEM] * 4,
        out_shape=[pltpu.VMEM((pack_rows, LANES), F32), held, held, held],
        scratch_shapes=[
            pltpu.VMEM((latent, width), BF16),
            pltpu.VMEM((tokens, width), BF16),
            pltpu.VMEM((latent, width), BF16),
            pltpu.VMEM((latent, width), BF16),
            pltpu.VMEM((2, width), BF16),
            pltpu.SemaphoreType.DMA((4, 2, tiles)),
        ],
        compiler_params=ROOM,
        cost_estimate=pl.CostEstimate(
            flops=6 * tokens * latent * width, bytes_accessed=6 * (tokens + latent) * width, transcendentals=0
        ),
        name="latents",
    )(*(streamed(a) for a in (enter_fwd, enter_rev, cot_rev, proj_down, proj_up, gain.reshape(2, width))))
    own_up = pl.pallas_call(
        fetch_kernel,
        in_specs=[ANY] * 2,
        out_specs=VMEM,
        out_shape=pltpu.VMEM((latent, width), BF16),
        scratch_shapes=[pltpu.SemaphoreType.DMA],
        compiler_params=ROOM,
        cost_estimate=pl.CostEstimate(flops=0, bytes_accessed=2 * latent * width, transcendentals=0),
        name="fetch",
    )(streamed(proj_up), packed)
    pair = halves_of_sum(packed, "dp")

    def leaving(start, count, *after):
        return call(
            lambda *refs: leaving_kernel(start, *refs),
            "leaving",
            shape((count, width), BF16),
            *pair,
            rows1,
            own_up,
            *after,
            read=4,
            flops=2 * count * latent * width,
        )

    def grads(chunk, *after):
        start, stop = chunks[chunk]
        return call(
            lambda *refs: grad_kernel(experts, start, *refs),
            "grads",
            [shape((2, depth, stop - start), BF16)] * experts,
            *pair,
            scaled2,
            cot2,
            *after,
            read=4,
            scratch=[pltpu.VMEM((2, latent, tokens), F32)],
            flops=4 * tokens * latent * (stop - start),
        )

    head = 112
    first_rows = leaving(0, head)
    left_head = turned(first_rows, "pipe")
    first = grads(0, first_rows)
    shares, arrived, others = [], [], []
    for chunk in range(len(chunks)):
        own, *pieces = grads(chunk, *shares[-2:-1], *others[-1][:1]) if chunk else first
        others.append([exchange(piece, "expert", 1 + k) for k, piece in enumerate(pieces)])
        after = [left_head] if chunk == 1 else arrived[chunk - 2 : chunk - 1] if chunk > 1 else []
        shares.append(
            call(
                lambda *refs: share_kernel(experts, *refs),
                "share",
                shape(own.shape, BF16),
                own,
                *others[-1],
                *after,
                read=experts,
            )
        )
        arrived.append(mirrored(shares[-1], "pipe"))

    def place(start, rows, kept=(), after=()):
        return pl.pallas_call(
            lambda *refs: place_kernel(start, *refs),
            in_specs=[ANY] * (1 + len(kept) + len(after)),
            out_specs=[ANY, VMEM],
            out_shape=[shape((1, tokens, width), BF16), shape((8, LANES), F32)],
            scratch_shapes=[pltpu.SemaphoreType.DMA],
            input_output_aliases={1 + k: k for k in range(len(kept))},
            compiler_params=ROOM,
            cost_estimate=pl.CostEstimate(flops=0, bytes_accessed=4 * rows.shape[0] * width, transcendentals=0),
            name="place",
        )(rows, *kept, *after)

    placed, token = place(0, left_head)

    fresh, peaks, steps = [], None, []
    for chunk, (start, stop) in enumerate(chunks):
        kept = () if peaks is None else (peaks,)
        after = (token,) if chunk == 1 else ()
        some, peaks = call(
            lambda *refs: update_kernel(start, *refs),
            "update",
            [shape((2, depth, stop - start), F32), shape((8, LANES), F32)],
            arrived[chunk],
            master,
            moment,
            second,
            *kept,
            *after,
            read=4 + len(kept),
            scratch=[pltpu.VMEM((2, LANES, LANES), F32)],
            flops=40 * depth * (stop - start),
        )
        fresh.append(some)
        steps.append(peaks)

    left_tail = shifted(leaving(head, tokens - head, steps[-3]), "pipe")

    group = LANES // depth
    peak_rows = [peaks] + [exchange(peaks, "expert", k) for k in range(1, experts)]
    coded, token = call(
        lambda *refs: code_kernel(group, *refs),
        "codes",
        [shape((2, 1, depth, width), BF16), shape((8, LANES), F32)],
        *peak_rows[:group],
        *fresh,
        read=group + len(fresh),
        flops=4 * depth * width,
    )
    scales = call(
        lambda *refs: scale_kernel(group, experts, *refs),
        "scales",
        shape((2, 1, experts // group, blocks), F32),
        *peak_rows,
        token,
        read=experts,
    )
    left, _ = place(head, left_tail, (placed,), (token,))
    return (left, coded, scales)


def solution(mesh):
    in_specs = (
        P("pipe", "expert", "dp"),
        P("pipe", "expert", "dp"),
        P("pipe", "expert", "dp"),
        P(None, "pipe", "dp"),
        P(None, "pipe", None, "dp"),
        P(None, "pipe", None, "dp"),
        P(None, "pipe", "expert", "dp"),
        P(None, "pipe", "expert", "dp"),
        P(None, "pipe", "expert", "dp"),
    )
    out_specs = (
        P("pipe", "expert", "dp"),
        P(None, "pipe", "expert", "dp"),
        P(None, "pipe", None, "dp"),
    )
    return jax.shard_map(shards, mesh=mesh, in_specs=in_specs, out_specs=out_specs, check_vma=False)
```

```python
import jax
import jax.numpy as jnp
from jax import lax
from jax.experimental import pallas as pl
from jax.experimental.pallas import tpu as pltpu
from jax.sharding import PartitionSpec as P

D = 7168
LANES = 128
F32 = jnp.float32
BF16 = jnp.bfloat16
BOTH_LAST = (((1,), (1,)), ((), ()))
ROOM = pltpu.CompilerParams(vmem_limit_bytes=16 << 20)
ANY = pl.BlockSpec(memory_space=pl.ANY)
VMEM = pl.BlockSpec(memory_space=pltpu.VMEM)


def exchange(block, axis, offset):
    count = lax.axis_size(axis)
    return lax.ppermute(block, axis, [(i, i ^ offset) for i in range(count)])


def mirrored(block, axis):
    count = lax.axis_size(axis)
    return lax.ppermute(block, axis, [(i, count - 1 - i) for i in range(count)])


def turned(block, axis):
    count = lax.axis_size(axis)
    return lax.ppermute(block, axis, [(i, (i + 1) % count) for i in range(count)])


def shifted(block, axis):
    count = lax.axis_size(axis)
    return lax.ppermute(block, axis, [(i, i + 1) for i in range(count - 1)])


def halves_of_sum(block, axis):
    count = lax.axis_size(axis)
    offset = 1
    while True:
        other = exchange(block, axis, offset)
        offset *= 2
        if offset >= count:
            return block, other
        block = block + other


def shape(dims, dtype):
    return jax.ShapeDtypeStruct(dims, dtype)


def call(kernel, name, outs, *operands, read, scratch=(), flops=0):
    many = isinstance(outs, list)
    nbytes = sum(o.size * o.dtype.itemsize for o in operands[:read])
    return pl.pallas_call(
        kernel,
        in_specs=[VMEM] * read + [ANY] * (len(operands) - read),
        out_specs=[VMEM] * len(outs) if many else VMEM,
        out_shape=outs,
        scratch_shapes=list(scratch),
        compiler_params=ROOM,
        cost_estimate=pl.CostEstimate(flops=flops, bytes_accessed=nbytes, transcendentals=0),
        name=name,
    )(*operands)


def folded_squares(rows):
    tokens, width = rows.shape
    total = jnp.zeros((tokens, LANES), F32)
    for at in range(0, width, LANES):
        part = rows[:, at : at + LANES]
        total = total + part * part
    return total


def latent_kernel(tiles, x1, x2, c2, down, up, gain, out_ref, vx1, scaled2, vc2, va1, vx2, va2, vb2, vgain, sems):
    tokens, width = vx1.shape
    latent = va1.shape[0]
    tile = width // tiles
    groups = (
        ((x1.at[0], vx1), (down.at[0, 0], va1)),
        ((x2.at[0], vx2), (down.at[1, 0], va2)),
        ((c2.at[0], vc2), (up.at[1, 0], vb2)),
    )

    def copies(job, at):
        cols = pl.ds(at * tile, tile)
        return [
            pltpu.make_async_copy(src.at[:, cols], dst.at[:, cols], sems.at[job, k, at])
            for k, (src, dst) in enumerate(groups[job])
        ]

    whole_gain = pltpu.make_async_copy(gain, vgain, sems.at[len(groups), 0, 0])
    whole_gain.start()
    for job in range(len(groups)):
        for at in range(tiles):
            for copy in copies(job, at):
                copy.start()
    base = 2 * latent + tokens
    out_ref[...] = jnp.zeros_like(out_ref)
    whole_gain.wait()

    def step(job, at):
        for copy in copies(job, at):
            copy.wait()
        cols = pl.ds(pl.multiple_of(at * tile, LANES), tile)
        if job < 2:
            rows = (vx1, vx2)[job][:, cols].astype(F32)
            right = (rows * vgain[job : job + 1, cols].astype(F32)).astype(BF16)
            squares = folded_squares(rows)
        if job == 0:
            raw = lax.dot_general(right, va1[:, cols], BOTH_LAST, preferred_element_type=F32)
            for piece in range(latent // LANES):
                out_ref[base + piece * tokens : base + (piece + 1) * tokens] += raw[:, piece * LANES : (piece + 1) * LANES]
            out_ref[base + (latent // LANES) * tokens :] += squares
        elif job == 1:
            scaled2[:, cols] = right
            out_ref[:latent] += lax.dot_general(va2[:, cols], right, BOTH_LAST, preferred_element_type=F32)
            out_ref[2 * latent : base] += squares
        else:
            out_ref[latent : 2 * latent] += lax.dot_general(
                vb2[:, cols], vc2[:, cols], BOTH_LAST, preferred_element_type=F32
            )

    for job in range(len(groups)):
        lax.fori_loop(0, tiles, lambda at, _, job=job: step(job, at) or 0, 0)


def fetch_kernel(in_ref, *rest):
    out_ref, sem = rest[-2:]
    copy = pltpu.make_async_copy(in_ref.at[0, 0], out_ref, sem)
    copy.start()
    copy.wait()


def leaving_kernel(start, own_ref, other_ref, x_ref, b_ref, *rest):
    out_ref = rest[-1]
    latent = b_ref.shape[0]
    count, width = out_ref.shape
    tokens = x_ref.shape[0]

    def summed(at):
        rows = slice(at + start, at + start + count)
        return own_ref[rows] + other_ref[rows]

    base = own_ref.shape[0] - tokens
    rscale = lax.rsqrt(jnp.sum(summed(base), axis=1, keepdims=True) / D + 1e-06)
    base -= (latent // LANES) * tokens
    hidden = jnp.concatenate([summed(base + at * tokens) * rscale for at in range(latent // LANES)], axis=1).astype(BF16)
    last = lax.axis_index("pipe") == lax.axis_size("pipe") - 1
    step = width // (4 if width % (4 * LANES) == 0 else 2)
    for at in range(0, width, step):
        cols = slice(at, at + step)
        rows = x_ref[start : start + count, cols].astype(F32)
        rows += jnp.dot(hidden, b_ref[:, cols], preferred_element_type=F32)
        out_ref[:, cols] = jnp.where(last, 0.0, rows).astype(BF16)


def grad_kernel(experts, start, own_ref, other_ref, x_ref, c_ref, *rest):
    outs, rows_ref = rest[-1 - experts : -1], rest[-1]
    latent = rows_ref.shape[1]
    depth = latent // experts
    cols = slice(start, start + outs[0].shape[2])
    me = lax.axis_index("expert")
    squares = own_ref[2 * latent : 2 * latent + LANES] + other_ref[2 * latent : 2 * latent + LANES]
    rscale = lax.rsqrt(jnp.sum(squares.T, axis=0, keepdims=True) / D + 1e-06)
    rows_ref[0] = (own_ref[latent : 2 * latent] + other_ref[latent : 2 * latent]) * rscale
    rows_ref[1] = (own_ref[:latent] + other_ref[:latent]) * rscale
    for side, right in enumerate((x_ref[:, cols], c_ref[:, cols])):
        left = jnp.concatenate(
            [rows_ref[side, pl.ds(pl.multiple_of((me ^ k) * depth, depth), depth), :] for k in range(experts)]
        )
        both = jnp.dot(left.astype(BF16), right, preferred_element_type=F32).astype(BF16)
        for k in range(experts):
            outs[k][side] = both[k * depth : (k + 1) * depth]


def share_kernel(experts, *refs):
    total = refs[0][...].astype(F32)
    for ref in refs[1:experts]:
        total = total + ref[...].astype(F32)
    refs[-1][...] = total.astype(BF16)


def update_kernel(start, share_ref, master_ref, moment_ref, second_ref, *rest):
    fresh_ref, peak_ref, wide = rest[-3:]
    cols = slice(start, start + share_ref.shape[2])
    grad = share_ref[...].astype(F32)
    first = 0.9 * moment_ref[:, 0, :, cols].astype(F32) + 0.1 * grad
    secnd = 0.95 * second_ref[:, 0, :, cols].astype(F32) + 0.05 * grad * grad
    update = first / (1.0 - 0.9**10) / (jnp.sqrt(secnd / (1.0 - 0.95**10)) + 1e-08)
    weights = master_ref[:, 0, :, cols]
    fresh = weights - 0.01 * (update + 0.1 * weights)
    fresh_ref[...] = fresh
    peak_ref[...] = jnp.zeros_like(peak_ref) if start == 0 else rest[0][...]
    wide[...] = jnp.zeros_like(wide)
    for side in range(2):
        peak = jnp.max(jnp.abs(fresh[side]), axis=0, keepdims=True)
        for at in range(0, peak.shape[1], LANES):
            block = (start + at) // LANES
            wide[side, block : block + 1, :] = peak[:, at : at + LANES]
        peak_ref[side : side + 1, :] = jnp.maximum(
            peak_ref[side : side + 1, :], jnp.max(wide[side].T, axis=0, keepdims=True)
        )


def merged(refs):
    top = refs[0][...]
    for ref in refs[1:]:
        top = jnp.maximum(top, ref[...])
    return top + 1e-06


def code_kernel(group, *refs):
    peak_refs, fresh_refs, (code_ref, token_ref) = refs[:group], refs[group:-2], refs[-2:]
    token_ref[...] = jnp.zeros_like(token_ref)
    column = (1.0 / merged(peak_refs)).T
    for side in range(2):
        inverse = jnp.broadcast_to(column[:, side : side + 1], (LANES, LANES))
        block = 0
        for ref in fresh_refs:
            for at in range(0, ref.shape[2], LANES):
                code_ref[side, 0, :, block * LANES : (block + 1) * LANES] = (
                    ref[side, :, at : at + LANES] * inverse[block : block + 1]
                ).astype(BF16)
                block += 1


def finish_kernel(start, group, count, *refs):
    tail_refs, peak_refs, (left_ref, scale_ref, sems) = refs[:count], refs[count + 2 : -3], refs[-3:]
    copies = []
    for k, ref in enumerate(tail_refs):
        rows = pl.ds(start + k * ref.shape[0], ref.shape[0])
        copies.append(pltpu.make_async_copy(ref, left_ref.at[0, rows], sems.at[k]))
    for copy in copies:
        copy.start()
    blocks = scale_ref.shape[3]
    mine = lax.axis_index("expert") // group
    for far in range(len(peak_refs) // group):
        top = merged(peak_refs[far * group : (far + 1) * group])
        for side in range(2):
            scale_ref[side, 0, pl.ds(mine ^ far, 1), :] = top[side : side + 1, :blocks]
    for copy in copies:
        copy.wait()


def place_kernel(in_ref, out_ref, token_ref, sem):
    copy = pltpu.make_async_copy(in_ref, out_ref.at[0, pl.ds(0, in_ref.shape[0])], sem)
    copy.start()
    token_ref[...] = jnp.zeros_like(token_ref)
    copy.wait()


def shards(enter_fwd, enter_rev, cot_rev, gain, proj_down, proj_up, master, moment, second):
    tokens, width = enter_fwd.shape[1:]
    latent = proj_down.shape[2]
    experts = lax.axis_size("expert")
    depth = latent // experts
    blocks = width // LANES
    tiles = 2
    weights = [8, 7, 7, 6]
    edges = [blocks * sum(weights[:k]) // sum(weights) * LANES for k in range(len(weights) + 1)]
    chunks = list(zip(edges[:-1], edges[1:]))

    def streamed(array):
        return pltpu.with_memory_space_constraint(array, pltpu.HBM)

    pack_rows = 2 * latent + tokens + (latent // LANES + 1) * tokens
    held = pltpu.VMEM((tokens, width), BF16)
    packed, rows1, scaled2, cot2 = pl.pallas_call(
        lambda *refs: latent_kernel(tiles, *refs),
        in_specs=[ANY] * 6,
        out_specs=[VMEM] * 4,
        out_shape=[pltpu.VMEM((pack_rows, LANES), F32), held, held, held],
        scratch_shapes=[
            pltpu.VMEM((latent, width), BF16),
            pltpu.VMEM((tokens, width), BF16),
            pltpu.VMEM((latent, width), BF16),
            pltpu.VMEM((latent, width), BF16),
            pltpu.VMEM((2, width), BF16),
            pltpu.SemaphoreType.DMA((4, 2, tiles)),
        ],
        compiler_params=ROOM,
        cost_estimate=pl.CostEstimate(
            flops=6 * tokens * latent * width, bytes_accessed=6 * (tokens + latent) * width, transcendentals=0
        ),
        name="latents",
    )(*(streamed(a) for a in (enter_fwd, enter_rev, cot_rev, proj_down, proj_up, gain.reshape(2, width))))
    own_up = pl.pallas_call(
        fetch_kernel,
        in_specs=[ANY] * 2,
        out_specs=VMEM,
        out_shape=pltpu.VMEM((latent, width), BF16),
        scratch_shapes=[pltpu.SemaphoreType.DMA],
        compiler_params=ROOM,
        cost_estimate=pl.CostEstimate(flops=0, bytes_accessed=2 * latent * width, transcendentals=0),
        name="fetch",
    )(streamed(proj_up), packed)
    pair = halves_of_sum(packed, "dp")

    def leaving(start, count, *after):
        return call(
            lambda *refs: leaving_kernel(start, *refs),
            "leaving",
            shape((count, width), BF16),
            *pair,
            rows1,
            own_up,
            *after,
            read=4,
            flops=2 * count * latent * width,
        )

    def grads(chunk, *after):
        start, stop = chunks[chunk]
        return call(
            lambda *refs: grad_kernel(experts, start, *refs),
            "grads",
            [shape((2, depth, stop - start), BF16)] * experts,
            *pair,
            scaled2,
            cot2,
            *after,
            read=4,
            scratch=[pltpu.VMEM((2, latent, tokens), F32)],
            flops=4 * tokens * latent * (stop - start),
        )

    head = 96
    first_rows = leaving(0, head)
    left_head = turned(first_rows, "pipe")
    first = grads(0, first_rows)
    shares, arrived, others = [], [], []
    for chunk in range(len(chunks)):
        own, *pieces = grads(chunk, *shares[-2:-1], *others[-1][:1]) if chunk else first
        others.append([exchange(piece, "expert", 1 + k) for k, piece in enumerate(pieces)])
        after = [left_head] if chunk == 1 else arrived[chunk - 2 : chunk - 1] if chunk > 1 else []
        shares.append(
            call(
                lambda *refs: share_kernel(experts, *refs),
                "share",
                shape(own.shape, BF16),
                own,
                *others[-1],
                *shares[-1:],
                *after,
                read=experts,
            )
        )
        arrived.append(mirrored(shares[-1], "pipe"))

    placed, token = pl.pallas_call(
        place_kernel,
        in_specs=[ANY],
        out_specs=[ANY, VMEM],
        out_shape=[shape((1, tokens, width), BF16), shape((8, LANES), F32)],
        scratch_shapes=[pltpu.SemaphoreType.DMA],
        compiler_params=ROOM,
        cost_estimate=pl.CostEstimate(flops=0, bytes_accessed=4 * head * width, transcendentals=0),
        name="place",
    )(left_head)

    fresh, peaks, steps = [], None, []
    for chunk, (start, stop) in enumerate(chunks):
        kept = () if peaks is None else (peaks,)
        after = (token,) if chunk == 1 else ()
        some, peaks = call(
            lambda *refs: update_kernel(start, *refs),
            "update",
            [shape((2, depth, stop - start), F32), shape((8, LANES), F32)],
            arrived[chunk],
            master,
            moment,
            second,
            *kept,
            *after,
            read=4 + len(kept),
            scratch=[pltpu.VMEM((2, LANES, LANES), F32)],
            flops=40 * depth * (stop - start),
        )
        fresh.append(some)
        steps.append(peaks)

    half = (tokens - head) // 2
    tail_rows = leaving(head, half, steps[-3])
    left_tails = [shifted(tail_rows, "pipe"), shifted(leaving(head + half, half, steps[-3]), "pipe")]

    group = LANES // depth
    peak_rows = [peaks] + [exchange(peaks, "expert", k) for k in range(1, experts)]
    coded, token = call(
        lambda *refs: code_kernel(group, *refs),
        "codes",
        [shape((2, 1, depth, width), BF16), shape((8, LANES), F32)],
        *peak_rows[:group],
        *fresh,
        read=group + len(fresh),
        flops=4 * depth * width,
    )
    count = len(left_tails)
    left, scales = pl.pallas_call(
        lambda *refs: finish_kernel(head, group, count, *refs),
        in_specs=[ANY] * (count + 2) + [VMEM] * experts,
        out_specs=[ANY, VMEM],
        out_shape=[shape((1, tokens, width), BF16), shape((2, 1, experts // group, blocks), F32)],
        scratch_shapes=[pltpu.SemaphoreType.DMA((count,))],
        input_output_aliases={count: 0},
        compiler_params=ROOM,
        cost_estimate=pl.CostEstimate(flops=0, bytes_accessed=4 * (tokens - head) * width, transcendentals=0),
        name="finish",
    )(*left_tails, placed, token, *peak_rows)
    return (left, coded, scales)


def solution(mesh):
    in_specs = (
        P("pipe", "expert", "dp"),
        P("pipe", "expert", "dp"),
        P("pipe", "expert", "dp"),
        P(None, "pipe", "dp"),
        P(None, "pipe", None, "dp"),
        P(None, "pipe", None, "dp"),
        P(None, "pipe", "expert", "dp"),
        P(None, "pipe", "expert", "dp"),
        P(None, "pipe", "expert", "dp"),
    )
    out_specs = (
        P("pipe", "expert", "dp"),
        P(None, "pipe", "expert", "dp"),
        P(None, "pipe", None, "dp"),
    )
    return jax.shard_map(shards, mesh=mesh, in_specs=in_specs, out_specs=out_specs, check_vma=False)
```

```python
import jax
import jax.numpy as jnp
from jax import lax
from jax.experimental import pallas as pl
from jax.experimental.pallas import tpu as pltpu
from jax.sharding import PartitionSpec as P

D = 7168
LANES = 128
F32 = jnp.float32
BF16 = jnp.bfloat16
BOTH_LAST = (((1,), (1,)), ((), ()))
ROOM = pltpu.CompilerParams(vmem_limit_bytes=16 << 20)
ANY = pl.BlockSpec(memory_space=pl.ANY)
VMEM = pl.BlockSpec(memory_space=pltpu.VMEM)


def exchange(block, axis, offset):
    count = lax.axis_size(axis)
    return lax.ppermute(block, axis, [(i, i ^ offset) for i in range(count)])


def mirrored(block, axis):
    count = lax.axis_size(axis)
    return lax.ppermute(block, axis, [(i, count - 1 - i) for i in range(count)])


def turned(block, axis):
    count = lax.axis_size(axis)
    return lax.ppermute(block, axis, [(i, (i + 1) % count) for i in range(count)])


def shifted(block, axis):
    count = lax.axis_size(axis)
    return lax.ppermute(block, axis, [(i, i + 1) for i in range(count - 1)])


def halves_of_sum(block, axis):
    count = lax.axis_size(axis)
    offset = 1
    while True:
        other = exchange(block, axis, offset)
        offset *= 2
        if offset >= count:
            return block, other
        block = block + other


def shape(dims, dtype):
    return jax.ShapeDtypeStruct(dims, dtype)


def call(kernel, name, outs, *operands, read, scratch=(), flops=0):
    many = isinstance(outs, list)
    nbytes = sum(o.size * o.dtype.itemsize for o in operands[:read])
    return pl.pallas_call(
        kernel,
        in_specs=[VMEM] * read + [ANY] * (len(operands) - read),
        out_specs=[VMEM] * len(outs) if many else VMEM,
        out_shape=outs,
        scratch_shapes=list(scratch),
        compiler_params=ROOM,
        cost_estimate=pl.CostEstimate(flops=flops, bytes_accessed=nbytes, transcendentals=0),
        name=name,
    )(*operands)


def folded_squares(rows):
    tokens, width = rows.shape
    total = jnp.zeros((tokens, LANES), F32)
    for at in range(0, width, LANES):
        part = rows[:, at : at + LANES]
        total = total + part * part
    return total


def latent_kernel(tiles, x1, x2, c2, down, up, gain, out_ref, vx1, scaled2, vc2, va1, vx2, va2, vb2, vgain, sems):
    tokens, width = vx1.shape
    latent = va1.shape[0]
    tile = width // tiles
    groups = (
        ((x1.at[0], vx1), (down.at[0, 0], va1)),
        ((x2.at[0], vx2), (down.at[1, 0], va2)),
        ((c2.at[0], vc2), (up.at[1, 0], vb2)),
    )

    def copies(job, at):
        cols = pl.ds(at * tile, tile)
        return [
            pltpu.make_async_copy(src.at[:, cols], dst.at[:, cols], sems.at[job, k, at])
            for k, (src, dst) in enumerate(groups[job])
        ]

    whole_gain = pltpu.make_async_copy(gain, vgain, sems.at[len(groups), 0, 0])
    whole_gain.start()
    for job in range(len(groups)):
        for at in range(tiles):
            for copy in copies(job, at):
                copy.start()
    base = 2 * latent + tokens
    out_ref[...] = jnp.zeros_like(out_ref)
    whole_gain.wait()

    def step(job, at):
        for copy in copies(job, at):
            copy.wait()
        cols = pl.ds(pl.multiple_of(at * tile, LANES), tile)
        if job < 2:
            rows = (vx1, vx2)[job][:, cols].astype(F32)
            right = (rows * vgain[job : job + 1, cols].astype(F32)).astype(BF16)
            squares = folded_squares(rows)
        if job == 0:
            raw = lax.dot_general(right, va1[:, cols], BOTH_LAST, preferred_element_type=F32)
            for piece in range(latent // LANES):
                out_ref[base + piece * tokens : base + (piece + 1) * tokens] += raw[:, piece * LANES : (piece + 1) * LANES]
            out_ref[base + (latent // LANES) * tokens :] += squares
        elif job == 1:
            scaled2[:, cols] = right
            out_ref[:latent] += lax.dot_general(va2[:, cols], right, BOTH_LAST, preferred_element_type=F32)
            out_ref[2 * latent : base] += squares
        else:
            out_ref[latent : 2 * latent] += lax.dot_general(
                vb2[:, cols], vc2[:, cols], BOTH_LAST, preferred_element_type=F32
            )

    for job in range(len(groups)):
        lax.fori_loop(0, tiles, lambda at, _, job=job: step(job, at) or 0, 0)


def fetch_kernel(in_ref, *rest):
    out_ref, sem = rest[-2:]
    copy = pltpu.make_async_copy(in_ref.at[0, 0], out_ref, sem)
    copy.start()
    copy.wait()


def leaving_kernel(start, own_ref, other_ref, x_ref, b_ref, *rest):
    out_ref = rest[-1]
    latent = b_ref.shape[0]
    count, width = out_ref.shape
    tokens = x_ref.shape[0]

    def summed(at):
        rows = slice(at + start, at + start + count)
        return own_ref[rows] + other_ref[rows]

    base = own_ref.shape[0] - tokens
    rscale = lax.rsqrt(jnp.sum(summed(base), axis=1, keepdims=True) / D + 1e-06)
    base -= (latent // LANES) * tokens
    hidden = jnp.concatenate([summed(base + at * tokens) * rscale for at in range(latent // LANES)], axis=1).astype(BF16)
    last = lax.axis_index("pipe") == lax.axis_size("pipe") - 1
    step = width // (4 if width % (4 * LANES) == 0 else 2)
    for at in range(0, width, step):
        cols = slice(at, at + step)
        rows = x_ref[start : start + count, cols].astype(F32)
        rows += jnp.dot(hidden, b_ref[:, cols], preferred_element_type=F32)
        out_ref[:, cols] = jnp.where(last, 0.0, rows).astype(BF16)


def grad_kernel(experts, start, own_ref, other_ref, x_ref, c_ref, *rest):
    outs, rows_ref = rest[-1 - experts : -1], rest[-1]
    latent = rows_ref.shape[1]
    depth = latent // experts
    cols = slice(start, start + outs[0].shape[2])
    me = lax.axis_index("expert")
    squares = own_ref[2 * latent : 2 * latent + LANES] + other_ref[2 * latent : 2 * latent + LANES]
    rscale = lax.rsqrt(jnp.sum(squares.T, axis=0, keepdims=True) / D + 1e-06)
    rows_ref[0] = (own_ref[latent : 2 * latent] + other_ref[latent : 2 * latent]) * rscale
    rows_ref[1] = (own_ref[:latent] + other_ref[:latent]) * rscale
    for side, right in enumerate((x_ref[:, cols], c_ref[:, cols])):
        left = jnp.concatenate(
            [rows_ref[side, pl.ds(pl.multiple_of((me ^ k) * depth, depth), depth), :] for k in range(experts)]
        )
        both = jnp.dot(left.astype(BF16), right, preferred_element_type=F32).astype(BF16)
        for k in range(experts):
            outs[k][side] = both[k * depth : (k + 1) * depth]


def share_kernel(experts, *refs):
    total = refs[0][...].astype(F32)
    for ref in refs[1:experts]:
        total = total + ref[...].astype(F32)
    refs[-1][...] = total.astype(BF16)


def update_kernel(start, share_ref, master_ref, moment_ref, second_ref, *rest):
    fresh_ref, peak_ref, wide = rest[-3:]
    cols = slice(start, start + share_ref.shape[2])
    grad = share_ref[...].astype(F32)
    first = 0.9 * moment_ref[:, 0, :, cols].astype(F32) + 0.1 * grad
    secnd = 0.95 * second_ref[:, 0, :, cols].astype(F32) + 0.05 * grad * grad
    update = first / (1.0 - 0.9**10) / (jnp.sqrt(secnd / (1.0 - 0.95**10)) + 1e-08)
    weights = master_ref[:, 0, :, cols]
    fresh = weights - 0.01 * (update + 0.1 * weights)
    fresh_ref[...] = fresh
    peak_ref[...] = jnp.zeros_like(peak_ref) if start == 0 else rest[0][...]
    wide[...] = jnp.zeros_like(wide)
    for side in range(2):
        peak = jnp.max(jnp.abs(fresh[side]), axis=0, keepdims=True)
        for at in range(0, peak.shape[1], LANES):
            block = (start + at) // LANES
            wide[side, block : block + 1, :] = peak[:, at : at + LANES]
        peak_ref[side : side + 1, :] = jnp.maximum(
            peak_ref[side : side + 1, :], jnp.max(wide[side].T, axis=0, keepdims=True)
        )


def merged(refs):
    top = refs[0][...]
    for ref in refs[1:]:
        top = jnp.maximum(top, ref[...])
    return top + 1e-06


def code_kernel(group, *refs):
    peak_refs, fresh_refs, (code_ref, token_ref) = refs[:group], refs[group:-2], refs[-2:]
    token_ref[...] = jnp.zeros_like(token_ref)
    column = (1.0 / merged(peak_refs)).T
    for side in range(2):
        inverse = jnp.broadcast_to(column[:, side : side + 1], (LANES, LANES))
        block = 0
        for ref in fresh_refs:
            for at in range(0, ref.shape[2], LANES):
                code_ref[side, 0, :, block * LANES : (block + 1) * LANES] = (
                    ref[side, :, at : at + LANES] * inverse[block : block + 1]
                ).astype(BF16)
                block += 1


def scale_kernel(group, experts, *refs):
    peak_refs, scale_ref = refs[:experts], refs[-1]
    blocks = scale_ref.shape[3]
    mine = lax.axis_index("expert") // group
    for far in range(len(peak_refs) // group):
        top = merged(peak_refs[far * group : (far + 1) * group])
        for side in range(2):
            scale_ref[side, 0, pl.ds(mine ^ far, 1), :] = top[side : side + 1, :blocks]


def place_kernel(start, count, *refs):
    out_ref, token_ref, sems = refs[-3:]
    copies = []
    for k, ref in enumerate(refs[:count]):
        rows = pl.ds(start + k * ref.shape[0], ref.shape[0])
        copies.append(pltpu.make_async_copy(ref, out_ref.at[0, rows], sems.at[k]))
    for copy in copies:
        copy.start()
    token_ref[...] = jnp.zeros_like(token_ref)
    for copy in copies:
        copy.wait()


def shards(enter_fwd, enter_rev, cot_rev, gain, proj_down, proj_up, master, moment, second):
    tokens, width = enter_fwd.shape[1:]
    latent = proj_down.shape[2]
    experts = lax.axis_size("expert")
    depth = latent // experts
    blocks = width // LANES
    tiles = 2
    weights = [8, 7, 7, 6]
    edges = [blocks * sum(weights[:k]) // sum(weights) * LANES for k in range(len(weights) + 1)]
    chunks = list(zip(edges[:-1], edges[1:]))

    def streamed(array):
        return pltpu.with_memory_space_constraint(array, pltpu.HBM)

    pack_rows = 2 * latent + tokens + (latent // LANES + 1) * tokens
    held = pltpu.VMEM((tokens, width), BF16)
    packed, rows1, scaled2, cot2 = pl.pallas_call(
        lambda *refs: latent_kernel(tiles, *refs),
        in_specs=[ANY] * 6,
        out_specs=[VMEM] * 4,
        out_shape=[pltpu.VMEM((pack_rows, LANES), F32), held, held, held],
        scratch_shapes=[
            pltpu.VMEM((latent, width), BF16),
            pltpu.VMEM((tokens, width), BF16),
            pltpu.VMEM((latent, width), BF16),
            pltpu.VMEM((latent, width), BF16),
            pltpu.VMEM((2, width), BF16),
            pltpu.SemaphoreType.DMA((4, 2, tiles)),
        ],
        compiler_params=ROOM,
        cost_estimate=pl.CostEstimate(
            flops=6 * tokens * latent * width, bytes_accessed=6 * (tokens + latent) * width, transcendentals=0
        ),
        name="latents",
    )(*(streamed(a) for a in (enter_fwd, enter_rev, cot_rev, proj_down, proj_up, gain.reshape(2, width))))
    own_up = pl.pallas_call(
        fetch_kernel,
        in_specs=[ANY] * 2,
        out_specs=VMEM,
        out_shape=pltpu.VMEM((latent, width), BF16),
        scratch_shapes=[pltpu.SemaphoreType.DMA],
        compiler_params=ROOM,
        cost_estimate=pl.CostEstimate(flops=0, bytes_accessed=2 * latent * width, transcendentals=0),
        name="fetch",
    )(streamed(proj_up), packed)
    pair = halves_of_sum(packed, "dp")

    def leaving(start, count, *after):
        return call(
            lambda *refs: leaving_kernel(start, *refs),
            "leaving",
            shape((count, width), BF16),
            *pair,
            rows1,
            own_up,
            *after,
            read=4,
            flops=2 * count * latent * width,
        )

    def grads(chunk, *after):
        start, stop = chunks[chunk]
        return call(
            lambda *refs: grad_kernel(experts, start, *refs),
            "grads",
            [shape((2, depth, stop - start), BF16)] * experts,
            *pair,
            scaled2,
            cot2,
            *after,
            read=4,
            scratch=[pltpu.VMEM((2, latent, tokens), F32)],
            flops=4 * tokens * latent * (stop - start),
        )

    head = 96
    first_rows = leaving(0, head)
    left_head = turned(first_rows, "pipe")
    first = grads(0, first_rows)
    shares, arrived, others = [], [], []
    for chunk in range(len(chunks)):
        own, *pieces = grads(chunk, *shares[-2:-1], *others[-1][:1]) if chunk else first
        others.append([exchange(piece, "expert", 1 + k) for k, piece in enumerate(pieces)])
        after = [left_head] if chunk == 1 else arrived[chunk - 2 : chunk - 1] if chunk > 1 else []
        shares.append(
            call(
                lambda *refs: share_kernel(experts, *refs),
                "share",
                shape(own.shape, BF16),
                own,
                *others[-1],
                *after,
                read=experts,
            )
        )
        arrived.append(mirrored(shares[-1], "pipe"))

    def place(start, some, kept=(), after=()):
        count = len(some)
        return pl.pallas_call(
            lambda *refs: place_kernel(start, count, *refs),
            in_specs=[ANY] * (count + len(kept) + len(after)),
            out_specs=[ANY, VMEM],
            out_shape=[shape((1, tokens, width), BF16), shape((8, LANES), F32)],
            scratch_shapes=[pltpu.SemaphoreType.DMA((count,))],
            input_output_aliases={count + k: k for k in range(len(kept))},
            compiler_params=ROOM,
            cost_estimate=pl.CostEstimate(
                flops=0, bytes_accessed=4 * count * some[0].shape[0] * width, transcendentals=0
            ),
            name="place",
        )(*some, *kept, *after)

    placed, token = place(0, [left_head])

    fresh, peaks, steps = [], None, []
    for chunk, (start, stop) in enumerate(chunks):
        kept = () if peaks is None else (peaks,)
        after = (token,) if chunk == 1 else ()
        some, peaks = call(
            lambda *refs: update_kernel(start, *refs),
            "update",
            [shape((2, depth, stop - start), F32), shape((8, LANES), F32)],
            arrived[chunk],
            master,
            moment,
            second,
            *kept,
            *after,
            read=4 + len(kept),
            scratch=[pltpu.VMEM((2, LANES, LANES), F32)],
            flops=40 * depth * (stop - start),
        )
        fresh.append(some)
        steps.append(peaks)

    half = (tokens - head) // 2
    tail_rows = leaving(head, half, steps[-3])
    left_tails = [shifted(tail_rows, "pipe"), shifted(leaving(head + half, half, steps[-3]), "pipe")]

    group = LANES // depth
    peak_rows = [peaks] + [exchange(peaks, "expert", k) for k in range(1, experts)]
    coded, token = call(
        lambda *refs: code_kernel(group, *refs),
        "codes",
        [shape((2, 1, depth, width), BF16), shape((8, LANES), F32)],
        *peak_rows[:group],
        *fresh,
        read=group + len(fresh),
        flops=4 * depth * width,
    )
    placed, token = place(head, left_tails, (placed,), (token,))
    scales = call(
        lambda *refs: scale_kernel(group, experts, *refs),
        "scales",
        shape((2, 1, experts // group, blocks), F32),
        *peak_rows,
        token,
        read=experts,
    )
    return (placed, coded, scales)


def solution(mesh):
    in_specs = (
        P("pipe", "expert", "dp"),
        P("pipe", "expert", "dp"),
        P("pipe", "expert", "dp"),
        P(None, "pipe", "dp"),
        P(None, "pipe", None, "dp"),
        P(None, "pipe", None, "dp"),
        P(None, "pipe", "expert", "dp"),
        P(None, "pipe", "expert", "dp"),
        P(None, "pipe", "expert", "dp"),
    )
    out_specs = (
        P("pipe", "expert", "dp"),
        P(None, "pipe", "expert", "dp"),
        P(None, "pipe", None, "dp"),
    )
    return jax.shard_map(shards, mesh=mesh, in_specs=in_specs, out_specs=out_specs, check_vma=False)
```

```python
import jax
import jax.numpy as jnp
from jax import lax
from jax.experimental import pallas as pl
from jax.experimental.pallas import tpu as pltpu
from jax.sharding import PartitionSpec as P

D = 7168
LANES = 128
F32 = jnp.float32
BF16 = jnp.bfloat16
BOTH_LAST = (((1,), (1,)), ((), ()))
ROOM = pltpu.CompilerParams(vmem_limit_bytes=16 << 20)
ANY = pl.BlockSpec(memory_space=pl.ANY)
VMEM = pl.BlockSpec(memory_space=pltpu.VMEM)


def exchange(block, axis, offset):
    count = lax.axis_size(axis)
    return lax.ppermute(block, axis, [(i, i ^ offset) for i in range(count)])


def mirrored(block, axis):
    count = lax.axis_size(axis)
    return lax.ppermute(block, axis, [(i, count - 1 - i) for i in range(count)])


def turned(block, axis):
    count = lax.axis_size(axis)
    return lax.ppermute(block, axis, [(i, (i + 1) % count) for i in range(count)])


def shifted(block, axis):
    count = lax.axis_size(axis)
    return lax.ppermute(block, axis, [(i, i + 1) for i in range(count - 1)])


def halves_of_sum(block, axis):
    count = lax.axis_size(axis)
    offset = 1
    while True:
        other = exchange(block, axis, offset)
        offset *= 2
        if offset >= count:
            return block, other
        block = block + other


def shape(dims, dtype):
    return jax.ShapeDtypeStruct(dims, dtype)


def call(kernel, name, outs, *operands, read, scratch=(), flops=0):
    many = isinstance(outs, list)
    nbytes = sum(o.size * o.dtype.itemsize for o in operands[:read])
    return pl.pallas_call(
        kernel,
        in_specs=[VMEM] * read + [ANY] * (len(operands) - read),
        out_specs=[VMEM] * len(outs) if many else VMEM,
        out_shape=outs,
        scratch_shapes=list(scratch),
        compiler_params=ROOM,
        cost_estimate=pl.CostEstimate(flops=flops, bytes_accessed=nbytes, transcendentals=0),
        name=name,
    )(*operands)


def folded_squares(rows):
    tokens, width = rows.shape
    total = jnp.zeros((tokens, LANES), F32)
    for at in range(0, width, LANES):
        part = rows[:, at : at + LANES]
        total = total + part * part
    return total


def latent_kernel(tiles, x1, x2, c2, down, up, gain, out_ref, vx1, scaled2, vc2, va1, vx2, va2, vb2, vgain, sems):
    tokens, width = vx1.shape
    latent = va1.shape[0]
    tile = width // tiles
    groups = (
        ((x1.at[0], vx1), (down.at[0, 0], va1)),
        ((x2.at[0], vx2), (down.at[1, 0], va2)),
        ((c2.at[0], vc2), (up.at[1, 0], vb2)),
    )

    def copies(job, at):
        cols = pl.ds(at * tile, tile)
        return [
            pltpu.make_async_copy(src.at[:, cols], dst.at[:, cols], sems.at[job, k, at])
            for k, (src, dst) in enumerate(groups[job])
        ]

    whole_gain = pltpu.make_async_copy(gain, vgain, sems.at[len(groups), 0, 0])
    whole_gain.start()
    for job in range(len(groups)):
        for at in range(tiles):
            for copy in copies(job, at):
                copy.start()
    base = 2 * latent + tokens
    out_ref[...] = jnp.zeros_like(out_ref)
    whole_gain.wait()

    def step(job, at):
        for copy in copies(job, at):
            copy.wait()
        cols = pl.ds(pl.multiple_of(at * tile, LANES), tile)
        if job < 2:
            rows = (vx1, vx2)[job][:, cols].astype(F32)
            right = (rows * vgain[job : job + 1, cols].astype(F32)).astype(BF16)
            squares = folded_squares(rows)
        if job == 0:
            raw = lax.dot_general(right, va1[:, cols], BOTH_LAST, preferred_element_type=F32)
            for piece in range(latent // LANES):
                out_ref[base + piece * tokens : base + (piece + 1) * tokens] += raw[:, piece * LANES : (piece + 1) * LANES]
            out_ref[base + (latent // LANES) * tokens :] += squares
        elif job == 1:
            scaled2[:, cols] = right
            out_ref[:latent] += lax.dot_general(va2[:, cols], right, BOTH_LAST, preferred_element_type=F32)
            out_ref[2 * latent : base] += squares
        else:
            out_ref[latent : 2 * latent] += lax.dot_general(
                vb2[:, cols], vc2[:, cols], BOTH_LAST, preferred_element_type=F32
            )

    for job in range(len(groups)):
        lax.fori_loop(0, tiles, lambda at, _, job=job: step(job, at) or 0, 0)


def fetch_kernel(in_ref, *rest):
    out_ref, sem = rest[-2:]
    copy = pltpu.make_async_copy(in_ref.at[0, 0], out_ref, sem)
    copy.start()
    copy.wait()


def leaving_kernel(start, own_ref, other_ref, x_ref, b_ref, *rest):
    out_ref = rest[-1]
    latent = b_ref.shape[0]
    count, width = out_ref.shape
    tokens = x_ref.shape[0]

    def summed(at):
        rows = slice(at + start, at + start + count)
        return own_ref[rows] + other_ref[rows]

    base = own_ref.shape[0] - tokens
    rscale = lax.rsqrt(jnp.sum(summed(base), axis=1, keepdims=True) / D + 1e-06)
    base -= (latent // LANES) * tokens
    hidden = jnp.concatenate([summed(base + at * tokens) * rscale for at in range(latent // LANES)], axis=1).astype(BF16)
    last = lax.axis_index("pipe") == lax.axis_size("pipe") - 1
    step = width // (4 if width % (4 * LANES) == 0 else 2)
    for at in range(0, width, step):
        cols = slice(at, at + step)
        rows = x_ref[start : start + count, cols].astype(F32)
        rows += jnp.dot(hidden, b_ref[:, cols], preferred_element_type=F32)
        out_ref[:, cols] = jnp.where(last, 0.0, rows).astype(BF16)


def grad_kernel(experts, start, own_ref, other_ref, x_ref, c_ref, *rest):
    outs, rows_ref = rest[-1 - experts : -1], rest[-1]
    latent = rows_ref.shape[1]
    depth = latent // experts
    cols = slice(start, start + outs[0].shape[2])
    me = lax.axis_index("expert")
    squares = own_ref[2 * latent : 2 * latent + LANES] + other_ref[2 * latent : 2 * latent + LANES]
    rscale = lax.rsqrt(jnp.sum(squares.T, axis=0, keepdims=True) / D + 1e-06)
    rows_ref[0] = (own_ref[latent : 2 * latent] + other_ref[latent : 2 * latent]) * rscale
    rows_ref[1] = (own_ref[:latent] + other_ref[:latent]) * rscale
    for side, right in enumerate((x_ref[:, cols], c_ref[:, cols])):
        left = jnp.concatenate(
            [rows_ref[side, pl.ds(pl.multiple_of((me ^ k) * depth, depth), depth), :] for k in range(experts)]
        )
        both = jnp.dot(left.astype(BF16), right, preferred_element_type=F32).astype(BF16)
        for k in range(experts):
            outs[k][side] = both[k * depth : (k + 1) * depth]


def share_kernel(experts, *refs):
    total = refs[0][...].astype(F32)
    for ref in refs[1:experts]:
        total = total + ref[...].astype(F32)
    refs[-1][...] = total.astype(BF16)


def update_kernel(start, share_ref, master_ref, moment_ref, second_ref, *rest):
    fresh_ref, peak_ref, wide = rest[-3:]
    cols = slice(start, start + share_ref.shape[2])
    grad = share_ref[...].astype(F32)
    first = 0.9 * moment_ref[:, 0, :, cols].astype(F32) + 0.1 * grad
    secnd = 0.95 * second_ref[:, 0, :, cols].astype(F32) + 0.05 * grad * grad
    update = first / (1.0 - 0.9**10) / (jnp.sqrt(secnd / (1.0 - 0.95**10)) + 1e-08)
    weights = master_ref[:, 0, :, cols]
    fresh = weights - 0.01 * (update + 0.1 * weights)
    fresh_ref[...] = fresh
    peak_ref[...] = jnp.zeros_like(peak_ref) if start == 0 else rest[0][...]
    wide[...] = jnp.zeros_like(wide)
    for side in range(2):
        peak = jnp.max(jnp.abs(fresh[side]), axis=0, keepdims=True)
        for at in range(0, peak.shape[1], LANES):
            block = (start + at) // LANES
            wide[side, block : block + 1, :] = peak[:, at : at + LANES]
        peak_ref[side : side + 1, :] = jnp.maximum(
            peak_ref[side : side + 1, :], jnp.max(wide[side].T, axis=0, keepdims=True)
        )


def merged(refs):
    top = refs[0][...]
    for ref in refs[1:]:
        top = jnp.maximum(top, ref[...])
    return top + 1e-06


def code_kernel(group, *refs):
    peak_refs, fresh_refs, (code_ref, token_ref) = refs[:group], refs[group:-2], refs[-2:]
    token_ref[...] = jnp.zeros_like(token_ref)
    column = (1.0 / merged(peak_refs)).T
    for side in range(2):
        inverse = jnp.broadcast_to(column[:, side : side + 1], (LANES, LANES))
        block = 0
        for ref in fresh_refs:
            for at in range(0, ref.shape[2], LANES):
                code_ref[side, 0, :, block * LANES : (block + 1) * LANES] = (
                    ref[side, :, at : at + LANES] * inverse[block : block + 1]
                ).astype(BF16)
                block += 1


def scale_kernel(group, experts, *refs):
    peak_refs, scale_ref = refs[:experts], refs[-1]
    blocks = scale_ref.shape[3]
    mine = lax.axis_index("expert") // group
    for far in range(len(peak_refs) // group):
        top = merged(peak_refs[far * group : (far + 1) * group])
        for side in range(2):
            scale_ref[side, 0, pl.ds(mine ^ far, 1), :] = top[side : side + 1, :blocks]


def place_kernel(start, count, *refs):
    out_ref, token_ref, sems = refs[-3:]
    copies = []
    for k, ref in enumerate(refs[:count]):
        rows = pl.ds(start + k * ref.shape[0], ref.shape[0])
        copies.append(pltpu.make_async_copy(ref, out_ref.at[0, rows], sems.at[k]))
    for copy in copies:
        copy.start()
    token_ref[...] = jnp.zeros_like(token_ref)
    for copy in copies:
        copy.wait()


def shards(enter_fwd, enter_rev, cot_rev, gain, proj_down, proj_up, master, moment, second):
    tokens, width = enter_fwd.shape[1:]
    latent = proj_down.shape[2]
    experts = lax.axis_size("expert")
    depth = latent // experts
    blocks = width // LANES
    tiles = 2
    weights = [8, 8, 7, 5]
    edges = [blocks * sum(weights[:k]) // sum(weights) * LANES for k in range(len(weights) + 1)]
    chunks = list(zip(edges[:-1], edges[1:]))

    def streamed(array):
        return pltpu.with_memory_space_constraint(array, pltpu.HBM)

    pack_rows = 2 * latent + tokens + (latent // LANES + 1) * tokens
    held = pltpu.VMEM((tokens, width), BF16)
    packed, rows1, scaled2, cot2 = pl.pallas_call(
        lambda *refs: latent_kernel(tiles, *refs),
        in_specs=[ANY] * 6,
        out_specs=[VMEM] * 4,
        out_shape=[pltpu.VMEM((pack_rows, LANES), F32), held, held, held],
        scratch_shapes=[
            pltpu.VMEM((latent, width), BF16),
            pltpu.VMEM((tokens, width), BF16),
            pltpu.VMEM((latent, width), BF16),
            pltpu.VMEM((latent, width), BF16),
            pltpu.VMEM((2, width), BF16),
            pltpu.SemaphoreType.DMA((4, 2, tiles)),
        ],
        compiler_params=ROOM,
        cost_estimate=pl.CostEstimate(
            flops=6 * tokens * latent * width, bytes_accessed=6 * (tokens + latent) * width, transcendentals=0
        ),
        name="latents",
    )(*(streamed(a) for a in (enter_fwd, enter_rev, cot_rev, proj_down, proj_up, gain.reshape(2, width))))
    own_up = pl.pallas_call(
        fetch_kernel,
        in_specs=[ANY] * 2,
        out_specs=VMEM,
        out_shape=pltpu.VMEM((latent, width), BF16),
        scratch_shapes=[pltpu.SemaphoreType.DMA],
        compiler_params=ROOM,
        cost_estimate=pl.CostEstimate(flops=0, bytes_accessed=2 * latent * width, transcendentals=0),
        name="fetch",
    )(streamed(proj_up), packed)
    pair = halves_of_sum(packed, "dp")

    def leaving(start, count, *after):
        return call(
            lambda *refs: leaving_kernel(start, *refs),
            "leaving",
            shape((count, width), BF16),
            *pair,
            rows1,
            own_up,
            *after,
            read=4,
            flops=2 * count * latent * width,
        )

    def grads(chunk, *after):
        start, stop = chunks[chunk]
        return call(
            lambda *refs: grad_kernel(experts, start, *refs),
            "grads",
            [shape((2, depth, stop - start), BF16)] * experts,
            *pair,
            scaled2,
            cot2,
            *after,
            read=4,
            scratch=[pltpu.VMEM((2, latent, tokens), F32)],
            flops=4 * tokens * latent * (stop - start),
        )

    head = 96
    first_rows = leaving(0, head)
    left_head = turned(first_rows, "pipe")
    first = grads(0, first_rows)
    shares, arrived, others = [], [], []
    for chunk in range(len(chunks)):
        own, *pieces = grads(chunk, *shares[-2:-1], *others[-1][:1]) if chunk else first
        others.append([exchange(piece, "expert", 1 + k) for k, piece in enumerate(pieces)])
        after = [left_head] if chunk == 1 else arrived[chunk - 2 : chunk - 1] if chunk > 1 else []
        shares.append(
            call(
                lambda *refs: share_kernel(experts, *refs),
                "share",
                shape(own.shape, BF16),
                own,
                *others[-1],
                *after,
                read=experts,
            )
        )
        arrived.append(mirrored(shares[-1], "pipe"))

    def place(start, some, kept=(), after=()):
        count = len(some)
        return pl.pallas_call(
            lambda *refs: place_kernel(start, count, *refs),
            in_specs=[ANY] * (count + len(kept) + len(after)),
            out_specs=[ANY, VMEM],
            out_shape=[shape((1, tokens, width), BF16), shape((8, LANES), F32)],
            scratch_shapes=[pltpu.SemaphoreType.DMA((count,))],
            input_output_aliases={count + k: k for k in range(len(kept))},
            compiler_params=ROOM,
            cost_estimate=pl.CostEstimate(
                flops=0, bytes_accessed=4 * count * some[0].shape[0] * width, transcendentals=0
            ),
            name="place",
        )(*some, *kept, *after)

    placed, token = place(0, [left_head])

    fresh, peaks, steps = [], None, []
    for chunk, (start, stop) in enumerate(chunks):
        kept = () if peaks is None else (peaks,)
        after = (token,) if chunk == 1 else ()
        some, peaks = call(
            lambda *refs: update_kernel(start, *refs),
            "update",
            [shape((2, depth, stop - start), F32), shape((8, LANES), F32)],
            arrived[chunk],
            master,
            moment,
            second,
            *kept,
            *after,
            read=4 + len(kept),
            scratch=[pltpu.VMEM((2, LANES, LANES), F32)],
            flops=40 * depth * (stop - start),
        )
        fresh.append(some)
        steps.append(peaks)

    half = (tokens - head) // 2
    tail_rows = leaving(head, half, steps[-3])
    left_tails = [shifted(tail_rows, "pipe"), shifted(leaving(head + half, half, steps[-3]), "pipe")]

    group = LANES // depth
    peak_rows = [peaks] + [exchange(peaks, "expert", k) for k in range(1, experts)]
    coded, token = call(
        lambda *refs: code_kernel(group, *refs),
        "codes",
        [shape((2, 1, depth, width), BF16), shape((8, LANES), F32)],
        *peak_rows[:group],
        *fresh,
        read=group + len(fresh),
        flops=4 * depth * width,
    )
    placed, token = place(head, left_tails, (placed,), (token,))
    scales = call(
        lambda *refs: scale_kernel(group, experts, *refs),
        "scales",
        shape((2, 1, experts // group, blocks), F32),
        *peak_rows,
        token,
        read=experts,
    )
    return (placed, coded, scales)


def solution(mesh):
    in_specs = (
        P("pipe", "expert", "dp"),
        P("pipe", "expert", "dp"),
        P("pipe", "expert", "dp"),
        P(None, "pipe", "dp"),
        P(None, "pipe", None, "dp"),
        P(None, "pipe", None, "dp"),
        P(None, "pipe", "expert", "dp"),
        P(None, "pipe", "expert", "dp"),
        P(None, "pipe", "expert", "dp"),
    )
    out_specs = (
        P("pipe", "expert", "dp"),
        P(None, "pipe", "expert", "dp"),
        P(None, "pipe", None, "dp"),
    )
    return jax.shard_map(shards, mesh=mesh, in_specs=in_specs, out_specs=out_specs, check_vma=False)
```

```python
import jax
import jax.numpy as jnp
from jax import lax
from jax.experimental import pallas as pl
from jax.experimental.pallas import tpu as pltpu
from jax.sharding import PartitionSpec as P

D = 7168
LANES = 128
F32 = jnp.float32
BF16 = jnp.bfloat16
BOTH_LAST = (((1,), (1,)), ((), ()))
ROOM = pltpu.CompilerParams(vmem_limit_bytes=16 << 20)
ANY = pl.BlockSpec(memory_space=pl.ANY)
VMEM = pl.BlockSpec(memory_space=pltpu.VMEM)


def exchange(block, axis, offset):
    count = lax.axis_size(axis)
    return lax.ppermute(block, axis, [(i, i ^ offset) for i in range(count)])


def mirrored(block, axis):
    count = lax.axis_size(axis)
    return lax.ppermute(block, axis, [(i, count - 1 - i) for i in range(count)])


def turned(block, axis):
    count = lax.axis_size(axis)
    return lax.ppermute(block, axis, [(i, (i + 1) % count) for i in range(count)])


def shifted(block, axis):
    count = lax.axis_size(axis)
    return lax.ppermute(block, axis, [(i, i + 1) for i in range(count - 1)])


def halves_of_sum(block, axis):
    count = lax.axis_size(axis)
    offset = 1
    while True:
        other = exchange(block, axis, offset)
        offset *= 2
        if offset >= count:
            return block, other
        block = block + other


def shape(dims, dtype):
    return jax.ShapeDtypeStruct(dims, dtype)


def call(kernel, name, outs, *operands, read, scratch=(), flops=0):
    many = isinstance(outs, list)
    nbytes = sum(o.size * o.dtype.itemsize for o in operands[:read])
    return pl.pallas_call(
        kernel,
        in_specs=[VMEM] * read + [ANY] * (len(operands) - read),
        out_specs=[VMEM] * len(outs) if many else VMEM,
        out_shape=outs,
        scratch_shapes=list(scratch),
        compiler_params=ROOM,
        cost_estimate=pl.CostEstimate(flops=flops, bytes_accessed=nbytes, transcendentals=0),
        name=name,
    )(*operands)


def folded_squares(rows):
    tokens, width = rows.shape
    total = jnp.zeros((tokens, LANES), F32)
    for at in range(0, width, LANES):
        part = rows[:, at : at + LANES]
        total = total + part * part
    return total


def latent_kernel(tiles, x1, x2, c2, down, up, gain_ref, out_ref, vx1, scaled2, vc2, va1, vx2, va2, vb2, sems):
    tokens, width = vx1.shape
    latent = va1.shape[0]
    tile = width // tiles
    groups = (
        ((x1.at[0], vx1), (down.at[0, 0], va1)),
        ((x2.at[0], vx2), (down.at[1, 0], va2)),
        ((c2.at[0], vc2), (up.at[1, 0], vb2)),
    )

    def copies(job, at):
        cols = pl.ds(at * tile, tile)
        return [
            pltpu.make_async_copy(src.at[:, cols], dst.at[:, cols], sems.at[job, k, at])
            for k, (src, dst) in enumerate(groups[job])
        ]

    for job in range(len(groups)):
        for at in range(tiles):
            for copy in copies(job, at):
                copy.start()
    base = 2 * latent + tokens
    out_ref[...] = jnp.zeros_like(out_ref)

    def step(job, at):
        for copy in copies(job, at):
            copy.wait()
        cols = pl.ds(pl.multiple_of(at * tile, LANES), tile)
        if job < 2:
            rows = (vx1, vx2)[job][:, cols].astype(F32)
            right = (rows * gain_ref[job : job + 1, cols]).astype(BF16)
            squares = folded_squares(rows)
        if job == 0:
            raw = lax.dot_general(right, va1[:, cols], BOTH_LAST, preferred_element_type=F32)
            for piece in range(latent // LANES):
                out_ref[base + piece * tokens : base + (piece + 1) * tokens] += raw[:, piece * LANES : (piece + 1) * LANES]
            out_ref[base + (latent // LANES) * tokens :] += squares
        elif job == 1:
            scaled2[:, cols] = right
            out_ref[:latent] += lax.dot_general(va2[:, cols], right, BOTH_LAST, preferred_element_type=F32)
            out_ref[2 * latent : base] += squares
        else:
            out_ref[latent : 2 * latent] += lax.dot_general(
                vb2[:, cols], vc2[:, cols], BOTH_LAST, preferred_element_type=F32
            )

    for job in range(len(groups)):
        lax.fori_loop(0, tiles, lambda at, _, job=job: step(job, at) or 0, 0)


def fetch_kernel(in_ref, *rest):
    out_ref, sem = rest[-2:]
    copy = pltpu.make_async_copy(in_ref.at[0, 0], out_ref, sem)
    copy.start()
    copy.wait()


def leaving_kernel(start, own_ref, other_ref, x_ref, b_ref, *rest):
    out_ref = rest[-1]
    latent = b_ref.shape[0]
    count, width = out_ref.shape
    tokens = x_ref.shape[0]

    def summed(at):
        rows = slice(at + start, at + start + count)
        return own_ref[rows] + other_ref[rows]

    base = own_ref.shape[0] - tokens
    rscale = lax.rsqrt(jnp.sum(summed(base), axis=1, keepdims=True) / D + 1e-06)
    base -= (latent // LANES) * tokens
    hidden = jnp.concatenate([summed(base + at * tokens) * rscale for at in range(latent // LANES)], axis=1).astype(BF16)
    last = lax.axis_index("pipe") == lax.axis_size("pipe") - 1
    step = width // (4 if width % (4 * LANES) == 0 else 2)
    for at in range(0, width, step):
        cols = slice(at, at + step)
        rows = x_ref[start : start + count, cols].astype(F32)
        rows += jnp.dot(hidden, b_ref[:, cols], preferred_element_type=F32)
        out_ref[:, cols] = jnp.where(last, 0.0, rows).astype(BF16)


def grad_kernel(experts, start, own_ref, other_ref, x_ref, c_ref, *rest):
    outs, rows_ref = rest[-1 - experts : -1], rest[-1]
    latent = rows_ref.shape[1]
    depth = latent // experts
    cols = slice(start, start + outs[0].shape[2])
    me = lax.axis_index("expert")
    squares = own_ref[2 * latent : 2 * latent + LANES] + other_ref[2 * latent : 2 * latent + LANES]
    rscale = lax.rsqrt(jnp.sum(squares.T, axis=0, keepdims=True) / D + 1e-06)
    rows_ref[0] = (own_ref[latent : 2 * latent] + other_ref[latent : 2 * latent]) * rscale
    rows_ref[1] = (own_ref[:latent] + other_ref[:latent]) * rscale
    for side, right in enumerate((x_ref[:, cols], c_ref[:, cols])):
        left = jnp.concatenate(
            [rows_ref[side, pl.ds(pl.multiple_of((me ^ k) * depth, depth), depth), :] for k in range(experts)]
        )
        both = jnp.dot(left.astype(BF16), right, preferred_element_type=F32).astype(BF16)
        for k in range(experts):
            outs[k][side] = both[k * depth : (k + 1) * depth]


def share_kernel(experts, *refs):
    total = refs[0][...].astype(F32)
    for ref in refs[1:experts]:
        total = total + ref[...].astype(F32)
    refs[-1][...] = total.astype(BF16)


def update_kernel(start, share_ref, master_ref, moment_ref, second_ref, *rest):
    fresh_ref, peak_ref, wide = rest[-3:]
    cols = slice(start, start + share_ref.shape[2])
    grad = share_ref[...].astype(F32)
    first = 0.9 * moment_ref[:, 0, :, cols].astype(F32) + 0.1 * grad
    secnd = 0.95 * second_ref[:, 0, :, cols].astype(F32) + 0.05 * grad * grad
    update = first / (1.0 - 0.9**10) / (jnp.sqrt(secnd / (1.0 - 0.95**10)) + 1e-08)
    weights = master_ref[:, 0, :, cols]
    fresh = weights - 0.01 * (update + 0.1 * weights)
    fresh_ref[...] = fresh
    peak_ref[...] = jnp.zeros_like(peak_ref) if start == 0 else rest[0][...]
    wide[...] = jnp.zeros_like(wide)
    for side in range(2):
        peak = jnp.max(jnp.abs(fresh[side]), axis=0, keepdims=True)
        for at in range(0, peak.shape[1], LANES):
            block = (start + at) // LANES
            wide[side, block : block + 1, :] = peak[:, at : at + LANES]
        peak_ref[side : side + 1, :] = jnp.maximum(
            peak_ref[side : side + 1, :], jnp.max(wide[side].T, axis=0, keepdims=True)
        )


def merged(refs):
    top = refs[0][...]
    for ref in refs[1:]:
        top = jnp.maximum(top, ref[...])
    return top + 1e-06


def code_kernel(group, *refs):
    peak_refs, fresh_refs, (code_ref, token_ref) = refs[:group], refs[group:-2], refs[-2:]
    token_ref[...] = jnp.zeros_like(token_ref)
    column = (1.0 / merged(peak_refs)).T
    for side in range(2):
        inverse = jnp.broadcast_to(column[:, side : side + 1], (LANES, LANES))
        block = 0
        for ref in fresh_refs:
            for at in range(0, ref.shape[2], LANES):
                code_ref[side, 0, :, block * LANES : (block + 1) * LANES] = (
                    ref[side, :, at : at + LANES] * inverse[block : block + 1]
                ).astype(BF16)
                block += 1


def scale_kernel(group, experts, *refs):
    peak_refs, scale_ref = refs[:experts], refs[-1]
    blocks = scale_ref.shape[3]
    mine = lax.axis_index("expert") // group
    for far in range(len(peak_refs) // group):
        top = merged(peak_refs[far * group : (far + 1) * group])
        for side in range(2):
            scale_ref[side, 0, pl.ds(mine ^ far, 1), :] = top[side : side + 1, :blocks]


def place_kernel(start, count, *refs):
    out_ref, token_ref, sems = refs[-3:]
    copies = []
    for k, ref in enumerate(refs[:count]):
        rows = pl.ds(start + k * ref.shape[0], ref.shape[0])
        copies.append(pltpu.make_async_copy(ref, out_ref.at[0, rows], sems.at[k]))
    for copy in copies:
        copy.start()
    token_ref[...] = jnp.zeros_like(token_ref)
    for copy in copies:
        copy.wait()


def shards(enter_fwd, enter_rev, cot_rev, gain, proj_down, proj_up, master, moment, second):
    tokens, width = enter_fwd.shape[1:]
    latent = proj_down.shape[2]
    experts = lax.axis_size("expert")
    depth = latent // experts
    blocks = width // LANES
    tiles = 2
    weights = [8, 7, 7, 6]
    edges = [blocks * sum(weights[:k]) // sum(weights) * LANES for k in range(len(weights) + 1)]
    chunks = list(zip(edges[:-1], edges[1:]))

    def streamed(array):
        return pltpu.with_memory_space_constraint(array, pltpu.HBM)

    pack_rows = 2 * latent + tokens + (latent // LANES + 1) * tokens
    held = pltpu.VMEM((tokens, width), BF16)
    packed, rows1, scaled2, cot2 = pl.pallas_call(
        lambda *refs: latent_kernel(tiles, *refs),
        in_specs=[ANY] * 5 + [VMEM],
        out_specs=[VMEM] * 4,
        out_shape=[pltpu.VMEM((pack_rows, LANES), F32), held, held, held],
        scratch_shapes=[
            pltpu.VMEM((latent, width), BF16),
            pltpu.VMEM((tokens, width), BF16),
            pltpu.VMEM((latent, width), BF16),
            pltpu.VMEM((latent, width), BF16),
            pltpu.SemaphoreType.DMA((3, 2, tiles)),
        ],
        compiler_params=ROOM,
        cost_estimate=pl.CostEstimate(
            flops=6 * tokens * latent * width, bytes_accessed=6 * (tokens + latent) * width, transcendentals=0
        ),
        name="latents",
    )(
        *(streamed(a) for a in (enter_fwd, enter_rev, cot_rev, proj_down, proj_up)),
        gain.reshape(2, width).astype(F32),
    )
    own_up = pl.pallas_call(
        fetch_kernel,
        in_specs=[ANY] * 2,
        out_specs=VMEM,
        out_shape=pltpu.VMEM((latent, width), BF16),
        scratch_shapes=[pltpu.SemaphoreType.DMA],
        compiler_params=ROOM,
        cost_estimate=pl.CostEstimate(flops=0, bytes_accessed=2 * latent * width, transcendentals=0),
        name="fetch",
    )(streamed(proj_up), packed)
    pair = halves_of_sum(packed, "dp")

    def leaving(start, count, *after):
        return call(
            lambda *refs: leaving_kernel(start, *refs),
            "leaving",
            shape((count, width), BF16),
            *pair,
            rows1,
            own_up,
            *after,
            read=4,
            flops=2 * count * latent * width,
        )

    def grads(chunk, *after):
        start, stop = chunks[chunk]
        return call(
            lambda *refs: grad_kernel(experts, start, *refs),
            "grads",
            [shape((2, depth, stop - start), BF16)] * experts,
            *pair,
            scaled2,
            cot2,
            *after,
            read=4,
            scratch=[pltpu.VMEM((2, latent, tokens), F32)],
            flops=4 * tokens * latent * (stop - start),
        )

    head = 96
    first_rows = leaving(0, head)
    left_head = turned(first_rows, "pipe")
    first = grads(0, first_rows)
    shares, arrived, others = [], [], []
    for chunk in range(len(chunks)):
        own, *pieces = grads(chunk, *shares[-2:-1], *others[-1][:1]) if chunk else first
        others.append([exchange(piece, "expert", 1 + k) for k, piece in enumerate(pieces)])
        after = [left_head] if chunk == 1 else arrived[chunk - 2 : chunk - 1] if chunk > 1 else []
        shares.append(
            call(
                lambda *refs: share_kernel(experts, *refs),
                "share",
                shape(own.shape, BF16),
                own,
                *others[-1],
                *after,
                read=experts,
            )
        )
        arrived.append(mirrored(shares[-1], "pipe"))

    def place(start, some, kept=(), after=()):
        count = len(some)
        return pl.pallas_call(
            lambda *refs: place_kernel(start, count, *refs),
            in_specs=[ANY] * (count + len(kept) + len(after)),
            out_specs=[ANY, VMEM],
            out_shape=[shape((1, tokens, width), BF16), shape((8, LANES), F32)],
            scratch_shapes=[pltpu.SemaphoreType.DMA((count,))],
            input_output_aliases={count + k: k for k in range(len(kept))},
            compiler_params=ROOM,
            cost_estimate=pl.CostEstimate(
                flops=0, bytes_accessed=4 * count * some[0].shape[0] * width, transcendentals=0
            ),
            name="place",
        )(*some, *kept, *after)

    placed, token = place(0, [left_head])

    fresh, peaks, steps = [], None, []
    for chunk, (start, stop) in enumerate(chunks):
        kept = () if peaks is None else (peaks,)
        after = (token,) if chunk == 1 else ()
        some, peaks = call(
            lambda *refs: update_kernel(start, *refs),
            "update",
            [shape((2, depth, stop - start), F32), shape((8, LANES), F32)],
            arrived[chunk],
            master,
            moment,
            second,
            *kept,
            *after,
            read=4 + len(kept),
            scratch=[pltpu.VMEM((2, LANES, LANES), F32)],
            flops=40 * depth * (stop - start),
        )
        fresh.append(some)
        steps.append(peaks)

    half = (tokens - head) // 2
    tail_rows = leaving(head, half, steps[-3])
    left_tails = [shifted(tail_rows, "pipe"), shifted(leaving(head + half, half, steps[-3]), "pipe")]

    group = LANES // depth
    peak_rows = [peaks] + [exchange(peaks, "expert", k) for k in range(1, experts)]
    coded, token = call(
        lambda *refs: code_kernel(group, *refs),
        "codes",
        [shape((2, 1, depth, width), BF16), shape((8, LANES), F32)],
        *peak_rows[:group],
        *fresh,
        read=group + len(fresh),
        flops=4 * depth * width,
    )
    placed, token = place(head, left_tails, (placed,), (token,))
    scales = call(
        lambda *refs: scale_kernel(group, experts, *refs),
        "scales",
        shape((2, 1, experts // group, blocks), F32),
        *peak_rows,
        token,
        read=experts,
    )
    return (placed, coded, scales)


def solution(mesh):
    in_specs = (
        P("pipe", "expert", "dp"),
        P("pipe", "expert", "dp"),
        P("pipe", "expert", "dp"),
        P(None, "pipe", "dp"),
        P(None, "pipe", None, "dp"),
        P(None, "pipe", None, "dp"),
        P(None, "pipe", "expert", "dp"),
        P(None, "pipe", "expert", "dp"),
        P(None, "pipe", "expert", "dp"),
    )
    out_specs = (
        P("pipe", "expert", "dp"),
        P(None, "pipe", "expert", "dp"),
        P(None, "pipe", None, "dp"),
    )
    return jax.shard_map(shards, mesh=mesh, in_specs=in_specs, out_specs=out_specs, check_vma=False)
```
